32 devices in a mesh: group: 8 (over z, y), inner: 4 (over x, core).
Axes of the slice: x: 2, y: 2, z: 4, core: 2. Of those that a mesh axis runs over, the one named last changes fastest.
Arguments:
- inputs: bfloat16 [32768, 768], P(('group', 'inner')), may hold values from -6 to 6
- upstream: bfloat16 [32768, 768], P(('group', 'inner')), may hold values from -6 to 6
- buckets: int32 [32], P(('group', 'inner')), may hold values from 0 to 1
- lengths: int32 [32, 8], P(('group', 'inner')), may hold values from 32 to 128
- layer_keep: int32 [32, 8], P(('group', 'inner')), may hold values 0 or 1
- attend_weight: bfloat16 [768, 2304], P(('group', 'inner')), may hold values from -0.21875 to 0.21875
- attend_bias: bfloat16 [1536], P(('group', 'inner')), may hold values from -1.796875 to 1.796875
- merge_weight: bfloat16 [768, 768], P(('group', 'inner')), may hold values from -1.75 to 1.75
- merge_bias: bfloat16 [768], P(('group', 'inner')), may hold values from -1.796875 to 1.796875
- expand_weight: bfloat16 [768, 3072], P(('group', 'inner')), may hold values from -0.21875 to 0.21875
- expand_bias: bfloat16 [3072], P(('group', 'inner')), may hold values from -3 to 3
- shrink_weight: bfloat16 [3072, 768], P(('group', 'inner')), may hold values from -0.21875 to 0.21875
- shrink_bias: bfloat16 [768], P(('group', 'inner')), may hold values from -1.796875 to 1.796875
- norm_gain: bfloat16 [2, 768], P(None, ('group', 'inner')), may hold values from 0.5 to 1.5
- norm_shift: bfloat16 [2, 768], P(None, ('group', 'inner')), may hold values from -1.796875 to 1.796875
Outputs:
- outputs: bfloat16 [32768, 768], P(('group', 'inner'))
- input_grad: float32 [32768, 768], P(('group', 'inner'))
- attend_weight_grad: float32 [768, 2304], P(('group', 'inner'))
- attend_bias_grad: float32 [1536], P(('group', 'inner'))
- merge_weight_grad: float32 [768, 768], P(('group', 'inner'))
- merge_bias_grad: float32 [768], P(('group', 'inner'))
- expand_weight_grad: float32 [768, 3072], P(('group', 'inner'))
- expand_bias_grad: float32 [3072], P(('group', 'inner'))
- shrink_weight_grad: float32 [3072, 768], P(('group', 'inner'))
- shrink_bias_grad: float32 [768], P(('group', 'inner'))
- norm_gain_grad: float32 [2, 768], P(None, ('group', 'inner'))
- norm_shift_grad: float32 [2, 768], P(None, ('group', 'inner'))
The draws below stay inside these ranges and needn't reach their ends.
All inputs are finite; a program needn't handle non-finite values. No bound on the sum of `layer_keep` on one device may be relied on, other than what follows from the above.
Results may differ from the reference program's by a relative error of at most 0.014.
Values may be sent and summed in bfloat16 or wider, within the bound.
A program may use at most 192 MiB of HBM per device.

```python
import jax
import jax.numpy as jnp
from jax import lax

D = 768
FF = 3072
HEADS = 12
HD = 64
LONG = 512
SHORT = 128
TOK_DEV = 1024
SLOTS = 8
TOKENS = 32768
N_GROUP = 8
N_INNER = 4


def with_ends(array, stream_key, low, high):
    shape = array.shape
    spot = [jax.random.randint(jax.random.fold_in(stream_key, axis), (), 0, shape[axis]) for axis in range(len(shape))]
    array = array.at[tuple(spot)].set(low)
    longest = shape.index(max(shape))
    spot[longest] = (spot[longest] + 1) % shape[longest]
    return array.at[tuple(spot)].set(high)


def with_spikes(entries, key, source, target, shards_of, factor):
    owner, partner = [(jnp.arange(entries.shape[dim]) // (entries.shape[dim] // shards_of)).reshape([-1 if axis == dim else 1 for axis in range(entries.ndim)]) for dim in (source, target)]
    chosen = jax.random.permutation(key, shards_of)[partner]
    strong = (owner == chosen) | (owner == (partner + shards_of // 2) % shards_of)
    return jnp.where(strong, factor * entries, entries)


def block_scale(stream_key, dims, cuts, low, largest):
    loudness, own = 1.0, jax.random.fold_in(stream_key, 6)
    for dim, parts in cuts:
        draws = jnp.exp(jax.random.uniform(jax.random.fold_in(own, dim), (parts,), jnp.float32, low / len(cuts), largest / len(cuts)))
        loudness = loudness * jnp.repeat(draws, dims[dim] // parts).reshape([-1 if axis == dim else 1 for axis in range(len(dims))])
    return loudness


def gaussian(key, extent, scale, most, cuts=(), kind=jnp.bfloat16):
    array = jax.random.normal(key, extent, jnp.float32) * scale
    if len(cuts) > 0:
        array = block_scale(key, extent, cuts, -0.22, 0.18) * array
    return jnp.clip(array, min=-most, max=most).astype(kind)


def noise_with(key, dims, width, reach, split, heavy, held_as=jnp.bfloat16):
    values = width * jax.random.normal(key, dims, jnp.float32)
    if split:
        values = values * block_scale(key, dims, split, -0.22, 0.18)
    return jnp.clip(with_spikes(values, jax.random.fold_in(key, 3), *heavy), -reach, reach).astype(held_as)


def setup_inputs(seed: int = 0) -> dict:
    key_of = jax.random.split(jax.random.key(seed), 16)
    return {
        "inputs": noise_with(key_of[0], (TOKENS, D), 1.0, 6.0, ((0, 32),), (0, 1, 32, 2.75)),
        "upstream": noise_with(key_of[1], (TOKENS, D), 1.0, 6.0, ((0, 32),), (0, 1, 32, 2.75)),
        "buckets": with_ends(jax.random.randint(key_of[2], (N_GROUP * N_INNER,), 0, 2), jax.random.fold_in(key_of[2], 1), 0, 1).astype(jnp.int32),
        "lengths": with_ends(jax.random.randint(key_of[3], (N_GROUP * N_INNER, SLOTS), SHORT // 4, SHORT + 1), jax.random.fold_in(key_of[3], 1), SHORT // 4, SHORT).astype(jnp.int32),
        "layer_keep": with_ends((jax.random.randint(key_of[4], (N_GROUP * N_INNER, SLOTS), 0, 4) < 3).astype(jnp.int32), jax.random.fold_in(key_of[4], 1), 0, 1),
        "attend_weight": gaussian(key_of[5], (D, 3 * D), D ** -0.5, 0.21875, ((0, 32),)),
        "attend_bias": gaussian(key_of[6], (2 * D,), 0.3, 1.796875, ((0, 32),)),
        "merge_weight": gaussian(key_of[7], (D, D), (D // 64) ** -0.5, 1.75, ((0, 32),)),
        "merge_bias": gaussian(key_of[8], (D,), 0.3, 1.796875, ((0, 32),)),
        "expand_weight": gaussian(key_of[9], (D, FF), D ** -0.5, 0.21875, ((0, 32),)),
        "expand_bias": gaussian(key_of[10], (FF,), 0.5, 3.0, ((0, 32),)),
        "shrink_weight": gaussian(key_of[11], (FF, D), (FF // 4) ** -0.5, 0.21875, ((0, 32),)),
        "shrink_bias": gaussian(key_of[12], (D,), 0.3, 1.796875, ((0, 32),)),
        "norm_gain": jnp.clip(1.0 + 0.1 * jax.random.normal(key_of[13], (2, D), jnp.float32), 0.5, 1.5).astype(jnp.bfloat16),
        "norm_shift": gaussian(key_of[14], (2, D), 0.3, 1.796875, ((1, 32),)),
    }


@jax.custom_vjp
def low(v):
    return lax.optimization_barrier(v.astype(jnp.bfloat16)).astype(jnp.float32)

@jax.custom_vjp
def low_back(v):
    return v

def low_keep(v):
    return (low(v), None)

def low_pass(kept, grad):
    return (grad,)

def back_keep(v):
    return (v, None)

def back_low(kept, grad):
    return (low(grad),)
low.defvjp(low_keep, low_pass)
low_back.defvjp(back_keep, back_low)
epsilon = 1e-05
masked_score = -1e+30

def product(left, right):
    return jnp.dot(left, right, precision=lax.Precision.HIGHEST, preferred_element_type=jnp.float32)

def layer_norm(hidden, gains, shifts):
    center = hidden - lax.optimization_barrier(jnp.mean(hidden, axis=-1, keepdims=True))
    spread = lax.optimization_barrier(jnp.mean(center * center, axis=-1, keepdims=True))
    return center * lax.rsqrt(spread + epsilon) * gains + shifts

def token_info(bucket, slot_lengths, slot_keeps):
    position = jnp.arange(TOK_DEV, dtype=jnp.int32)
    span_size = jnp.where(bucket > 0, LONG, SHORT).astype(jnp.int32)
    sequence = position // span_size
    within = position - sequence * span_size
    slot_index = sequence * (span_size // SHORT)
    matches = (slot_index[:, None] == jnp.arange(SLOTS, dtype=jnp.int32)[None, :]).astype(jnp.int32)
    length = lax.optimization_barrier(jnp.sum(matches * slot_lengths[None, :], axis=1)) + bucket * (LONG - SHORT)
    keep_flags = lax.optimization_barrier(jnp.sum(matches * slot_keeps[None, :], axis=1))
    return (sequence, within < length, keep_flags > 0)

def attend_block(pieces):
    queries, key_rows, values, sequence, valid_key = pieces
    scores = low_back(jnp.einsum('qhd,khd->hqk', queries, key_rows, precision=lax.Precision.HIGHEST))
    allowed = (sequence[:, None] == sequence[None, :]) & valid_key[None, :]
    scores = jnp.where(allowed[None], scores, masked_score)
    highest = lax.optimization_barrier(jnp.max(scores, axis=-1, keepdims=True))
    raised = jnp.exp(scores - highest)
    weights = raised / lax.optimization_barrier(jnp.sum(raised, axis=-1, keepdims=True))
    return jnp.einsum('hqk,khd->qhd', low(weights), values, precision=lax.Precision.HIGHEST)

def forward(params, tokens, sequence, valid_key, keep_flags):
    attend_matrix, attend_offset, merge_matrix, merge_offset, expand_matrix, expand_offset, shrink_matrix, shrink_offset, gains, shifts = params
    model_width = tokens.shape[1]
    blocks = TOK_DEV // LONG
    packed = product(low(tokens), attend_matrix)
    queries = low(low_back((packed[:, :model_width] + attend_offset[:model_width]) * 0.125))
    key_rows = low(low_back(packed[:, model_width:2 * model_width]))
    values = low(low_back(packed[:, 2 * model_width:] + attend_offset[model_width:]))

    def heads_view(source):
        return source.reshape(blocks, LONG, HEADS, HD)
    mixed_rows = lax.map(jax.checkpoint(attend_block), (heads_view(queries), heads_view(key_rows), heads_view(values), sequence.reshape(blocks, LONG), valid_key.reshape(blocks, LONG)))
    mixed_rows = low(low_back(mixed_rows.reshape(TOK_DEV, model_width)))
    branch = low_back(product(mixed_rows, merge_matrix) + merge_offset)
    normed = layer_norm(tokens + branch, gains[0], shifts[0])
    expanded = low_back(product(low(normed), expand_matrix) + expand_offset)
    active = low(jax.nn.gelu(expanded, approximate=False))
    shrunk = low_back(product(active, shrink_matrix) + shrink_offset)
    result = layer_norm(normed + shrunk, gains[1], shifts[1])
    return jnp.where(keep_flags[:, None], result, tokens)

def reference(inputs, upstream, buckets, lengths, layer_keep, attend_weight, attend_bias, merge_weight, merge_bias, expand_weight, expand_bias, shrink_weight, shrink_bias, norm_gain, norm_shift):
    params = tuple((weight.astype(jnp.float32) for weight in (attend_weight, attend_bias, merge_weight, merge_bias, expand_weight, expand_bias, shrink_weight, shrink_bias, norm_gain, norm_shift)))
    device_count = N_GROUP * N_INNER
    token_rows = inputs.reshape(device_count, TOK_DEV, D)
    grad_rows = upstream.reshape(device_count, TOK_DEV, D)

    def device_step(totals, pieces):
        tokens, cotangent, bucket, slot_lengths, slot_keeps = pieces
        sequence, valid_key, keep_flags = token_info(bucket, slot_lengths, slot_keeps)

        def local_forward(weights, source):
            return forward(weights, source, sequence, valid_key, keep_flags)
        output, pull_back = jax.vjp(local_forward, params, tokens.astype(jnp.float32))
        weight_grads, token_grad = pull_back(cotangent.astype(jnp.float32))
        totals = jax.tree.map(jnp.add, totals, weight_grads)
        return (totals, (output.astype(jnp.bfloat16), token_grad))
    empty_sums = tuple((jnp.zeros_like(weight) for weight in params))
    totals, (outputs, token_grads) = lax.scan(device_step, empty_sums, (token_rows, grad_rows, buckets, lengths, layer_keep))
    return (outputs.reshape(TOKENS, D), token_grads.reshape(TOKENS, D), totals[0], totals[1], totals[2], totals[3], totals[4], totals[5], totals[6], totals[7], totals[8], totals[9])
```

```python
import jax
import jax.numpy as jnp
from jax import lax
from jax.experimental import pallas as pl
from jax.experimental.pallas import tpu as pltpu
from jax.sharding import PartitionSpec as P

HEADS = 12
HD = 64
LONG = 512
SHORT = 128
TOK_DEV = 1024
SLOTS = 8
D = 768
FF = 3072
LANES = 128
epsilon = 1e-05
masked_score = -1e30
f32 = jnp.float32
bf16 = jnp.bfloat16


def dot_nn(a, b):
    return lax.dot_general(a, b, (((1,), (0,)), ((), ())), preferred_element_type=f32)


def dot_nt(a, b):
    return lax.dot_general(a, b, (((1,), (1,)), ((), ())), preferred_element_type=f32)


def dot_tn(a, b):
    return lax.dot_general(a, b, (((0,), (0,)), ((), ())), preferred_element_type=f32)


def lane_index(rows):
    return lax.broadcasted_iota(jnp.int32, (rows, LANES), 1)


def token_tables(bucket, lengths, keeps, query_const, key_const, keep_table):
    shape = (TOK_DEV, LANES)
    position = lax.broadcasted_iota(jnp.int32, shape, 0)
    is_long = jnp.broadcast_to(bucket, shape) > 0
    slot = jnp.where(is_long, (position >> 9) << 2, position >> 7)
    offset = jnp.where(is_long, position & (LONG - 1), position & (SHORT - 1))
    length = jnp.zeros(shape, jnp.int32)
    keep = jnp.zeros(shape, jnp.int32)
    for b in range(SLOTS):
        here = slot == b
        length = jnp.where(here, lengths[b], length)
        keep = jnp.where(here, keeps[b], keep)
    length = length + bucket * (LONG - SHORT)
    valid = offset < length
    within = jnp.where(is_long, 0, (position >> 7) & 3)
    lane = lax.broadcasted_iota(jnp.int32, shape, 1) & (HD - 1)
    is_span = (lane >= 4) & (lane < 8)
    same = lane - 4 == within
    zero, one = jnp.zeros(shape, f32), jnp.ones(shape, f32)
    query_const[...] = jnp.where(lane == 3, one, jnp.where(is_span & ~same, one, zero)).astype(bf16)
    key_const[...] = jnp.where(
        lane < 3,
        one,
        jnp.where(((lane == 3) & ~valid) | (is_span & same), masked_score * one, zero),
    ).astype(bf16)
    keep_table[...] = jnp.where(keep > 0, one, zero)


def three_parts(column, rows):
    wide = jnp.broadcast_to(column, (rows, LANES))
    high = wide.astype(bf16)
    rest = wide - high.astype(f32)
    middle = rest.astype(bf16)
    low = (rest - middle.astype(f32)).astype(bf16)
    return high, middle, low


def attend_forward(index, query_const, key_const, q_ref, k_ref, v_ref, mixed_ref, logsum_ref, tile):
    pair, block = index // 2, index % 2
    cols = pl.ds(pl.multiple_of(pair * LANES, LANES), LANES)
    rows = pl.ds(pl.multiple_of(block * LONG, LONG), LONG)
    lane_k = lane_index(LONG)
    k2, v2 = k_ref[rows, cols], v_ref[rows, cols]
    kc = key_const[rows, :]
    k_aug = [jnp.where((lane_k // HD) == half, k2, kc) for half in range(2)]
    lane_q = lane_index(tile)
    for t in range(LONG // tile):
        qrows = pl.ds(pl.multiple_of(block * LONG + t * tile, tile), tile)
        q2, qc = q_ref[qrows, cols], query_const[qrows, :]
        outs = []
        sums = logsum_ref[qrows, :]
        for half in range(2):
            q_aug = jnp.where((lane_q // HD) == half, q2, qc)
            scores = dot_nt(q_aug, k_aug[half])
            highest = jnp.max(scores, axis=1, keepdims=True)
            raised = jnp.exp(scores - highest)
            total = jnp.sum(raised, axis=1, keepdims=True)
            out = dot_nn(raised.astype(bf16), v2)
            outs.append(out * (1.0 / total))
            sums = jnp.where(lane_q == 2 * pair + half, highest + jnp.log(total), sums)
        logsum_ref[qrows, :] = sums
        mixed_ref[qrows, cols] = jnp.where(lane_q < HD, outs[0], outs[1]).astype(bf16)


def attend_backward(index, query_const, key_const, q_ref, k_ref, v_ref, mixed_ref, logsum_ref, mixed_grad_ref,
                    dq_ref, dk_ref, dv_ref, tile):
    pair, block = index // 2, index % 2
    cols = pl.ds(pl.multiple_of(pair * LANES, LANES), LANES)
    rows = pl.ds(pl.multiple_of(block * LONG, LONG), LONG)
    lane = lane_index(LONG)
    q2, dm2 = q_ref[rows, cols], mixed_grad_ref[rows, cols]
    product = dm2.astype(f32) * mixed_ref[rows, cols].astype(f32)
    sums = logsum_ref[rows, :]
    qc = query_const[rows, :]
    zero = jnp.zeros((LONG, LANES), bf16)
    q_aug, d_aug = [], []
    for half in range(2):
        mine = (lane // HD) == half
        at = lane & (HD - 1)
        logsum = jnp.sum(jnp.where(lane == 2 * pair + half, sums, 0.0), axis=1, keepdims=True)
        delta = jnp.sum(jnp.where(mine, product, 0.0), axis=1, keepdims=True)
        lh, lm, ll = three_parts(-logsum, LONG)
        dh, dm, dl = three_parts(-delta, LONG)
        extra = jnp.where(at == 0, lh, jnp.where(at == 1, lm, jnp.where(at == 2, ll, qc)))
        q_aug.append(jnp.where(mine, q2, extra))
        extra = jnp.where(at == 0, dh, jnp.where(at == 1, dm, jnp.where(at == 2, dl, zero)))
        d_aug.append(jnp.where(mine, dm2, extra))
    dq = [jnp.zeros((LONG, LANES), f32) for _ in range(2)]
    lane_t = lane_index(tile)
    one = jnp.ones((tile, LANES), bf16)
    zero_t = jnp.zeros((tile, LANES), bf16)
    for t in range(LONG // tile):
        krows = pl.ds(pl.multiple_of(block * LONG + t * tile, tile), tile)
        k2, v2, kc = k_ref[krows, cols], v_ref[krows, cols], key_const[krows, :]
        vc = jnp.where((lane_t & (HD - 1)) < 3, one, zero_t)
        dk, dv = [], []
        for half in range(2):
            mine = (lane_t // HD) == half
            weights = jnp.exp(dot_nt(jnp.where(mine, k2, kc), q_aug[half]))
            grads = weights * dot_nt(jnp.where(mine, v2, vc), d_aug[half])
            low, low_grads = weights.astype(bf16), grads.astype(bf16)
            dv.append(dot_nn(low, dm2))
            dk.append(dot_nn(low_grads, q2))
            dq[half] = dq[half] + dot_tn(low_grads, k2)
        dk_ref[krows, cols] = jnp.where(lane_t < HD, dk[0], dk[1]).astype(bf16)
        dv_ref[krows, cols] = jnp.where(lane_t < HD, dv[0], dv[1]).astype(bf16)
    dq_ref[rows, cols] = (jnp.where(lane < HD, dq[0], dq[1]).astype(bf16).astype(f32) * 0.125).astype(bf16)


def gelu_parts(x):
    z = jnp.abs(x) * 0.7071067811865476
    t = 1.0 / (1.0 + 0.3275911 * z)
    bell = jnp.exp(-z * z)
    tail = t * (0.127414796 + t * (-0.142248368 + t * (0.7107068705 + t * (-0.7265760135 + t * 0.5307027145)))) * bell
    phi = jnp.where(x >= 0.0, 1.0 - tail, tail)
    return x * phi, phi + x * (bell * 0.3989422804014327)


def norm_parts(x):
    center = x - jnp.mean(x, axis=-1, keepdims=True)
    spread = jnp.mean(center * center, axis=-1, keepdims=True)
    rstd = lax.rsqrt(spread + epsilon)
    return center * rstd, rstd


def norm_back(dy_hat, x_hat, rstd):
    a = jnp.mean(dy_hat, axis=-1, keepdims=True)
    b = jnp.mean(dy_hat * x_hat, axis=-1, keepdims=True)
    return rstd * (dy_hat - a - x_hat * b)

MESH = pl.DeviceIdType.MESH
Z, X, Y = 4, 2, 2
CHIPS = Z * Y * X
JOBS = 6
PART = FF // JOBS
BLOCK = D // CHIPS
FF_BLOCK = FF // CHIPS
SLICE = FF_BLOCK // JOBS


class Place:
    def __init__(self):
        group, inner = lax.axis_index("group"), lax.axis_index("inner")
        self.z, self.y, self.x, self.c = group // Y, group % Y, inner // 2, inner % 2
        self.index = group * (X * 2) + inner
        self.chip = group * X + self.x
        self.twin = (group, self.x * 2 + 1 - self.c)
        self.over_x = (group, (1 - self.x) * 2 + self.c)
        self.over_y = (self.z * Y + 1 - self.y, inner)
        self.other_z = (self.z + 1 - 2 * (self.z % 2), (self.z + 2) % Z, Z - 1 - self.z)
        self.over_z = tuple((z * Y + self.y, inner) for z in self.other_z)

    def greet(self):
        barrier = pltpu.get_barrier_semaphore()
        peers = (self.twin, self.over_x, self.over_y) + self.over_z
        for peer in peers:
            pl.semaphore_signal(barrier, 1, device_id=peer, device_id_type=MESH)
        pl.semaphore_wait(barrier, len(peers))


def remote(source, target, send, recv, peer):
    return pltpu.make_async_remote_copy(
        src_ref=source, dst_ref=target, send_sem=send, recv_sem=recv, device_id=peer, device_id_type=MESH
    )


def aligned(value, unit):
    return pl.multiple_of(value, unit)


class Cut:
    def __init__(self, rows, cols, first=None, near=(slice(None), slice(None))):
        self.rows, self.cols, self.first, self.near = rows, cols, first, near


def row_parts(start, low, high, cols):
    return (
        Cut(pl.ds(aligned(start, 16), low), cols, "x", (pl.ds(0, low), slice(None))),
        Cut(pl.ds(aligned(start + low, 16), high), cols, "y", (pl.ds(low, high), slice(None))),
    )


def attend_cuts(core, g):
    cols = pl.ds(aligned(256 * g + 128 * core, 128), 128)
    low, high = (16, 32) if g % 2 == 0 else (32, 16)
    return Cut(pl.ds(0, BLOCK), cols), row_parts(0, low, high, cols)


def merge_cuts(core):
    cols = pl.ds(aligned(384 * core, 128), 384)
    return Cut(pl.ds(0, BLOCK), cols), row_parts(0, 32, 16, cols)


def expand_cuts(core, j):
    at = PART * j + 256 * core
    rows = pl.ds(0, BLOCK)
    whole = Cut(rows, pl.ds(aligned(at, 128), 256))
    return whole, tuple(
        Cut(rows, pl.ds(aligned(at + 128 * n, 128), 128), "xy"[n], (slice(None), pl.ds(128 * n, 128))) for n in range(2)
    )


def shrink_cuts(core, j):
    cols = pl.ds(aligned(384 * core, 128), 384)
    half = SLICE // 2
    return Cut(pl.ds(aligned(SLICE * j, SLICE), SLICE), cols), row_parts(SLICE * j, half, half, cols)


ALL = slice(None)


def blocks(ref, z, y, x, cut):
    if len(ref.shape) == 6:
        return ref.at[z, y, x, :, cut.rows, cut.cols]
    return ref.at[z, y, x, cut.rows, cut.cols]


class Gather:
    def __init__(self, place, ref, cuts, send, recv, twin_send, twin_recv):
        self.place, self.ref, (self.whole, self.parts) = place, ref, cuts
        self.send, self.recv, self.twin_send, self.twin_recv = send, recv, twin_send, twin_recv

    def along_z(self, n, part):
        p = self.place
        here = blocks(self.ref, p.z, p.y, p.x, part)
        return [remote(here, here, self.send.at[n, m], self.recv.at[n, m], p.over_z[m]) for m in range(3)]

    def second(self, n, part):
        p = self.place
        here = blocks(self.ref, ALL, p.y, p.x, part)
        return remote(here, here, self.send.at[n, 3], self.recv.at[n, 3], p.over_x if part.first == "x" else p.over_y)

    def third(self, n, part):
        p = self.place
        if part.first == "x":
            here, peer = blocks(self.ref, ALL, p.y, ALL, part), p.over_y
        else:
            here, peer = blocks(self.ref, ALL, ALL, p.x, part), p.over_x
        return remote(here, here, self.send.at[n, 4], self.recv.at[n, 4], peer)

    def to_twin(self):
        here = blocks(self.ref, ALL, ALL, ALL, self.whole)
        return remote(here, here, self.twin_send, self.twin_recv, self.place.twin)

    def start_z(self):
        for n, part in enumerate(self.parts):
            for copy in self.along_z(n, part):
                copy.start()

    def start_second(self):
        for n, part in enumerate(self.parts):
            for copy in self.along_z(n, part):
                copy.wait_recv()
            self.second(n, part).start()

    def start_third(self):
        for n, part in enumerate(self.parts):
            self.second(n, part).wait_recv()
            self.third(n, part).start()

    def start_twin(self):
        for n, part in enumerate(self.parts):
            self.third(n, part).wait_recv()
        self.to_twin().start()

    def ready(self):
        self.to_twin().wait_recv()

    def finish(self):
        for n, part in enumerate(self.parts):
            for copy in self.along_z(n, part):
                copy.wait_send()
            self.second(n, part).wait_send()
            self.third(n, part).wait_send()
        self.to_twin().wait_send()

VEC_ROWS = 16
ROW_MERGE, ROW_EXPAND, ROW_SHRINK, ROW_GAIN, ROW_SHIFT = 2, 3, 9, 10, 12


def place_vectors(place, pieces_ref, out_ref):
    pieces = pieces_ref[...].astype(bf16)
    source = lax.broadcasted_iota(jnp.int32, (LANES, D), 0)
    target = lax.broadcasted_iota(jnp.int32, (LANES, D), 1)

    def spread(width, offset):
        chosen = (target == source + offset) & (source < width)
        return dot_nn(pieces, jnp.where(chosen, 1.0, 0.0).astype(bf16))

    per_row = D // 48
    attend = spread(48, 48 * (place.index % per_row))
    single = spread(24, 24 * place.index)
    expand = spread(SLICE, SLICE * place.chip)
    out_ref[...] = jnp.zeros((VEC_ROWS, D), f32)
    half = place.index // per_row
    out_ref[0:1, :] = jnp.where(half == 0, attend[0:1], 0.0)
    out_ref[1:2, :] = jnp.where(half == 1, attend[0:1], 0.0)
    out_ref[2:3, :] = single[1:2]
    out_ref[3:6, :] = jnp.where(place.c == 0, expand[2:5], 0.0)
    out_ref[6:9, :] = jnp.where(place.c == 1, expand[2:5], 0.0)
    out_ref[9:14, :] = single[5:10]


def compose(place, pack_ref, twin_ref, target_ref, source_cols, target_cols):
    half = BLOCK // 2
    mine = pack_ref[:, source_cols].astype(f32)[:half]
    other = twin_ref[:, source_cols].astype(f32)[:half]
    first = jnp.where(place.c == 0, mine, other)
    second = jnp.where(place.c == 0, other, mine)
    both = jnp.concatenate([first, second], axis=0).astype(bf16)
    if len(target_ref.shape) == 6:
        n = target_cols[0]
        target_ref[place.z, place.y, place.x, n, :, target_cols[1]] = both
    else:
        target_ref[place.z, place.y, place.x, :, target_cols] = both


def forward_kernel(
    bucket, lengths, keeps, x_any, g_any, pack_ref, shrink_ref, pieces_ref,
    out_any, wa_any, wm_any, we_any, ws_any, qkv_any, mixed_any, logsum_any, xhat_any, rstd_any, lowt_any, xt_any,
    active_any, slope_any, second_any, vec_out, gain_out,
    wa, wm, we, ws, pack_twin, vecs, vec_land, x_ref, g_ref, q, k, v, query_const, key_const, keep_table,
    mixed, logsum, xhat, rstd, low, turned, active, slope, acc, out,
    send, recv, twin_send, twin_recv, own_send, own_recv, vec_send, vec_recv, local, flow,
):
    place = Place()
    c = place.c
    x_copy = pltpu.make_async_copy(x_any, x_ref, local.at[0])
    g_copy = pltpu.make_async_copy(g_any, g_ref, local.at[1])
    x_copy.start()
    g_copy.start()
    place.greet()

    own_pack = remote(pack_ref, pack_twin, own_send.at[0], own_recv.at[0], place.twin)
    own_pack.start()
    half = FF_BLOCK // 2
    their_cols = pl.ds(aligned(384 * (1 - c), 128), 384)
    my_rows = pl.ds(aligned(half * c, half), half)
    own_shrink = remote(
        shrink_ref.at[:, their_cols],
        ws.at[place.z, place.y, place.x, my_rows, their_cols],
        own_send.at[1], own_recv.at[1], place.twin,
    )
    own_shrink.start()
    place_vectors(place, pieces_ref, vecs.at[0])

    def vec_copy(step, m, peer):
        return remote(vecs.at[step], vec_land.at[step + m], vec_send.at[step + m], vec_recv.at[step + m], peer)

    vec_steps = [vec_copy(0, 0, place.twin), vec_copy(1, 0, place.over_x), vec_copy(2, 0, place.over_y)]
    vec_last = [vec_copy(3, m, place.over_z[m]) for m in range(3)]

    def vec_next(step):
        vec_steps[step].wait_recv()
        vecs[step + 1] = vecs[step] + vec_land[step]

    vec_steps[0].start()

    def gather(ref, cuts, at):
        return Gather(place, ref, cuts, send.at[at], recv.at[at], twin_send.at[at], twin_recv.at[at])

    def job(t):
        if isinstance(t, int) and t < 3:
            return [gather(wa, attend_cuts(c, t), t)]
        if isinstance(t, int) and t == 3:
            return [gather(wm, merge_cuts(c), 3)]
        j = t - 4
        return [
            gather(we, expand_cuts(c, j), 4 + 2 * j),
            gather(ws, shrink_cuts(c, j), 5 + 2 * j),
        ]

    def each(t, action):
        for one in job(t):
            getattr(one, action)()

    own_pack.wait_recv()
    for n in range(3):
        for g in range(3):
            cols = aligned(256 * g + 128 * c, 128)
            compose(place, pack_ref, pack_twin, wa, pl.ds(aligned(D * n + cols, 128), 128), (n, pl.ds(cols, 128)))
    each(0, "start_z")
    cols = aligned(384 * c, 128)
    compose(place, pack_ref, pack_twin, wm, pl.ds(aligned(3 * D + cols, 128), 384), pl.ds(cols, 384))
    for t in range(1, 4):
        each(t, "start_z")
    vec_next(0)
    vec_steps[1].start()
    for j in range(JOBS):
        cols = aligned(PART * j + 256 * c, 128)
        compose(place, pack_ref, pack_twin, we, pl.ds(aligned(4 * D + cols, 128), 256), pl.ds(cols, 256))
    my_cols = pl.ds(aligned(384 * c, 128), 384)
    ws[place.z, place.y, place.x, my_rows, my_cols] = shrink_ref[:, my_cols]
    own_shrink.wait_recv()
    for t in range(4, 4 + JOBS):
        each(t, "start_z")
    vec_next(1)
    vec_steps[2].start()
    each(0, "start_second")
    token_tables(
        bucket[0], [lengths[0, b] for b in range(SLOTS)], [keeps[0, b] for b in range(SLOTS)],
        query_const, key_const, keep_table,
    )
    vec_next(2)
    for copy in vec_last:
        copy.start()
    each(1, "start_second")
    each(0, "start_third")
    x_copy.wait()
    turned[...] = x_ref[...].T
    xt_out = pltpu.make_async_copy(turned, xt_any, flow.at[2, 0])
    xt_out.start()
    logsum[...] = jnp.zeros_like(logsum)
    for copy in vec_last:
        copy.wait_recv()
    vec = vecs.at[4]
    vec[...] = vecs[3] + vec_land[3] + vec_land[4] + vec_land[5]

    def tick(t):
        each(t, "start_twin")
        if t + 2 < 4 + JOBS:
            each(t + 2, "start_second")
        if t + 1 < 4 + JOBS:
            each(t + 1, "start_third")

    outgoing = []

    def emit(source, target, n):
        copy = pltpu.make_async_copy(source, target, local.at[n])
        copy.start()
        outgoing.append(copy)

    def project(g):
        cols = pl.ds(aligned(256 * g, 256), 256)
        x = x_ref[...]
        q[:, cols] = ((dot_nn(x, wa[:, :, :, 0, :, cols].reshape(D, 256)) + vec[0:1, cols]) * 0.125).astype(bf16)
        k[:, cols] = dot_nn(x, wa[:, :, :, 1, :, cols].reshape(D, 256)).astype(bf16)
        v[:, cols] = (dot_nn(x, wa[:, :, :, 2, :, cols].reshape(D, 256)) + vec[1:2, cols]).astype(bf16)

    tick(0)

    def heads(i, carry):
        for g in range(3):

            @pl.when(i == 4 * g)
            def _():
                each(g, "ready")

        @pl.when(i % 4 == 0)
        def _():
            project(i // 4)

        for g in range(3):

            @pl.when(i == 4 * g + 2)
            def _():
                tick(g + 1)

        attend_forward(i, query_const, key_const, q, k, v, mixed, logsum, LONG)
        return carry

    lax.fori_loop(0, 12, heads, 0)
    emit(wa, wa_any, 2)
    emit(q, qkv_any.at[0], 3)
    emit(k, qkv_any.at[1], 4)
    emit(v, qkv_any.at[2], 5)
    emit(mixed, mixed_any, 6)
    emit(logsum, logsum_any, 7)

    tick(4)
    each(3, "ready")
    emit(wm, wm_any, 8)
    first = x_ref[...].astype(f32) + dot_nn(mixed[...], wm[...].reshape(D, D)) + vec[ROW_MERGE : ROW_MERGE + 1, :]
    x_hat, deviation = norm_parts(first)
    xhat[...] = x_hat
    rstd[...] = jnp.broadcast_to(deviation, (TOK_DEV, LANES))
    normed = x_hat * vec[ROW_GAIN : ROW_GAIN + 1, :] + vec[ROW_SHIFT : ROW_SHIFT + 1, :]
    low[...] = normed.astype(bf16)
    acc[...] = normed + vec[ROW_SHRINK : ROW_SHRINK + 1, :]
    emit(xhat, xhat_any, 9)
    emit(rstd, rstd_any, 10)
    xt_out.wait()
    turned[...] = low[...].T
    emit(turned, lowt_any, 11)

    def flow_copies(j):
        return (
            pltpu.make_async_copy(active.at[j % 2], active_any.at[j], flow.at[0, j % 2]),
            pltpu.make_async_copy(slope.at[j % 2], slope_any.at[j], flow.at[1, j % 2]),
        )

    def part(j, carry):
        @pl.when(j > 0)
        def _():
            each(j + 4, "start_twin")

        @pl.when((j > 0) & (j + 2 < JOBS))
        def _():
            each(j + 6, "start_second")

        @pl.when((j > 0) & (j + 1 < JOBS))
        def _():
            each(j + 5, "start_third")

        @pl.when(j >= 2)
        def _():
            for copy in flow_copies(j):
                copy.wait()

        each(j + 4, "ready")
        a_ref, s_ref = active.at[j % 2], slope.at[j % 2]
        for h in range(2):
            cols = pl.ds(aligned(PART * j + 256 * h, 256), 256)
            bias = vec[pl.ds(ROW_EXPAND + j, 1), pl.ds(256 * h, 256)]
            expanded = dot_nn(low[...], we[:, :, :, :, cols].reshape(D, 256)) + bias
            a, s = gelu_parts(expanded)
            a_ref[:, 256 * h : 256 * h + 256] = a.astype(bf16)
            s_ref[:, 256 * h : 256 * h + 256] = s.astype(bf16)
        rows = pl.ds(aligned(SLICE * j, SLICE), SLICE)
        acc[...] += dot_nn(a_ref[...], ws[:, :, :, rows, :].reshape(PART, D))
        for copy in flow_copies(j):
            copy.start()
        return carry

    lax.fori_loop(0, JOBS, part, 0)
    emit(we, we_any, 12)
    emit(ws, ws_any, 13)
    g_copy.wait()
    gain_out[...] = jnp.zeros_like(gain_out)
    tile = 512

    def last(i, carry):
        rows = pl.ds(aligned(i * tile, tile), tile)
        x_hat, deviation = norm_parts(acc[rows, :])
        gain = vec[ROW_GAIN + 1 : ROW_GAIN + 2, :]
        result = x_hat * gain + vec[ROW_SHIFT + 1 : ROW_SHIFT + 2, :]
        keep = jnp.tile(keep_table[rows, :], (1, D // LANES)) > 0.0
        out[rows, :] = jnp.where(keep, result, x_ref[rows, :].astype(f32)).astype(bf16)
        dy = jnp.where(keep, g_ref[rows, :].astype(f32), 0.0)
        grad = norm_back(dy * gain, x_hat, deviation)
        acc[rows, :] = grad
        gain_out[ROW_GAIN + 1 : ROW_GAIN + 2, :] += jnp.sum(dy * x_hat, axis=0, keepdims=True)
        gain_out[ROW_SHIFT + 1 : ROW_SHIFT + 2, :] += jnp.sum(dy, axis=0, keepdims=True)
        gain_out[ROW_SHRINK : ROW_SHRINK + 1, :] += jnp.sum(grad.astype(bf16).astype(f32), axis=0, keepdims=True)
        return carry

    lax.fori_loop(0, TOK_DEV // tile, last, 0)
    emit(acc, second_any, 14)
    emit(out, out_any, 15)
    vec_out[...] = vec[...]
    for j in (JOBS - 2, JOBS - 1):
        for copy in flow_copies(j):
            copy.wait()
    for copy in outgoing:
        copy.wait()
    own_pack.wait_send()
    own_shrink.wait_send()
    for copy in vec_steps + vec_last:
        copy.wait_send()
    for t in range(4):
        each(t, "finish")

    def finish(j, carry):
        each(j + 4, "finish")
        return carry

    lax.fori_loop(0, JOBS, finish, 0)


ANY = pl.BlockSpec(memory_space=pl.ANY)
VM = pl.BlockSpec(memory_space=pltpu.VMEM)
SM = pl.BlockSpec(memory_space=pltpu.SMEM)


def shape(dims, kind):
    return jax.ShapeDtypeStruct(dims, kind)


T = TOK_DEV
WEIGHTS = (
    ((Z, Y, X, 3, BLOCK, D), bf16),
    ((Z, Y, X, BLOCK, D), bf16),
    ((Z, Y, X, BLOCK, FF), bf16),
    ((Z, Y, X, FF_BLOCK, D), bf16),
)


def forward_call(buckets, lengths, keeps, inputs, upstream, pack, shrink, pieces):
    dma = pltpu.SemaphoreType.DMA
    saved = (
        ((3, T, D), bf16),
        ((T, D), bf16),
        ((T, LANES), f32),
        ((T, D), f32),
        ((T, LANES), f32),
        ((D, T), bf16),
        ((D, T), bf16),
        ((JOBS, T, PART), bf16),
        ((JOBS, T, PART), bf16),
        ((T, D), f32),
    )
    results = (((T, D), bf16),) + WEIGHTS + saved
    vec = ((VEC_ROWS, D), f32)
    n_gathers = 4 + 2 * JOBS
    return pl.pallas_call(
        forward_kernel,
        out_shape=tuple(shape(*s) for s in results + (vec, vec)),
        in_specs=[SM, SM, SM, ANY, ANY, VM, VM, VM],
        out_specs=[ANY] * len(results) + [VM, VM],
        scratch_shapes=[pltpu.VMEM(*s) for s in WEIGHTS]
        + [
            pltpu.VMEM((32, 3 * D + D + FF), bf16),
            pltpu.VMEM((5, VEC_ROWS, D), f32),
            pltpu.VMEM((6, VEC_ROWS, D), f32),
            pltpu.VMEM((T, D), bf16),
            pltpu.VMEM((T, D), bf16),
            pltpu.VMEM((T, D), bf16),
            pltpu.VMEM((T, D), bf16),
            pltpu.VMEM((T, D), bf16),
            pltpu.VMEM((T, LANES), bf16),
            pltpu.VMEM((T, LANES), bf16),
            pltpu.VMEM((T, LANES), f32),
            pltpu.VMEM((T, D), bf16),
            pltpu.VMEM((T, LANES), f32),
            pltpu.VMEM((T, D), f32),
            pltpu.VMEM((T, LANES), f32),
            pltpu.VMEM((T, D), bf16),
            pltpu.VMEM((D, T), bf16),
            pltpu.VMEM((2, T, PART), bf16),
            pltpu.VMEM((2, T, PART), bf16),
            pltpu.VMEM((T, D), f32),
            pltpu.VMEM((T, D), bf16),
            dma((n_gathers, 2, 5)),
            dma((n_gathers, 2, 5)),
            dma((n_gathers,)),
            dma((n_gathers,)),
            dma((2,)),
            dma((2,)),
            dma((6,)),
            dma((6,)),
            dma((20,)),
            dma((3, 2)),
        ],
        compiler_params=pltpu.CompilerParams(collective_id=0, has_side_effects=True, vmem_limit_bytes=VMEM_LIMIT),
        cost_estimate=pl.CostEstimate(flops=20_000_000_000, bytes_accessed=60_000_000, transcendentals=10_000_000),
    )(buckets, lengths, keeps, inputs, upstream, pack, shrink, pieces)


VMEM_LIMIT = 60 * 2**20


def pack_weights(attend, merge, expand):
    expand = expand.reshape(-1, CHIPS, JOBS, SLICE).transpose(0, 2, 1, 3).reshape(-1, FF)
    pack = jnp.concatenate([attend, merge, expand], axis=1)
    return jnp.pad(pack, ((0, 8), (0, 0)))


def pack_pieces(attend_bias, merge_bias, expand_bias, shrink_bias, gain, shift):
    def row(piece):
        return jnp.pad(piece.astype(f32), ((0, 0), (0, LANES - piece.shape[1])))

    rows = [
        row(attend_bias[None]), row(merge_bias[None]), row(expand_bias.reshape(3, SLICE)), row(shrink_bias[None]),
        row(gain), row(shift), jnp.zeros((6, LANES), f32),
    ]
    return jnp.concatenate(rows, axis=0)

class Reduce:
    def __init__(self, place, ref, lands, final, cuts, twin_cuts, sems):
        self.place, self.ref, (self.whole, self.parts), self.twin_whole = place, ref, cuts, twin_cuts[0]
        self.lands, self.final = lands, final
        self.send, self.recv, self.twin_send, self.twin_recv = sems
        self.deep = len(ref.shape) == 6

    def land(self, step, n, part, m=None):
        rows, cols = part.near
        ref = self.lands[step]
        index = () if m is None else (m,)
        lead = len(ref.shape) - 2 - len(index)
        return ref.at[index + (ALL,) * lead + (rows, cols)]

    def sent(self, n, part, step):
        p = self.place
        if part.first == "x":
            return blocks(self.ref, ALL, ALL, 1 - p.x, part) if step == 1 else blocks(self.ref, ALL, 1 - p.y, p.x, part)
        return blocks(self.ref, ALL, 1 - p.y, ALL, part) if step == 1 else blocks(self.ref, ALL, p.y, 1 - p.x, part)

    def kept(self, n, part, step):
        p = self.place
        if part.first == "x":
            return blocks(self.ref, ALL, ALL, p.x, part) if step == 1 else blocks(self.ref, ALL, p.y, p.x, part)
        return blocks(self.ref, ALL, p.y, ALL, part) if step == 1 else blocks(self.ref, ALL, p.y, p.x, part)

    def twin(self):
        source = blocks(self.ref, ALL, ALL, ALL, self.twin_whole)
        return remote(source, self.lands[0], self.twin_send, self.twin_recv, self.place.twin)

    def stage(self, n, part, step):
        p = self.place
        peer = p.over_x if (part.first == "x") == (step == 1) else p.over_y
        return remote(
            self.sent(n, part, step), self.land(step, n, part), self.send.at[n, step - 1], self.recv.at[n, step - 1], peer
        )

    def along_z(self, n, part):
        p = self.place
        return [
            remote(
                blocks(self.ref, p.other_z[m], p.y, p.x, part), self.land(3, n, part, m),
                self.send.at[n, 2 + m], self.recv.at[n, 2 + m], p.over_z[m],
            )
            for m in range(3)
        ]

    def start_twin(self):
        self.twin().start()

    def start_first(self):
        self.twin().wait_recv()
        mine = blocks(self.ref, ALL, ALL, ALL, self.whole)
        mine[...] = (mine[...].astype(f32) + self.lands[0][...].astype(f32)).astype(bf16)
        for n, part in enumerate(self.parts):
            self.stage(n, part, 1).start()

    def add(self, n, part, step):
        self.stage(n, part, step).wait_recv()
        mine, other = self.kept(n, part, step), self.land(step, n, part)
        mine[...] = (mine[...].astype(f32) + other[...].astype(f32)).astype(bf16)

    def start_second(self):
        for n, part in enumerate(self.parts):
            self.add(n, part, 1)
            self.stage(n, part, 2).start()

    def start_z(self):
        for n, part in enumerate(self.parts):
            self.add(n, part, 2)
            for copy in self.along_z(n, part):
                copy.start()

    def total(self):
        p = self.place
        for n, part in enumerate(self.parts):
            for copy in self.along_z(n, part):
                copy.wait_recv()
            value = blocks(self.ref, p.z, p.y, p.x, part)[...].astype(f32)
            for m in range(3):
                value += self.land(3, n, part, m)[...].astype(f32)
            index = (ALL,) if self.deep else ()
            self.final[index + (part.rows, part.cols)] = value

    def finish(self):
        self.twin().wait_send()
        for n, part in enumerate(self.parts):
            for step in (1, 2):
                self.stage(n, part, step).wait_send()
            for copy in self.along_z(n, part):
                copy.wait_send()


def backward_kernel(
    bucket, lengths, keeps, wa_any, wm_any, we_any, ws_any, qkv_any, mixed_any, logsum_any, xhat_any, rstd_any,
    lowt_any, xt_any, active_any, slope_any, second_any, g_any, vec, gain_in,
    ig_any, ga_out, gm_out, ge_out, gs_out, vec_out,
    wa, wm, we, ws, ga,
    a0, a1, a2, a3, m0, m1, m2, m3, e0, e1, e2, e3, s0, s1, s2, s3, fa, fm, fe, fs,
    q, k, v, query_const, key_const, keep_table, mixed, logsum, xhat, rstd, turned, low_grad, active, slope, first,
    mixed_grad, gain, vec_land,
    send, recv, twin_send, twin_recv, last_send, last_recv, vec_send, vec_recv, local, flow,
):
    place = Place()
    c = place.c

    def load(source, target, n):
        copy = pltpu.make_async_copy(source, target, local.at[n])
        copy.start()
        return copy

    def flow_copies(j):
        return (
            pltpu.make_async_copy(active_any.at[j], active.at[j % 2], flow.at[0, j % 2]),
            pltpu.make_async_copy(slope_any.at[j], slope.at[j % 2], flow.at[1, j % 2]),
        )

    in_second = load(second_any, first, 0)
    in_ws = load(ws_any, ws, 1)
    for copy in flow_copies(0):
        copy.start()
    in_we = load(we_any, we, 2)
    in_lowt = load(lowt_any, turned, 3)
    later = [
        load(xhat_any, xhat, 4), load(rstd_any, rstd, 5), load(wm_any, wm, 6), load(mixed_any, mixed, 7),
        load(logsum_any, logsum, 8), load(qkv_any.at[0], q, 9), load(qkv_any.at[1], k, 10), load(qkv_any.at[2], v, 11),
        load(wa_any, wa, 12),
    ]
    place.greet()
    token_tables(
        bucket[0], [lengths[0, b] for b in range(SLOTS)], [keeps[0, b] for b in range(SLOTS)],
        query_const, key_const, keep_table,
    )
    gain[0] = gain_in[...]

    def reduction(ref, lands, final, cuts, at, *args):
        sems = (send.at[at], recv.at[at], twin_send.at[at], twin_recv.at[at])
        return Reduce(place, ref, lands, final, cuts(c, *args), cuts(1 - c, *args), sems)

    def job(t):
        if t < JOBS:
            return [
                reduction(we, [e0.at[t % 2]] + [r.at[t] for r in (e1, e2, e3)], fe, expand_cuts, 2 * t, t),
                reduction(ws, [s0.at[t % 2]] + [r.at[t] for r in (s1, s2, s3)], fs, shrink_cuts, 2 * t + 1, t),
            ]
        if t == JOBS:
            return [reduction(wm, [m0, m1, m2, m3], fm, merge_cuts, 2 * JOBS)]
        g = t - JOBS - 1
        return [reduction(ga, [r.at[g] for r in (a0, a1, a2, a3)], fa, attend_cuts, 2 * JOBS + 1 + g, g)]

    ACTIONS = {0: "start_twin", 1: "start_first", 2: "start_second", 3: "start_z", 4: "total"}

    def events(names):
        for step, t in names:
            for one in job(t):
                getattr(one, ACTIONS[step])()

    def when(index, table):
        for value, names in table.items():

            @pl.when(index == value)
            def _():
                events(names)

    in_second.wait()
    low_grad[...] = first[...].astype(bf16)
    in_ws.wait()
    in_we.wait()
    in_lowt.wait()

    def part(j, carry):
        for copy in flow_copies(j):
            copy.wait()

        @pl.when(j + 1 < JOBS)
        def _():
            for copy in flow_copies(j + 1):
                copy.start()

        a_ref, s_ref = active.at[j % 2], slope.at[j % 2]
        rows = pl.ds(aligned(SLICE * j, SLICE), SLICE)
        cols = pl.ds(aligned(PART * j, PART), PART)
        s_in = low_grad[...]
        for h in range(2):
            here = slice(256 * h, 256 * h + 256)
            e_in = dot_nt(s_in, ws[2 * h : 2 * h + 2, :, :, rows, :].reshape(256, D)) * s_ref[:, here].astype(f32)
            e_in = e_in.astype(bf16)
            s_ref[:, here] = e_in
            gain[0, pl.ds(ROW_EXPAND + j, 1), here] = jnp.sum(e_in.astype(f32), axis=0, keepdims=True)
        when(j, FFN_MIDDLE)
        for h in range(2):
            here = slice(256 * h, 256 * h + 256)
            grad = dot_tn(a_ref[:, here], s_in).astype(bf16)
            ws[2 * h : 2 * h + 2, :, :, rows, :] = grad.reshape(2, Y, X, SLICE, D)
        e_in = s_ref[...]
        first[...] += dot_nt(e_in, we[:, :, :, :, cols].reshape(D, PART))
        for h in range(2):
            here = pl.ds(aligned(PART * j + 256 * h, 256), 256)
            grad = dot_nn(turned[...], s_ref[:, 256 * h : 256 * h + 256]).astype(bf16)
            we[:, :, :, :, here] = grad.reshape(Z, Y, X, BLOCK, 256)
        when(j, {t: [(0, t)] for t in range(JOBS)})
        return carry

    lax.fori_loop(0, JOBS, part, 0)
    in_xt = load(xt_any, turned, 13)
    events(AFTER_FFN)
    for copy in later[:4]:
        copy.wait()
    for row in (ROW_MERGE, ROW_GAIN, ROW_SHIFT):
        gain[0, row : row + 1, :] = jnp.zeros((1, D), f32)
    tile = 512

    def middle(i, carry):
        rows = pl.ds(aligned(i * tile, tile), tile)
        dy, x_hat = first[rows, :], xhat[rows, :]
        deviation = jnp.tile(rstd[rows, :], (1, D // LANES))
        grad = norm_back(dy * vec[ROW_GAIN : ROW_GAIN + 1, :], x_hat, deviation)
        first[rows, :] = grad
        branch = grad.astype(bf16)
        low_grad[rows, :] = branch
        gain[0, ROW_GAIN : ROW_GAIN + 1, :] += jnp.sum(dy * x_hat, axis=0, keepdims=True)
        gain[0, ROW_SHIFT : ROW_SHIFT + 1, :] += jnp.sum(dy, axis=0, keepdims=True)
        gain[0, ROW_MERGE : ROW_MERGE + 1, :] += jnp.sum(branch.astype(f32), axis=0, keepdims=True)
        mixed_grad[rows, :] = dot_nt(branch, wm[...].reshape(D, D)).astype(bf16)
        return carry

    lax.fori_loop(0, TOK_DEV // tile, middle, 0)
    events(AFTER_NORM)
    wm[...] = dot_tn(mixed[...], low_grad[...]).astype(bf16).reshape(Z, Y, X, BLOCK, D)
    events([(0, JOBS)])
    for copy in later[4:]:
        copy.wait()
    in_xt.wait()

    def heads(i, carry):
        when(i, HEADS_BEFORE)
        attend_backward(i, query_const, key_const, q, k, v, mixed, logsum, mixed_grad, q, k, v, LONG)

        @pl.when(i % 4 == 3)
        def _():
            cols = pl.ds(aligned(256 * (i // 4), 256), 256)
            for n, grads in enumerate((q, k, v)):
                grad = dot_nn(turned[...], grads[:, cols]).astype(bf16)
                ga[:, :, :, n, :, cols] = grad.reshape(Z, Y, X, BLOCK, 256)
                if n != 1:
                    gain[0, n // 2 : n // 2 + 1, cols] = jnp.sum(grads[:, cols].astype(f32), axis=0, keepdims=True)

        when(i, {4 * g + 3: [(0, JOBS + 1 + g)] for g in range(3)})
        return carry

    lax.fori_loop(0, 12, heads, 0)

    def vec_copy(step, m, peer):
        return remote(gain.at[step], vec_land.at[step + m], vec_send.at[step + m], vec_recv.at[step + m], peer)

    vec_steps = [vec_copy(0, 0, place.twin), vec_copy(1, 0, place.over_x), vec_copy(2, 0, place.over_y)]
    vec_last = [vec_copy(3, m, place.over_z[m]) for m in range(3)]
    vec_steps[0].start()
    in_g = load(g_any, mixed, 14)

    half, ff_half = BLOCK // 2, FF_BLOCK // 2

    def last_copy(ref, n, cols, height):
        rows = pl.ds(aligned(height * (1 - c), 8), height)
        here = ref.at[:, rows, cols] if len(ref.shape) == 3 else ref.at[rows, cols]
        return remote(here, here, last_send.at[n], last_recv.at[n], place.twin)

    early_last = [last_copy(fm, 0, merge_cuts(c)[0].cols, half), last_copy(fs, 1, merge_cuts(c)[0].cols, ff_half)]
    early_last += [last_copy(fe, 2 + j, expand_cuts(c, j)[0].cols, half) for j in range(JOBS)]
    attend_last = [last_copy(fa, 2 + JOBS + g, attend_cuts(c, g)[0].cols, half) for g in range(3)]

    events(TAIL[0])
    vec_steps[0].wait_recv()
    gain[1] = gain[0] + vec_land[0]
    vec_steps[1].start()
    for copy in early_last:
        copy.start()
    in_g.wait()

    def inputs_part(i, carry):
        rows = pl.ds(aligned(i * tile, tile), tile)
        keep = jnp.tile(keep_table[rows, :], (1, D // LANES)) > 0.0
        total = first[rows, :] + jnp.where(keep, 0.0, mixed[rows, :].astype(f32))
        for n, grads in enumerate((q, k, v)):
            total += dot_nt(grads[rows, :], wa[:, :, :, n, :, :].reshape(D, D))
        first[rows, :] = total

        @pl.when(i == 0)
        def _():
            events(TAIL[1])
            vec_steps[1].wait_recv()
            gain[2] = gain[1] + vec_land[1]
            vec_steps[2].start()

        return carry

    lax.fori_loop(0, TOK_DEV // tile, inputs_part, 0)
    out_ig = pltpu.make_async_copy(first, ig_any, local.at[15])
    out_ig.start()
    events(TAIL[2])
    vec_steps[2].wait_recv()
    gain[3] = gain[2] + vec_land[2]
    for copy in vec_last:
        copy.start()
    attend_last[0].start()
    attend_last[1].start()
    for copy in early_last:
        copy.wait_recv()
    mine, ff_mine = pl.ds(aligned(half * c, 8), half), pl.ds(aligned(ff_half * c, 8), ff_half)
    gm_out[...] = fm[mine, :]
    ge_out[...] = fe[mine, :]
    gs_out[...] = fs[ff_mine, :]
    events(TAIL[3])
    attend_last[2].start()
    for copy in vec_last:
        copy.wait_recv()
    vec_out[...] = gain[3] + vec_land[3] + vec_land[4] + vec_land[5]
    for copy in early_last:
        copy.wait_send()
    for copy in vec_steps + vec_last:
        copy.wait_send()
    for t in range(JOBS + 4):
        for one in job(t):
            one.finish()
    for copy in attend_last:
        copy.wait_recv()
        copy.wait_send()
    for n in range(3):
        ga_out[:, D * n : D * n + D] = fa[n, mine, :]
    out_ig.wait()


FFN_MIDDLE = {
    1: [(1, 0)],
    2: [(1, 1)],
    3: [(2, 0), (1, 2)],
    4: [(2, 1), (1, 3)],
    5: [(1, 4)],
}
AFTER_FFN = [(3, 0), (2, 2)]
AFTER_NORM = [(1, 5), (3, 1)]
HEADS_BEFORE = {
    0: [(2, 3)],
    1: [(1, 6), (4, 0)],
    2: [(3, 2), (4, 1)],
    3: [(2, 4)],
    4: [(3, 3), (4, 2)],
    5: [(2, 5), (1, 7)],
    6: [(3, 4)],
    7: [(2, 6), (4, 3)],
    8: [(3, 5)],
    9: [(1, 8), (4, 4)],
    10: [(2, 7), (3, 6)],
    11: [(4, 5)],
}
TAIL = [
    [(1, 9), (3, 7), (2, 8), (4, 6)],
    [(2, 9), (3, 8), (4, 7)],
    [(3, 9), (4, 8)],
    [(4, 9)],
]


def backward_call(buckets, lengths, keeps, weights, saved, upstream, vec, gain):
    dma = pltpu.SemaphoreType.DMA

    def landing(jobs, rows, cols, deep=(), slots=None):
        lead = (jobs,) if jobs else ()
        return [
            pltpu.VMEM(((slots,) if slots else lead) + (Z, Y, X) + deep + (rows, cols), bf16),
            pltpu.VMEM(lead + (Z, 2) + deep + (rows, cols), bf16),
            pltpu.VMEM(lead + (Z,) + deep + (rows, cols), bf16),
            pltpu.VMEM(lead + (3,) + deep + (rows, cols), bf16),
        ]

    n_sums = 4 + 2 * JOBS
    half, ff_half = BLOCK // 2, FF_BLOCK // 2
    return pl.pallas_call(
        backward_kernel,
        out_shape=(
            shape((T, D), f32), shape((half, 3 * D), f32), shape((half, D), f32), shape((half, FF), f32),
            shape((ff_half, D), f32), shape((VEC_ROWS, D), f32),
        ),
        in_specs=[SM, SM, SM] + [ANY] * 15 + [VM, VM],
        out_specs=[ANY] + [VM] * 5,
        scratch_shapes=[pltpu.VMEM(*s) for s in WEIGHTS]
        + [pltpu.VMEM(*WEIGHTS[0])]
        + landing(3, BLOCK, 128, (3,))
        + landing(0, BLOCK, 384)
        + landing(JOBS, BLOCK, 256, slots=2)
        + landing(JOBS, SLICE, 384, slots=2)
        + [
            pltpu.VMEM((3, BLOCK, D), f32),
            pltpu.VMEM((BLOCK, D), f32),
            pltpu.VMEM((BLOCK, FF), f32),
            pltpu.VMEM((FF_BLOCK, D), f32),
            pltpu.VMEM((T, D), bf16),
            pltpu.VMEM((T, D), bf16),
            pltpu.VMEM((T, D), bf16),
            pltpu.VMEM((T, LANES), bf16),
            pltpu.VMEM((T, LANES), bf16),
            pltpu.VMEM((T, LANES), f32),
            pltpu.VMEM((T, D), bf16),
            pltpu.VMEM((T, LANES), f32),
            pltpu.VMEM((T, D), f32),
            pltpu.VMEM((T, LANES), f32),
            pltpu.VMEM((D, T), bf16),
            pltpu.VMEM((T, D), bf16),
            pltpu.VMEM((2, T, PART), bf16),
            pltpu.VMEM((2, T, PART), bf16),
            pltpu.VMEM((T, D), f32),
            pltpu.VMEM((T, D), bf16),
            pltpu.VMEM((4, VEC_ROWS, D), f32),
            pltpu.VMEM((6, VEC_ROWS, D), f32),
            dma((n_sums, 2, 5)),
            dma((n_sums, 2, 5)),
            dma((n_sums,)),
            dma((n_sums,)),
            dma((5 + JOBS,)),
            dma((5 + JOBS,)),
            dma((6,)),
            dma((6,)),
            dma((16,)),
            dma((2, 2)),
        ],
        compiler_params=pltpu.CompilerParams(collective_id=1, has_side_effects=True, vmem_limit_bytes=VMEM_LIMIT),
        cost_estimate=pl.CostEstimate(flops=40_000_000_000, bytes_accessed=60_000_000, transcendentals=10_000_000),
    )(buckets, lengths, keeps, *weights, *saved, upstream, vec, gain)

def layer_norm(hidden, gains, shifts):
    center = hidden - jnp.mean(hidden, axis=-1, keepdims=True)
    spread = jnp.mean(center * center, axis=-1, keepdims=True)
    return center * lax.rsqrt(spread + epsilon) * gains + shifts


def gelu_exact(values):
    return jax.nn.gelu(values, approximate=False)


def matmul(left, right):
    return jnp.dot(left, right, preferred_element_type=jnp.float32)


def token_info(bucket, slot_lengths, slot_keeps):
    position = jnp.arange(TOK_DEV, dtype=jnp.int32)
    span_size = jnp.where(bucket > 0, LONG, SHORT).astype(jnp.int32)
    sequence = position // span_size
    within = position - sequence * span_size
    slot_index = sequence * (span_size // SHORT)
    matches = (slot_index[:, None] == jnp.arange(SLOTS, dtype=jnp.int32)[None, :]).astype(jnp.int32)
    length = jnp.sum(matches * slot_lengths[None, :], axis=1) + bucket * (LONG - SHORT)
    keep_flags = jnp.sum(matches * slot_keeps[None, :], axis=1)
    return (sequence, within < length, keep_flags > 0)


def masked_scores(queries, key_rows, sequence, valid_key):
    scores = jnp.einsum("qhd,khd->hqk", queries, key_rows, preferred_element_type=jnp.float32)
    allowed = (sequence[:, None] == sequence[None, :]) & valid_key[None, :]
    return jnp.where(allowed[None], scores, masked_score)


def attend_block(pieces):
    queries, key_rows, values, sequence, valid_key = pieces
    scores = masked_scores(queries, key_rows, sequence, valid_key)
    highest = jnp.max(scores, axis=-1, keepdims=True)
    raised = jnp.exp(scores - highest)
    row_total = jnp.sum(raised, axis=-1, keepdims=True)
    weights = raised / row_total
    mixed_rows = jnp.einsum(
        "hqk,khd->qhd", weights.astype(jnp.bfloat16), values, preferred_element_type=jnp.float32
    )
    return (mixed_rows, highest[:, :, 0] + jnp.log(row_total[:, :, 0]))


def attend_back(pieces):
    queries, key_rows, values, sequence, valid_key, logsum, mixed_grad = pieces
    scores = masked_scores(queries, key_rows, sequence, valid_key)
    weights = jnp.exp(scores - logsum[:, :, None])
    weight_grad = jnp.einsum("qhd,khd->hqk", mixed_grad, values, preferred_element_type=jnp.float32)
    row_dot = jnp.sum(weights * weight_grad, axis=-1, keepdims=True)
    score_grad = (weights * (weight_grad - row_dot)).astype(jnp.bfloat16)
    query_part = jnp.einsum(
        "hqk,khd->qhd", score_grad, key_rows, preferred_element_type=jnp.float32
    ).astype(jnp.bfloat16)
    key_part = jnp.einsum(
        "hqk,qhd->khd", score_grad, queries, preferred_element_type=jnp.float32
    ).astype(jnp.bfloat16)
    value_part = jnp.einsum(
        "hqk,qhd->khd", weights.astype(jnp.bfloat16), mixed_grad, preferred_element_type=jnp.float32
    ).astype(jnp.bfloat16)
    return (query_part, key_part, value_part)


def heads_view(source):
    return source.reshape(source.shape[0] // LONG, LONG, HEADS, HD)


def forward_pass(inputs, weights, sequence, valid_key, keep_flags):
    (
        attend_matrix,
        attend_offset,
        merge_matrix,
        merge_offset,
        expand_matrix,
        expand_offset,
        shrink_matrix,
        shrink_offset,
        gains,
        shifts,
    ) = weights
    model_width = inputs.shape[1]
    blocks = inputs.shape[0] // LONG
    packed = matmul(inputs, attend_matrix)
    offset = attend_offset.astype(jnp.float32)
    queries = ((packed[:, :model_width] + offset[:model_width]) * 0.125).astype(jnp.bfloat16)
    key_rows = packed[:, model_width : 2 * model_width].astype(jnp.bfloat16)
    values = (packed[:, 2 * model_width :] + offset[model_width:]).astype(jnp.bfloat16)
    mixed_rows, logsum = lax.map(
        attend_block,
        (
            heads_view(queries),
            heads_view(key_rows),
            heads_view(values),
            sequence.reshape(blocks, LONG),
            valid_key.reshape(blocks, LONG),
        ),
    )
    mixed_rows = mixed_rows.reshape(-1, model_width).astype(jnp.bfloat16)
    tokens = inputs.astype(jnp.float32)
    first_sum = tokens + matmul(mixed_rows, merge_matrix) + merge_offset.astype(jnp.float32)
    normed = layer_norm(first_sum, gains[0].astype(jnp.float32), shifts[0].astype(jnp.float32))
    normed_low = normed.astype(jnp.bfloat16)
    expanded = matmul(normed_low, expand_matrix) + expand_offset.astype(jnp.float32)
    active = gelu_exact(expanded).astype(jnp.bfloat16)
    second_sum = normed + matmul(active, shrink_matrix) + shrink_offset.astype(jnp.float32)
    result = layer_norm(second_sum, gains[1].astype(jnp.float32), shifts[1].astype(jnp.float32))
    outputs = jnp.where(keep_flags[:, None], result, tokens).astype(jnp.bfloat16)
    return (
        outputs,
        (
            queries,
            key_rows,
            values,
            logsum,
            mixed_rows,
            first_sum,
            normed_low,
            expanded,
            active,
            second_sum,
        ),
    )


def backward_pass(inputs, upstream, weights, saved, sequence, valid_key, keep_flags):
    (
        attend_matrix,
        attend_offset,
        merge_matrix,
        merge_offset,
        expand_matrix,
        expand_offset,
        shrink_matrix,
        shrink_offset,
        gains,
        shifts,
    ) = weights
    (
        queries,
        key_rows,
        values,
        logsum,
        mixed_rows,
        first_sum,
        normed_low,
        expanded,
        active,
        second_sum,
    ) = saved
    model_width = inputs.shape[1]
    blocks = inputs.shape[0] // LONG
    cotangent = upstream.astype(jnp.float32)
    result_grad = jnp.where(keep_flags[:, None], cotangent, 0.0)
    second_out, pull_second = jax.vjp(
        layer_norm, second_sum, gains[1].astype(jnp.float32), shifts[1].astype(jnp.float32)
    )
    second_grad, gain_two, shift_two = pull_second(result_grad)
    shrink_in = second_grad.astype(jnp.bfloat16)
    shrink_grad = jnp.einsum("tf,td->fd", active, shrink_in, preferred_element_type=jnp.float32)
    shrink_offset_grad = jnp.sum(shrink_in.astype(jnp.float32), axis=0)
    active_grad = jnp.einsum(
        "td,fd->tf", shrink_in, shrink_matrix, preferred_element_type=jnp.float32
    )
    gelu_out, pull_gelu = jax.vjp(gelu_exact, expanded)
    expand_in = pull_gelu(active_grad)[0].astype(jnp.bfloat16)
    expand_grad = jnp.einsum("td,tf->df", normed_low, expand_in, preferred_element_type=jnp.float32)
    expand_offset_grad = jnp.sum(expand_in.astype(jnp.float32), axis=0)
    normed_grad = second_grad + jnp.einsum(
        "tf,df->td", expand_in, expand_matrix, preferred_element_type=jnp.float32
    )
    first_out, pull_first = jax.vjp(
        layer_norm, first_sum, gains[0].astype(jnp.float32), shifts[0].astype(jnp.float32)
    )
    first_grad, gain_one, shift_one = pull_first(normed_grad)
    branch_in = first_grad.astype(jnp.bfloat16)
    merge_grad = jnp.einsum("td,te->de", mixed_rows, branch_in, preferred_element_type=jnp.float32)
    merge_offset_grad = jnp.sum(branch_in.astype(jnp.float32), axis=0)
    mixed_grad = jnp.einsum(
        "te,de->td", branch_in, merge_matrix, preferred_element_type=jnp.float32
    ).astype(jnp.bfloat16)
    query_part, key_part, value_part = lax.map(
        attend_back,
        (
            heads_view(queries),
            heads_view(key_rows),
            heads_view(values),
            sequence.reshape(blocks, LONG),
            valid_key.reshape(blocks, LONG),
            logsum,
            heads_view(mixed_grad),
        ),
    )
    query_grad = query_part.reshape(-1, model_width) * 0.125
    packed_grad = jnp.concatenate(
        [query_grad, key_part.reshape(-1, model_width), value_part.reshape(-1, model_width)], axis=1
    )
    attend_grad = jnp.einsum("td,te->de", inputs, packed_grad, preferred_element_type=jnp.float32)
    attend_offset_grad = jnp.concatenate(
        [
            jnp.sum(query_grad.astype(jnp.float32), axis=0),
            jnp.sum(value_part.reshape(-1, model_width).astype(jnp.float32), axis=0),
        ]
    )
    input_grad = (
        first_grad
        + jnp.einsum("te,de->td", packed_grad, attend_matrix, preferred_element_type=jnp.float32)
        + jnp.where(keep_flags[:, None], 0.0, cotangent)
    )
    gain_grad = jnp.stack([gain_one, gain_two])
    shift_grad = jnp.stack([shift_one, shift_two])
    grads = (
        attend_grad,
        attend_offset_grad,
        merge_grad,
        merge_offset_grad,
        expand_grad,
        expand_offset_grad,
        shrink_grad,
        shrink_offset_grad,
        gain_grad,
        shift_grad,
    )
    return (grads, input_grad)


def general_device(
    inputs,
    upstream,
    buckets,
    lengths,
    layer_keep,
    attend_weight,
    attend_bias,
    merge_weight,
    merge_bias,
    expand_weight,
    expand_bias,
    shrink_weight,
    shrink_bias,
    norm_gain,
    norm_shift,
):
    sequence, valid_key, keep_flags = token_info(buckets[0], lengths[0], layer_keep[0])
    gathered = (
        lax.all_gather(attend_weight, ("group", "inner"), axis=0, tiled=True),
        lax.all_gather(attend_bias, ("group", "inner"), axis=0, tiled=True),
        lax.all_gather(merge_weight, ("group", "inner"), axis=0, tiled=True),
        lax.all_gather(merge_bias, ("group", "inner"), axis=0, tiled=True),
        lax.all_gather(expand_weight, ("group", "inner"), axis=0, tiled=True),
        lax.all_gather(expand_bias, ("group", "inner"), axis=0, tiled=True),
        lax.all_gather(shrink_weight, ("group", "inner"), axis=0, tiled=True),
        lax.all_gather(shrink_bias, ("group", "inner"), axis=0, tiled=True),
        lax.all_gather(norm_gain, ("group", "inner"), axis=1, tiled=True),
        lax.all_gather(norm_shift, ("group", "inner"), axis=1, tiled=True),
    )
    outputs, saved = forward_pass(inputs, gathered, sequence, valid_key, keep_flags)
    gathered = (
        lax.all_gather(attend_weight, ("group", "inner"), axis=0, tiled=True),
        lax.all_gather(attend_bias, ("group", "inner"), axis=0, tiled=True),
        lax.all_gather(merge_weight, ("group", "inner"), axis=0, tiled=True),
        lax.all_gather(merge_bias, ("group", "inner"), axis=0, tiled=True),
        lax.all_gather(expand_weight, ("group", "inner"), axis=0, tiled=True),
        lax.all_gather(expand_bias, ("group", "inner"), axis=0, tiled=True),
        lax.all_gather(shrink_weight, ("group", "inner"), axis=0, tiled=True),
        lax.all_gather(shrink_bias, ("group", "inner"), axis=0, tiled=True),
        lax.all_gather(norm_gain, ("group", "inner"), axis=1, tiled=True),
        lax.all_gather(norm_shift, ("group", "inner"), axis=1, tiled=True),
    )
    grads, input_grad = backward_pass(
        inputs, upstream, gathered, saved, sequence, valid_key, keep_flags
    )
    shares = (
        lax.psum_scatter(grads[0], ("group", "inner"), scatter_dimension=0, tiled=True),
        lax.psum_scatter(grads[1], ("group", "inner"), scatter_dimension=0, tiled=True),
        lax.psum_scatter(grads[2], ("group", "inner"), scatter_dimension=0, tiled=True),
        lax.psum_scatter(grads[3], ("group", "inner"), scatter_dimension=0, tiled=True),
        lax.psum_scatter(grads[4], ("group", "inner"), scatter_dimension=0, tiled=True),
        lax.psum_scatter(grads[5], ("group", "inner"), scatter_dimension=0, tiled=True),
        lax.psum_scatter(grads[6], ("group", "inner"), scatter_dimension=0, tiled=True),
        lax.psum_scatter(grads[7], ("group", "inner"), scatter_dimension=0, tiled=True),
        lax.psum_scatter(grads[8], ("group", "inner"), scatter_dimension=1, tiled=True),
        lax.psum_scatter(grads[9], ("group", "inner"), scatter_dimension=1, tiled=True),
    )
    return (
        outputs,
        input_grad,
        shares[0],
        shares[1],
        shares[2],
        shares[3],
        shares[4],
        shares[5],
        shares[6],
        shares[7],
        shares[8],
        shares[9],
    )

def slice_device(
    inputs, upstream, buckets, lengths, layer_keep, attend_weight, attend_bias, merge_weight, merge_bias,
    expand_weight, expand_bias, shrink_weight, shrink_bias, norm_gain, norm_shift,
):
    pack = pack_weights(attend_weight, merge_weight, expand_weight)
    pieces = pack_pieces(attend_bias, merge_bias, expand_bias, shrink_bias, norm_gain, norm_shift)
    results = forward_call(buckets, lengths, layer_keep, inputs, upstream, pack, shrink_weight, pieces)
    outputs, weights, saved, vec, gain = results[0], results[1:5], results[5:-2], results[-2], results[-1]
    input_grad, attend, merge, expand, shrink, sums = backward_call(
        buckets, lengths, layer_keep, weights, saved, upstream, vec, gain
    )
    expand = expand.reshape(-1, JOBS, CHIPS, SLICE).transpose(0, 2, 1, 3).reshape(-1, FF)
    group, inner = lax.axis_index("group"), lax.axis_index("inner")
    index = group * (2 * X) + inner
    chip, core = index // 2, index % 2
    width = D // (2 * CHIPS)
    at = width * index

    def cut(rows, count):
        return lax.dynamic_slice(sums, (rows, at), (count, width))

    return (
        outputs,
        input_grad,
        attend,
        lax.dynamic_slice(sums[:2].reshape(-1), (2 * at,), (2 * width,)),
        merge,
        cut(ROW_MERGE, 1)[0],
        expand,
        lax.dynamic_slice(sums, (ROW_EXPAND + 3 * core, SLICE * chip), (3, SLICE)).reshape(-1),
        shrink,
        cut(ROW_SHRINK, 1)[0],
        cut(ROW_GAIN, 2),
        cut(ROW_SHIFT, 2),
    )

def solution(mesh):
    on_slice = mesh.shape["group"] == Z * Y and mesh.shape["inner"] == 2 * X
    placed = (
        P(("group", "inner"), None),
        P(("group", "inner"), None),
        P(("group", "inner")),
        P(("group", "inner"), None),
        P(("group", "inner"), None),
        P(("group", "inner"), None),
        P(("group", "inner")),
        P(("group", "inner"), None),
        P(("group", "inner")),
        P(("group", "inner"), None),
        P(("group", "inner")),
        P(("group", "inner"), None),
        P(("group", "inner")),
        P(None, ("group", "inner")),
        P(None, ("group", "inner")),
    )
    return jax.shard_map(
        slice_device if on_slice else general_device,
        mesh=mesh,
        in_specs=placed,
        out_specs=(
            P(("group", "inner"), None),
            P(("group", "inner"), None),
            P(("group", "inner"), None),
            P(("group", "inner")),
            P(("group", "inner"), None),
            P(("group", "inner")),
            P(("group", "inner"), None),
            P(("group", "inner")),
            P(("group", "inner"), None),
            P(("group", "inner")),
            P(None, ("group", "inner")),
            P(None, ("group", "inner")),
        ),
        check_vma=False,
    )
```

```python
import jax
import jax.numpy as jnp
from jax import lax
from jax.experimental import pallas as pl
from jax.experimental.pallas import tpu as pltpu
from jax.sharding import PartitionSpec as P

HEADS = 12
HD = 64
LONG = 512
SHORT = 128
TOK_DEV = 1024
SLOTS = 8
D = 768
FF = 3072
LANES = 128
RSTD_LANE, KEEP_LANE = 12, 13
epsilon = 1e-05
masked_score = -1e30
f32 = jnp.float32
bf16 = jnp.bfloat16


def dot_nn(a, b):
    return lax.dot_general(a, b, (((1,), (0,)), ((), ())), preferred_element_type=f32)


def dot_nt(a, b):
    return lax.dot_general(a, b, (((1,), (1,)), ((), ())), preferred_element_type=f32)


def dot_tn(a, b):
    return lax.dot_general(a, b, (((0,), (0,)), ((), ())), preferred_element_type=f32)


def lane_index(rows):
    return lax.broadcasted_iota(jnp.int32, (rows, LANES), 1)


def token_tables(bucket, lengths, keeps, query_const, key_const, columns):
    shape = (TOK_DEV, LANES)
    position = lax.broadcasted_iota(jnp.int32, shape, 0)
    is_long = jnp.broadcast_to(bucket, shape) > 0
    slot = jnp.where(is_long, (position >> 9) << 2, position >> 7)
    offset = jnp.where(is_long, position & (LONG - 1), position & (SHORT - 1))
    length = jnp.zeros(shape, jnp.int32)
    keep = jnp.zeros(shape, jnp.int32)
    for b in range(SLOTS):
        here = slot == b
        length = jnp.where(here, lengths[b], length)
        keep = jnp.where(here, keeps[b], keep)
    length = length + bucket * (LONG - SHORT)
    valid = offset < length
    within = jnp.where(is_long, 0, (position >> 7) & 3)
    lane = lax.broadcasted_iota(jnp.int32, shape, 1) & (HD - 1)
    is_span = (lane >= 4) & (lane < 8)
    same = lane - 4 == within
    zero, one = jnp.zeros(shape, f32), jnp.ones(shape, f32)
    query_const[...] = jnp.where(lane == 3, one, jnp.where(is_span & ~same, one, zero)).astype(bf16)
    key_const[...] = jnp.where(
        lane < 3,
        one,
        jnp.where(((lane == 3) & ~valid) | (is_span & same), masked_score * one, zero),
    ).astype(bf16)
    columns[...] = jnp.where((lane_index(TOK_DEV) == KEEP_LANE) & (keep > 0), one, zero)


def column_of(columns, lane):
    return jnp.sum(jnp.where(lane_index(columns.shape[0]) == lane, columns, 0.0), axis=1, keepdims=True)


def three_parts(column, rows):
    wide = jnp.broadcast_to(column, (rows, LANES))
    high = wide.astype(bf16)
    rest = wide - high.astype(f32)
    middle = rest.astype(bf16)
    low = (rest - middle.astype(f32)).astype(bf16)
    return high, middle, low


def attend_forward(index, query_const, key_const, q_ref, k_ref, v_ref, mixed_ref, logsum_ref, tile):
    pair, block = index // 2, index % 2
    cols = pl.ds(pl.multiple_of(pair * LANES, LANES), LANES)
    rows = pl.ds(pl.multiple_of(block * LONG, LONG), LONG)
    lane_k = lane_index(LONG)
    k2, v2 = k_ref[rows, cols], v_ref[rows, cols]
    kc = key_const[rows, :]
    k_aug = [jnp.where((lane_k // HD) == half, k2, kc) for half in range(2)]
    lane_q = lane_index(tile)
    for t in range(LONG // tile):
        qrows = pl.ds(pl.multiple_of(block * LONG + t * tile, tile), tile)
        q2, qc = q_ref[qrows, cols], query_const[qrows, :]
        outs = []
        sums = logsum_ref[qrows, :]
        for half in range(2):
            q_aug = jnp.where((lane_q // HD) == half, q2, qc)
            scores = dot_nt(q_aug, k_aug[half])
            highest = jnp.max(scores, axis=1, keepdims=True)
            raised = jnp.exp(scores - highest)
            total = jnp.sum(raised, axis=1, keepdims=True)
            out = dot_nn(raised.astype(bf16), v2)
            outs.append(out * (1.0 / total))
            sums = jnp.where(lane_q == 2 * pair + half, highest + jnp.log(total), sums)
        logsum_ref[qrows, :] = sums
        mixed_ref[qrows, cols] = jnp.where(lane_q < HD, outs[0], outs[1]).astype(bf16)


def attend_backward(index, query_const, key_const, q_ref, k_ref, v_ref, mixed_ref, logsum_ref, mixed_grad_ref,
                    dq_ref, dk_ref, dv_ref, tile):
    pair, block = index // 2, index % 2
    cols = pl.ds(pl.multiple_of(pair * LANES, LANES), LANES)
    rows = pl.ds(pl.multiple_of(block * LONG, LONG), LONG)
    lane = lane_index(LONG)
    q2, dm2 = q_ref[rows, cols], mixed_grad_ref[rows, cols]
    product = dm2.astype(f32) * mixed_ref[rows, cols].astype(f32)
    sums = logsum_ref[rows, :]
    qc = query_const[rows, :]
    zero = jnp.zeros((LONG, LANES), bf16)
    q_aug, d_aug = [], []
    for half in range(2):
        mine = (lane // HD) == half
        at = lane & (HD - 1)
        logsum = jnp.sum(jnp.where(lane == 2 * pair + half, sums, 0.0), axis=1, keepdims=True)
        delta = jnp.sum(jnp.where(mine, product, 0.0), axis=1, keepdims=True)
        lh, lm, ll = three_parts(-logsum, LONG)
        dh, dm, dl = three_parts(-delta, LONG)
        extra = jnp.where(at == 0, lh, jnp.where(at == 1, lm, jnp.where(at == 2, ll, qc)))
        q_aug.append(jnp.where(mine, q2, extra))
        extra = jnp.where(at == 0, dh, jnp.where(at == 1, dm, jnp.where(at == 2, dl, zero)))
        d_aug.append(jnp.where(mine, dm2, extra))
    dq = [jnp.zeros((LONG, LANES), f32) for _ in range(2)]
    lane_t = lane_index(tile)
    one = jnp.ones((tile, LANES), bf16)
    zero_t = jnp.zeros((tile, LANES), bf16)
    for t in range(LONG // tile):
        krows = pl.ds(pl.multiple_of(block * LONG + t * tile, tile), tile)
        k2, v2, kc = k_ref[krows, cols], v_ref[krows, cols], key_const[krows, :]
        vc = jnp.where((lane_t & (HD - 1)) < 3, one, zero_t)
        dk, dv = [], []
        for half in range(2):
            mine = (lane_t // HD) == half
            weights = jnp.exp(dot_nt(jnp.where(mine, k2, kc), q_aug[half]))
            grads = weights * dot_nt(jnp.where(mine, v2, vc), d_aug[half])
            low, low_grads = weights.astype(bf16), grads.astype(bf16)
            dv.append(dot_nn(low, dm2))
            dk.append(dot_nn(low_grads, q2))
            dq[half] = dq[half] + dot_tn(low_grads, k2)
        dk_ref[krows, cols] = jnp.where(lane_t < HD, dk[0], dk[1]).astype(bf16)
        dv_ref[krows, cols] = jnp.where(lane_t < HD, dv[0], dv[1]).astype(bf16)
    dq_ref[rows, cols] = (jnp.where(lane < HD, dq[0], dq[1]).astype(bf16).astype(f32) * 0.125).astype(bf16)


def gelu_parts(x):
    z = jnp.abs(x) * 0.7071067811865476
    t = 1.0 / (1.0 + 0.3275911 * z)
    bell = jnp.exp(-z * z)
    tail = t * (0.127414796 + t * (-0.142248368 + t * (0.7107068705 + t * (-0.7265760135 + t * 0.5307027145)))) * bell
    phi = jnp.where(x >= 0.0, 1.0 - tail, tail)
    return x * phi, phi + x * (bell * 0.3989422804014327)


def norm_parts(x):
    center = x - jnp.mean(x, axis=-1, keepdims=True)
    spread = jnp.mean(center * center, axis=-1, keepdims=True)
    rstd = lax.rsqrt(spread + epsilon)
    return center * rstd, rstd


def norm_back(dy_hat, x_hat, rstd):
    a = jnp.mean(dy_hat, axis=-1, keepdims=True)
    b = jnp.mean(dy_hat * x_hat, axis=-1, keepdims=True)
    return rstd * (dy_hat - a - x_hat * b)

MESH = pl.DeviceIdType.MESH
Z, X, Y = 4, 2, 2
CHIPS = Z * Y * X
JOBS = 6
PART = FF // JOBS
BLOCK = D // CHIPS
FF_BLOCK = FF // CHIPS
SLICE = FF_BLOCK // JOBS
ALL = slice(None)


def aligned(value, unit):
    return pl.multiple_of(value, unit)


class Place:
    def __init__(self):
        group, inner = lax.axis_index("group"), lax.axis_index("inner")
        self.z, self.y, self.x, self.c = group // Y, group % Y, inner // 2, inner % 2
        self.index = group * (X * 2) + inner
        self.chip = group * X + self.x
        self.twin = (group, self.x * 2 + 1 - self.c)
        self.over = {
            "x": ((1 - self.x, (group, (1 - self.x) * 2 + self.c)),),
            "y": ((1 - self.y, (self.z * Y + 1 - self.y, inner)),),
            "z": tuple(
                (z, (z * Y + self.y, inner))
                for z in (self.z + 1 - 2 * (self.z % 2), (self.z + 2) % Z, Z - 1 - self.z)
            ),
        }
        self.peers = (self.twin,) + tuple(peer for axis in "xyz" for _, peer in self.over[axis])

    def greet(self):
        barrier = pltpu.get_barrier_semaphore()
        for peer in self.peers:
            pl.semaphore_signal(barrier, 1, device_id=peer, device_id_type=MESH)

    def met(self):
        pl.semaphore_wait(pltpu.get_barrier_semaphore(), len(self.peers))

    def at(self, whole, **given):
        return tuple(given[a] if a in given else ALL if a in whole else getattr(self, a) for a in "zyx")


def remote(source, target, send, recv, peer):
    return pltpu.make_async_remote_copy(
        src_ref=source, dst_ref=target, send_sem=send, recv_sem=recv, device_id=peer, device_id_type=MESH
    )


class Cut:
    def __init__(self, rows, cols, order=None, near=(ALL, ALL)):
        self.rows, self.cols, self.order, self.near = rows, cols, order, near


def row_parts(start, low, high, cols):
    return (
        Cut(pl.ds(aligned(start, 16), low), cols, "zxy", (pl.ds(0, low), ALL)),
        Cut(pl.ds(aligned(start + low, 16), high), cols, "zyx", (pl.ds(low, high), ALL)),
    )


def attend_cuts(core, g):
    cols = pl.ds(aligned(256 * g + 128 * core, 128), 128)
    low, high = (16, 32) if g % 2 == 0 else (32, 16)
    return Cut(pl.ds(0, BLOCK), cols), row_parts(0, low, high, cols)


def merge_cuts(core):
    cols = pl.ds(aligned(384 * core, 128), 384)
    return Cut(pl.ds(0, BLOCK), cols), row_parts(0, 32, 16, cols)


def expand_cuts(core, j):
    at = PART * j + 256 * core
    rows = pl.ds(0, BLOCK)
    return Cut(rows, pl.ds(aligned(at, 128), 256)), tuple(
        Cut(rows, pl.ds(aligned(at + 128 * n, 128), 128), EXPAND_ORDERS[n], (ALL, pl.ds(128 * n, 128)))
        for n in range(2)
    )


EXPAND_ORDERS = ("xzy", "yzx")


def shrink_cuts(core, j):
    cols = pl.ds(aligned(384 * core, 128), 384)
    half = SLICE // 2
    return Cut(pl.ds(aligned(SLICE * j, SLICE), SLICE), cols), row_parts(SLICE * j, half, half, cols)


def blocks(ref, at, cut):
    deep = (ALL,) if len(ref.shape) == 6 else ()
    return ref.at[at + deep + (cut.rows, cut.cols)]


class Gather:
    def __init__(self, place, ref, cuts, send, recv, twin_send, twin_recv):
        self.place, self.ref, (self.whole, self.parts) = place, ref, cuts
        self.send, self.recv, self.twin_send, self.twin_recv = send, recv, twin_send, twin_recv

    def stage(self, n, part, step):
        axis = part.order[step]
        here = blocks(self.ref, self.place.at(part.order[:step]), part)
        first = sum(len(self.place.over[a]) for a in part.order[:step])
        return [
            remote(here, here, self.send.at[n, first + m], self.recv.at[n, first + m], peer)
            for m, (_, peer) in enumerate(self.place.over[axis])
        ]

    def to_twin(self):
        here = blocks(self.ref, self.place.at("zyx"), self.whole)
        return remote(here, here, self.twin_send, self.twin_recv, self.place.twin)

    def run(self, step):
        for n, part in enumerate(self.parts):
            if step > 0:
                for copy in self.stage(n, part, step - 1):
                    copy.wait_recv()
            if step < 3:
                for copy in self.stage(n, part, step):
                    copy.start()
        if step == 3:
            self.to_twin().start()

    def ready(self):
        self.to_twin().wait_recv()

    def finish(self):
        for n, part in enumerate(self.parts):
            for step in range(3):
                for copy in self.stage(n, part, step):
                    copy.wait_send()
        self.to_twin().wait_send()


class Reduce:
    def __init__(self, place, ref, lands, final, cuts, twin_cuts, sems):
        self.place, self.ref, (self.whole, self.parts), self.twin_whole = place, ref, cuts, twin_cuts[0]
        self.lands, self.final = lands, final
        self.send, self.recv, self.twin_send, self.twin_recv = sems
        self.deep = (ALL,) if len(ref.shape) == 6 else ()

    def twin(self):
        source = blocks(self.ref, self.place.at("zyx"), self.twin_whole)
        return remote(source, self.lands[0], self.twin_send, self.twin_recv, self.place.twin)

    def land(self, part, step, m):
        ref = self.lands[step]
        axis, left = part.order[3 - step], part.order[: 3 - step]
        if step == 1:
            lead = (ALL, ALL)
        elif step == 2:
            lead = (m, ALL) if axis == "z" else (ALL,)
        else:
            lead = (m,)
        if step == 2 and axis != "z":
            ref = self.lands[4]
        return ref.at[lead + self.deep + part.near]

    def stage(self, n, part, step):
        axis, left = part.order[3 - step], part.order[: 3 - step]
        first = sum(len(self.place.over[a]) for a in part.order[4 - step :])
        return [
            remote(
                blocks(self.ref, self.place.at(left, **{axis: there}), part), self.land(part, step, m),
                self.send.at[n, first + m], self.recv.at[n, first + m], peer,
            )
            for m, (there, peer) in enumerate(self.place.over[axis])
        ]

    def run(self, step):
        if step == 0:
            self.twin().start()
            return
        if step == 1:
            self.twin().wait_recv()
            mine = blocks(self.ref, self.place.at("zyx"), self.whole)
            mine[...] = (mine[...].astype(f32) + self.lands[0][...].astype(f32)).astype(bf16)
        for n, part in enumerate(self.parts):
            if step > 1:
                left = part.order[: 4 - step]
                mine = blocks(self.ref, self.place.at(left), part)
                value = mine[...].astype(f32)
                for m, copy in enumerate(self.stage(n, part, step - 1)):
                    copy.wait_recv()
                    value += self.land(part, step - 1, m)[...].astype(f32)
                if step < 4:
                    mine[...] = value.astype(bf16)
                else:
                    self.final[self.deep + (part.rows, part.cols)] = value
            if step < 4:
                for copy in self.stage(n, part, step):
                    copy.start()

    def finish(self):
        self.twin().wait_send()
        for n, part in enumerate(self.parts):
            for step in (1, 2, 3):
                for copy in self.stage(n, part, step):
                    copy.wait_send()

T = TOK_DEV
VEC_ROWS = 16
PIECES = 8
ROW_MERGE, ROW_EXPAND, ROW_SHRINK, ROW_GAIN, ROW_SHIFT = 2, 3, 9, 10, 12
HALF, FF_HALF = BLOCK // 2, FF_BLOCK // 2
PACK = 3 * D + D + FF
GATHERS = 4 + 2 * JOBS
WEIGHTS = (
    ((Z, Y, X, 3, BLOCK, D), bf16),
    ((Z, Y, X, BLOCK, D), bf16),
    ((Z, Y, X, BLOCK, FF), bf16),
    ((Z, Y, X, FF_BLOCK, D), bf16),
)
VMEM_LIMIT = 255 * 2**18

G_START = [(0, 0), (0, 1), (1, 0), (0, 5), (0, 2), (1, 1), (2, 1), (2, 0), (0, 3), (1, 2), (0, 6), (0, 4), (1, 3), (1, 5), (3, 0), (2, 2), (1, 4)]
G_HEADS = {
    1: [(1, 6)],
    2: [(2, 3)],
    3: [(3, 1)],
    4: [],
    5: [(3, 2), (0, 8), (1, 7)],
    7: [(2, 4)],
    8: [],
    9: [(2, 6), (3, 5), (0, 9), (3, 3)],
    10: [(1, 8)],
}
G_READY = {
    0: [(0, 7)],
    4: [(2, 5)],
}
G_MERGE = [(3, 4), (2, 7)]
G_FFN = {
    1: [(3, 6), (2, 8)],
    4: [(3, 9)],
}
G_FFN_MIDDLE = {
    0: [(1, 9)],
    2: [(2, 9), (3, 7), (3, 8)],
}
R_FFN = {
}
R_FFN_MIDDLE = {
    1: [(1, 0)],
    2: [(1, 1)],
    3: [(1, 2)],
    4: [(2, 0), (2, 1), (1, 3)],
    5: [(1, 4)],
}
R_NORM = {
    0: [(2, 2)],
}
R_MERGE = []
R_HEADS = {
    2: [(2, 4), (1, 5)],
    4: [(2, 3)],
    5: [(3, 2)],
    6: [(2, 5)],
    7: [(3, 1), (2, 6), (3, 0), (1, 7)],
    8: [(3, 4)],
    9: [(1, 8)],
    11: [(3, 6), (4, 0)],
}
R_HEADS_END = {
    3: [(1, 6)],
    7: [(3, 3)],
    11: [(2, 8)],
}
R_TAIL = [[(3, 5), (2, 7), (1, 9), (4, 2), (3, 8), (4, 6)], [(4, 5)], [(3, 7), (4, 1), (4, 3), (2, 9), (3, 9), (4, 4), (4, 7), (4, 8)], [(4, 9)]]

def chosen(width, offset, start=0):
    source = lax.broadcasted_iota(jnp.int32, (LANES, D), 0)
    target = lax.broadcasted_iota(jnp.int32, (LANES, D), 1)
    mine = (source >= start) & (source < start + width)
    return jnp.where((target == source + (offset - start)) & mine, 1.0, 0.0).astype(bf16)


def vector_maps(place):
    per_row = D // (2 * HALF)
    return (
        chosen(2 * HALF, 2 * HALF * (place.index % per_row)),
        chosen(HALF, HALF * place.index),
        [chosen(SLICE, SLICE * place.chip, SLICE * n) for n in range(3)],
        place.index // per_row,
    )


def place_vectors(place, pieces_ref, out_ref):
    pieces = pieces_ref[...].astype(bf16)
    attend_map, single_map, expand_maps, half = vector_maps(place)
    attend = dot_nn(pieces, attend_map)
    single = dot_nn(pieces, single_map)
    expand = jnp.concatenate([dot_nn(pieces, m)[2:3] for m in expand_maps], axis=0)
    out_ref[...] = jnp.concatenate(
        [
            jnp.where(half == 0, attend[0:1], 0.0),
            jnp.where(half == 1, attend[0:1], 0.0),
            single[1:2],
            jnp.where(place.c == 0, expand, 0.0),
            jnp.where(place.c == 1, expand, 0.0),
            single[3:8],
            jnp.zeros((2, D), f32),
        ],
        axis=0,
    ).astype(bf16)


def own_vectors(place, sums):
    attend_map, single_map, expand_maps, half = vector_maps(place)
    high = sums.astype(bf16)
    rest = sums - high.astype(f32)
    middle = rest.astype(bf16)
    low = (rest - middle.astype(f32)).astype(bf16)
    parts = jnp.concatenate([high, middle, low], axis=0)

    def pick(chosen_map):
        found = dot_nt(parts, chosen_map)
        return found[:VEC_ROWS] + found[VEC_ROWS : 2 * VEC_ROWS] + found[2 * VEC_ROWS :]

    attend, single = pick(attend_map), pick(single_map)
    expand = 0.0
    for n, chosen_map in enumerate(expand_maps):
        found = pick(chosen_map)
        expand += jnp.where(place.c == 0, found[ROW_EXPAND + n], found[ROW_EXPAND + 3 + n])[None]
    return jnp.concatenate(
        [
            jnp.where(half == 0, attend[0:1], attend[1:2]),
            single[ROW_MERGE : ROW_MERGE + 1],
            expand,
            single[ROW_SHRINK : ROW_SHIFT + 2],
        ],
        axis=0,
    )


def lane_groups(read, write, moves):
    for target, sources in enumerate(moves):
        parts = []
        for group, (tile, at) in enumerate(sources):
            value = read(tile)
            shift = (group - at) * SLICE % LANES
            parts.append(pltpu.roll(value, shift, 1) if shift else value)
        lane = lax.broadcasted_iota(jnp.int32, parts[0].shape, 1) // SLICE
        write(target, jnp.where(lane < 2, jnp.where(lane == 0, parts[0], parts[1]), jnp.where(lane == 2, parts[2], parts[3])))


def ff_moves(inverse):
    outer, inner = (JOBS, CHIPS) if not inverse else (CHIPS, JOBS)
    units = [b * outer + a for a in range(outer) for b in range(inner)]
    return [[(u // 4, u % 4) for u in units[4 * t : 4 * t + 4]] for t in range(FF // LANES)]


def compose(place, pack_ref, twin_ref, source_cols):
    mine = pack_ref[:, source_cols].astype(f32)[:HALF]
    other = twin_ref[:, source_cols].astype(f32)[:HALF]
    first = jnp.where(place.c == 0, mine, other)
    second = jnp.where(place.c == 0, other, mine)
    return jnp.concatenate([first, second], axis=0).astype(bf16)


def layer_kernel(
    bucket, lengths, keeps, x_any, g_any, attend_ref, merge_ref, expand_ref, shrink_ref, pieces_ref,
    out_any, ig_any, ga_out, gm_out, ge_out, gs_out, vec_out, active_any, slope_any,
    wa, wm, we, ws, ga, pack, pack_twin, vec_parts, vec_land, vec,
    x, g, q, k, v, query_const, key_const, mixed, logsum, xhat, low, xt, lowt, active, slope, first,
    a0, a1, a3, a4, m0, m1, m3, m4, e0, e1, e2, e3, s0, s1, s3, s4, fa, fm, fe, fs, gain, gain_land,
    g_send, g_recv, gt_send, gt_recv, r_send, r_recv, rt_send, rt_recv, own_send, own_recv, vec_send, vec_recv,
    sum_send, sum_recv, last_send, last_recv, local, flow,
):
    place = Place()
    c = place.c
    place.greet()
    x_copy = pltpu.make_async_copy(x_any, x, local.at[0])
    g_copy = pltpu.make_async_copy(g_any, g, local.at[1])
    x_copy.start()
    g_copy.start()

    pack[0:HALF, 0 : 3 * D] = attend_ref[...]
    pack[0:HALF, 3 * D : 4 * D] = merge_ref[...]

    def put_expand(tile, value):
        pack[0:HALF, 4 * D + LANES * tile : 4 * D + LANES * (tile + 1)] = value.astype(bf16)

    lane_groups(
        lambda tile: expand_ref[:, LANES * tile : LANES * (tile + 1)].astype(f32), put_expand, ff_moves(False)
    )
    place_vectors(place, pieces_ref, vec_parts.at[0])
    token_tables(
        bucket[0], [lengths[0, b] for b in range(SLOTS)], [keeps[0, b] for b in range(SLOTS)],
        query_const, key_const, logsum,
    )
    x_copy.wait()
    xt[...] = x[...].T
    place.met()

    own_pack = remote(pack, pack_twin, own_send.at[0], own_recv.at[0], place.twin)
    own_pack.start()
    their_cols = pl.ds(aligned(384 * (1 - c), 128), 384)
    my_cols = pl.ds(aligned(384 * c, 128), 384)
    my_rows = pl.ds(aligned(FF_HALF * c, FF_HALF), FF_HALF)
    own_shrink = remote(
        shrink_ref.at[:, their_cols], ws.at[place.z, place.y, place.x, my_rows, their_cols],
        own_send.at[1], own_recv.at[1], place.twin,
    )

    def vec_copy(source, land, sends, recvs, step, m, peer):
        return remote(source.at[step], land.at[step + m], sends.at[step + m], recvs.at[step + m], peer)

    def vec_chain(source, land, sends, recvs):
        steps = [(place.twin,)] + [tuple(peer for _, peer in place.over[a]) for a in "xyz"]
        return [[vec_copy(source, land, sends, recvs, s, m, p) for m, p in enumerate(peers)] for s, peers in enumerate(steps)]

    vec_steps = vec_chain(vec_parts, vec_land, vec_send, vec_recv)
    sum_steps = vec_chain(gain, gain_land, sum_send, sum_recv)

    def add_next(steps, source, land, step):
        steps[step][0].wait_recv()
        source[step + 1] = (source[step].astype(f32) + land[step].astype(f32)).astype(source.dtype)
        for copy in steps[step + 1]:
            copy.start()

    def add_last(steps, source, land):
        total = source[3].astype(f32)
        for m, copy in enumerate(steps[3]):
            copy.wait_recv()
            total += land[3 + m].astype(f32)
        return total

    vec_steps[0][0].start()
    own_shrink.start()

    def gathers(t):
        def one(ref, cuts, at):
            return Gather(place, ref, cuts, g_send.at[at], g_recv.at[at], gt_send.at[at], gt_recv.at[at])

        if t < 3:
            return [one(wa, attend_cuts(c, t), t)]
        if t == 3:
            return [one(wm, merge_cuts(c), 3)]
        j = t - 4
        return [one(we, expand_cuts(c, j), 4 + 2 * j), one(ws, shrink_cuts(c, j), 5 + 2 * j)]

    def gather_events(names):
        for step, t in names:
            for one in gathers(t):
                one.run(step)

    def when(index, table, events):
        for value, names in table.items():

            @pl.when(index == value)
            def _():
                events(names)

    own_pack.wait_recv()
    for group in range(3):
        for n in range(3):
            cols = aligned(256 * group + 128 * c, 128)
            wa[place.z, place.y, place.x, n, :, pl.ds(cols, 128)] = compose(
                place, pack, pack_twin, pl.ds(aligned(D * n + cols, 128), 128)
            )
    wm[place.z, place.y, place.x, :, my_cols] = compose(
        place, pack, pack_twin, pl.ds(aligned(3 * D + 384 * c, 128), 384)
    )
    for j in range(JOBS):
        cols = aligned(PART * j + 256 * c, 128)
        we[place.z, place.y, place.x, :, pl.ds(cols, 256)] = compose(
            place, pack, pack_twin, pl.ds(aligned(4 * D + cols, 128), 256)
        )
    ws[place.z, place.y, place.x, my_rows, my_cols] = shrink_ref[:, my_cols]
    own_shrink.wait_recv()
    gather_events(G_START[:2])
    add_next(vec_steps, vec_parts, vec_land, 0)
    gather_events(G_START[2:4])
    add_next(vec_steps, vec_parts, vec_land, 1)
    gather_events(G_START[4:8])
    add_next(vec_steps, vec_parts, vec_land, 2)
    gather_events(G_START[8:])
    vec[...] = add_last(vec_steps, vec_parts, vec_land)

    def heads(i, carry):
        when(i, G_HEADS, gather_events)
        for group in range(3):

            @pl.when(i == 4 * group)
            def _():
                for one in gathers(group):
                    one.ready()

        @pl.when(i % 4 == 0)
        def _():
            cols = pl.ds(aligned(256 * (i // 4), 256), 256)
            tokens = x[...]
            part = dot_nn(tokens, wa[:, :, :, 0, :, cols].reshape(D, 256))
            q[:, cols] = ((part + vec[0:1, cols]) * 0.125).astype(bf16)
            k[:, cols] = dot_nn(tokens, wa[:, :, :, 1, :, cols].reshape(D, 256)).astype(bf16)
            part = dot_nn(tokens, wa[:, :, :, 2, :, cols].reshape(D, 256))
            v[:, cols] = (part + vec[1:2, cols]).astype(bf16)

        when(i, G_READY, gather_events)
        attend_forward(i, query_const, key_const, q, k, v, mixed, logsum, LONG)
        return carry

    lax.fori_loop(0, 12, heads, 0)
    gather_events(G_MERGE)
    for one in gathers(3):
        one.ready()
    tile = 512

    def merge_norm(i, carry):
        rows = pl.ds(aligned(i * tile, tile), tile)
        branch = dot_nn(mixed[rows, :], wm[...].reshape(D, D)) + vec[ROW_MERGE : ROW_MERGE + 1, :]
        x_hat, deviation = norm_parts(x[rows, :].astype(f32) + branch)
        xhat[rows, :] = x_hat.astype(bf16)
        logsum[rows, :] = jnp.where(lane_index(tile) == RSTD_LANE, deviation, logsum[rows, :])
        normed = x_hat * vec[ROW_GAIN : ROW_GAIN + 1, :] + vec[ROW_SHIFT : ROW_SHIFT + 1, :]
        low[rows, :] = normed.astype(bf16)
        first[rows, :] = normed + vec[ROW_SHRINK : ROW_SHRINK + 1, :]
        return carry

    lax.fori_loop(0, T // tile, merge_norm, 0)
    lowt[...] = low[...].T

    def out_copies(j):
        return (
            pltpu.make_async_copy(active.at[j % 2], active_any.at[j], flow.at[0, j % 2]),
            pltpu.make_async_copy(slope.at[j % 2], slope_any.at[j], flow.at[1, j % 2]),
        )

    def back_copies(j):
        return (
            pltpu.make_async_copy(active_any.at[j], active.at[j % 2], flow.at[0, j % 2]),
            pltpu.make_async_copy(slope_any.at[j], slope.at[j % 2], flow.at[1, j % 2]),
        )

    def expand_part(j, carry):
        when(j, G_FFN, gather_events)

        @pl.when(j >= 2)
        def _():
            for copy in out_copies(j - 2):
                copy.wait()

        for t in range(JOBS):

            @pl.when(j == t)
            def _():
                for one in gathers(4 + t):
                    one.ready()

        a_ref, s_ref = active.at[j % 2], slope.at[j % 2]
        for h in range(2):
            here = slice(256 * h, 256 * h + 256)
            cols = pl.ds(aligned(PART * j + 256 * h, 256), 256)
            bias = vec[pl.ds(ROW_EXPAND + j, 1), here]
            expanded = dot_nn(low[...], we[:, :, :, :, cols].reshape(D, 256)) + bias
            a, s = gelu_parts(expanded)
            a_ref[:, here] = a.astype(bf16)
            s_ref[:, here] = s.astype(bf16)
        when(j, G_FFN_MIDDLE, gather_events)
        rows = pl.ds(aligned(SLICE * j, SLICE), SLICE)
        first[...] += dot_nn(a_ref[...], ws[:, :, :, rows, :].reshape(PART, D))

        @pl.when(j < JOBS - 2)
        def _():
            for copy in out_copies(j):
                copy.start()

        return carry

    lax.fori_loop(0, JOBS, expand_part, 0)
    g_copy.wait()
    gain[0] = jnp.zeros((VEC_ROWS, D), f32)

    def end_of_forward(i, carry):
        rows = pl.ds(aligned(i * tile, tile), tile)
        x_hat, deviation = norm_parts(first[rows, :])
        weight = vec[ROW_GAIN + 1 : ROW_GAIN + 2, :]
        result = x_hat * weight + vec[ROW_SHIFT + 1 : ROW_SHIFT + 2, :]
        keep = column_of(logsum[rows, :], KEEP_LANE) > 0.0
        dy = jnp.where(keep, g[rows, :].astype(f32), 0.0)
        g[rows, :] = jnp.where(keep, result, x[rows, :].astype(f32)).astype(bf16)
        grad = norm_back(dy * weight, x_hat, deviation)
        first[rows, :] = grad
        branch = grad.astype(bf16)
        low[rows, :] = branch
        gain[0, ROW_GAIN + 1 : ROW_GAIN + 2, :] += jnp.sum(dy * x_hat, axis=0, keepdims=True)
        gain[0, ROW_SHIFT + 1 : ROW_SHIFT + 2, :] += jnp.sum(dy, axis=0, keepdims=True)
        gain[0, ROW_SHRINK : ROW_SHRINK + 1, :] += jnp.sum(branch.astype(f32), axis=0, keepdims=True)
        return carry

    lax.fori_loop(0, T // tile, end_of_forward, 0)
    out_copy = pltpu.make_async_copy(g, out_any, local.at[2])
    out_copy.start()

    def reductions(t):
        def one(ref, lands, final, cuts, at, *args):
            sems = (r_send.at[at], r_recv.at[at], rt_send.at[at], rt_recv.at[at])
            return Reduce(place, ref, lands, final, cuts(c, *args), cuts(1 - c, *args), sems)

        if t < JOBS:
            j = JOBS - 1 - t
            return [
                one(we, [e0.at[t % 2], e1.at[t], e2.at[t], e3.at[t], None], fe, expand_cuts, 2 * t, j),
                one(ws, [s0.at[t % 2], s1.at[t], None, s3.at[t], s4.at[t]], fs, shrink_cuts, 2 * t + 1, j),
            ]
        if t == JOBS:
            return [one(wm, [m0, m1, None, m3, m4], fm, merge_cuts, 2 * JOBS)]
        n = t - JOBS - 1
        return [one(ga, [a0.at[n % 2], a1.at[n], None, a3.at[n], a4.at[n]], fa, attend_cuts, 2 * JOBS + 1 + n, n)]

    def reduce_events(names):
        for step, t in names:
            for one in reductions(t):
                one.run(step)

    def expand_back(b, carry):
        j = JOBS - 1 - b

        @pl.when(b >= 2)
        def _():
            for copy in back_copies(j):
                copy.wait()

        when(b, R_FFN, reduce_events)
        a_ref, s_ref = active.at[j % 2], slope.at[j % 2]
        rows = pl.ds(aligned(SLICE * j, SLICE), SLICE)
        cols = pl.ds(aligned(PART * j, PART), PART)
        s_in = low[...]
        for h in range(2):
            here = slice(256 * h, 256 * h + 256)
            e_in = dot_nt(s_in, ws[2 * h : 2 * h + 2, :, :, rows, :].reshape(256, D)) * s_ref[:, here].astype(f32)
            e_in = e_in.astype(bf16)
            s_ref[:, here] = e_in
            gain[0, pl.ds(ROW_EXPAND + j, 1), here] = jnp.sum(e_in.astype(f32), axis=0, keepdims=True)
        when(b, R_FFN_MIDDLE, reduce_events)
        for h in range(2):
            grad = dot_tn(a_ref[:, 256 * h : 256 * h + 256], s_in).astype(bf16)
            ws[2 * h : 2 * h + 2, :, :, rows, :] = grad.reshape(2, Y, X, SLICE, D)
        first[...] += dot_nt(s_ref[...], we[:, :, :, :, cols].reshape(D, PART))
        for h in range(2):
            here = pl.ds(aligned(PART * j + 256 * h, 256), 256)
            grad = dot_nn(lowt[...], s_ref[:, 256 * h : 256 * h + 256]).astype(bf16)
            we[:, :, :, :, here] = grad.reshape(Z, Y, X, BLOCK, 256)
        when(b, {t: [(0, t)] for t in range(JOBS)}, reduce_events)

        @pl.when(b < JOBS - 2)
        def _():
            for copy in back_copies(j - 2):
                copy.start()

        return carry

    for t in range(4 + JOBS):
        for one in gathers(t):
            one.finish()
    lax.fori_loop(0, JOBS, expand_back, 0)

    def middle(i, carry):
        when(i, R_NORM, reduce_events)
        rows = pl.ds(aligned(i * tile, tile), tile)
        dy, x_hat = first[rows, :], xhat[rows, :].astype(f32)
        deviation = column_of(logsum[rows, :], RSTD_LANE)
        grad = norm_back(dy * vec[ROW_GAIN : ROW_GAIN + 1, :], x_hat, deviation)
        first[rows, :] = grad
        branch = grad.astype(bf16)
        low[rows, :] = branch
        gain[0, ROW_GAIN : ROW_GAIN + 1, :] += jnp.sum(dy * x_hat, axis=0, keepdims=True)
        gain[0, ROW_SHIFT : ROW_SHIFT + 1, :] += jnp.sum(dy, axis=0, keepdims=True)
        gain[0, ROW_MERGE : ROW_MERGE + 1, :] += jnp.sum(branch.astype(f32), axis=0, keepdims=True)
        x[rows, :] = dot_nt(branch, wm[...].reshape(D, D)).astype(bf16)
        return carry

    lax.fori_loop(0, T // tile, middle, 0)
    out_copy.wait()
    g_again = pltpu.make_async_copy(g_any, g, local.at[1])
    g_again.start()
    reduce_events(R_MERGE)
    wm[...] = dot_tn(mixed[...], low[...]).astype(bf16).reshape(Z, Y, X, BLOCK, D)
    reduce_events([(0, JOBS)])

    def heads_back(i, carry):
        when(i, R_HEADS, reduce_events)
        attend_backward(i, query_const, key_const, q, k, v, mixed, logsum, x, q, k, v, LONG)

        when(i, R_HEADS_END, reduce_events)

        @pl.when(i % 4 == 3)
        def _():
            cols = pl.ds(aligned(256 * (i // 4), 256), 256)
            for n, grads in enumerate((q, k, v)):
                grad = dot_nn(xt[...], grads[:, cols]).astype(bf16)
                ga[:, :, :, n, :, cols] = grad.reshape(Z, Y, X, BLOCK, 256)
                if n != 1:
                    gain[0, n // 2 : n // 2 + 1, cols] = jnp.sum(grads[:, cols].astype(f32), axis=0, keepdims=True)

        when(i, {4 * n + 3: [(0, JOBS + 1 + n)] for n in range(3)}, reduce_events)
        return carry

    lax.fori_loop(0, 12, heads_back, 0)
    sum_steps[0][0].start()

    def last_copy(ref, n, cols, height):
        rows = pl.ds(aligned(height * (1 - c), 8), height)
        here = ref.at[:, rows, cols] if len(ref.shape) == 3 else ref.at[rows, cols]
        return remote(here, here, last_send.at[n], last_recv.at[n], place.twin)

    early_last = [last_copy(fm, 0, my_cols, HALF), last_copy(fs, 1, my_cols, FF_HALF)]
    early_last += [last_copy(fe, 2 + j, expand_cuts(c, j)[0].cols, HALF) for j in range(JOBS)]
    attend_last = [last_copy(fa, 2 + JOBS + n, attend_cuts(c, n)[0].cols, HALF) for n in range(3)]

    reduce_events(R_TAIL[0])
    g_again.wait()

    def inputs_part(i, carry):
        @pl.when(i == 1)
        def _():
            reduce_events(R_TAIL[1])
            add_next(sum_steps, gain, gain_land, 0)

        rows = pl.ds(aligned(i * tile, tile), tile)
        keep = column_of(logsum[rows, :], KEEP_LANE) > 0.0
        total = first[rows, :] + jnp.where(keep, 0.0, g[rows, :].astype(f32))
        for n, grads in enumerate((q, k, v)):
            total += dot_nt(grads[rows, :], wa[:, :, :, n, :, :].reshape(D, D))
        first[rows, :] = total
        return carry

    lax.fori_loop(0, T // tile, inputs_part, 0)
    out_ig = pltpu.make_async_copy(first, ig_any, local.at[3])
    out_ig.start()
    add_next(sum_steps, gain, gain_land, 1)
    reduce_events(R_TAIL[2])
    for copy in early_last + attend_last[:2]:
        copy.start()
    add_next(sum_steps, gain, gain_land, 2)
    mine, ff_mine = pl.ds(aligned(HALF * c, 8), HALF), pl.ds(aligned(FF_HALF * c, 8), FF_HALF)
    for copy in early_last:
        copy.wait_recv()
    gm_out[...] = fm[mine, :]
    gs_out[...] = fs[ff_mine, :]

    def put_grad(tile, value):
        ge_out[:, LANES * tile : LANES * (tile + 1)] = value

    lane_groups(lambda tile: fe[mine, LANES * tile : LANES * (tile + 1)], put_grad, ff_moves(True))
    own_pack.wait_send()
    own_shrink.wait_send()
    for copy in early_last + sum(vec_steps + sum_steps[:3], []):
        copy.wait_send()
    for t in range(JOBS + 3):
        for one in reductions(t):
            one.finish()
    reduce_events(R_TAIL[3])
    attend_last[2].start()
    vec_out[...] = own_vectors(place, add_last(sum_steps, gain, gain_land))
    for copy in sum_steps[3]:
        copy.wait_send()
    for one in reductions(JOBS + 3):
        one.finish()
    for copy in attend_last:
        copy.wait_recv()
        copy.wait_send()
    for n in range(3):
        ga_out[:, D * n : D * n + D] = fa[n, mine, :]
    out_ig.wait()


ANY = pl.BlockSpec(memory_space=pl.ANY)
VM = pl.BlockSpec(memory_space=pltpu.VMEM)
SM = pl.BlockSpec(memory_space=pltpu.SMEM)


def layer_call(buckets, lengths, keeps, inputs, upstream, attend, merge, expand, shrink, pieces):
    dma = pltpu.SemaphoreType.DMA

    def landing(rows, cols, jobs=None, deep=(), slots=None, middle=False):
        lead = (jobs,) if jobs else ()
        dims = [((slots,) if slots else lead) + (Z, Y, X), lead + (Z, 2)]
        dims += [lead + (3, 2), lead + (1,)] if middle else [lead + (3,), lead + (Z,)]
        return [pltpu.VMEM(d + deep + (rows, cols), bf16) for d in dims]

    tokens = [pltpu.VMEM((T, D), bf16) for _ in range(5)]
    scratch = (
        [pltpu.VMEM(*s) for s in WEIGHTS]
        + [
            pltpu.VMEM(*WEIGHTS[0]),
            pltpu.VMEM((32, PACK), bf16),
            pltpu.VMEM((32, PACK), bf16),
            pltpu.VMEM((4, VEC_ROWS, D), bf16),
            pltpu.VMEM((6, VEC_ROWS, D), bf16),
            pltpu.VMEM((VEC_ROWS, D), f32),
        ]
        + tokens
        + [
            pltpu.VMEM((T, LANES), bf16),
            pltpu.VMEM((T, LANES), bf16),
            pltpu.VMEM((T, D), bf16),
            pltpu.VMEM((T, LANES), f32),
            pltpu.VMEM((T, D), bf16),
            pltpu.VMEM((T, D), bf16),
            pltpu.VMEM((D, T), bf16),
            pltpu.VMEM((D, T), bf16),
            pltpu.VMEM((2, T, PART), bf16),
            pltpu.VMEM((2, T, PART), bf16),
            pltpu.VMEM((T, D), f32),
        ]
        + landing(BLOCK, 128, 3, (3,), slots=2)
        + landing(BLOCK, 384)
        + landing(BLOCK, 256, JOBS, slots=2, middle=True)
        + landing(SLICE, 384, JOBS, slots=2)
        + [
            pltpu.VMEM((3, BLOCK, D), f32),
            pltpu.VMEM((BLOCK, D), f32),
            pltpu.VMEM((BLOCK, FF), f32),
            pltpu.VMEM((FF_BLOCK, D), f32),
            pltpu.VMEM((4, VEC_ROWS, D), f32),
            pltpu.VMEM((6, VEC_ROWS, D), f32),
        ]
        + 2 * [dma((GATHERS, 2, 5)), dma((GATHERS, 2, 5)), dma((GATHERS,)), dma((GATHERS,))]
        + 2 * [dma((2,))]
        + 4 * [dma((6,))]
        + 2 * [dma((5 + JOBS,))]
        + [dma((4,)), dma((2, 2))]
    )
    return pl.pallas_call(
        layer_kernel,
        out_shape=tuple(
            jax.ShapeDtypeStruct(*s)
            for s in (
                ((T, D), bf16), ((T, D), f32), ((HALF, 3 * D), f32), ((HALF, D), f32), ((HALF, FF), f32),
                ((FF_HALF, D), f32), ((PIECES, LANES), f32), ((JOBS, T, PART), bf16), ((JOBS, T, PART), bf16),
            )
        ),
        in_specs=[SM, SM, SM, ANY, ANY, VM, VM, VM, VM, VM],
        out_specs=[ANY, ANY] + [VM] * 5 + [ANY, ANY],
        scratch_shapes=scratch,
        compiler_params=pltpu.CompilerParams(collective_id=0, has_side_effects=True, vmem_limit_bytes=VMEM_LIMIT),
        cost_estimate=pl.CostEstimate(flops=60_000_000_000, bytes_accessed=60_000_000, transcendentals=20_000_000),
    )(buckets, lengths, keeps, inputs, upstream, attend, merge, expand, shrink, pieces)


def pack_pieces(attend_bias, merge_bias, expand_bias, shrink_bias, gain, shift):
    total = 0.0
    vectors = (attend_bias[None], merge_bias[None], expand_bias[None], shrink_bias[None], gain, shift)
    row = 0
    for piece in vectors:
        count, width = piece.shape
        total += jnp.pad(piece.astype(f32), ((row, PIECES - row - count), (0, LANES - width)))
        row += count
    return total


def finish_kernel(*refs):
    count = len(RESULTS)
    sources, own, wide, vectors = refs[:count], refs[count], refs[count + 1 : 2 * count + 1], refs[2 * count + 1 : -count - 2]
    held, arrive, leave = refs[-count - 2 : -2], refs[-2], refs[-1]
    steps = [
        (pltpu.make_async_copy(s, h, arrive.at[n]), pltpu.make_async_copy(h, w, leave.at[n]))
        for n, (s, h, w) in enumerate(zip(sources, held, wide))
    ]
    for into, _ in steps:
        into.start()
    row = 0
    for ref in vectors:
        if len(ref.shape) == 1:
            ref[...] = own[row, : ref.shape[0]]
            row += 1
        else:
            ref[...] = own[row : row + ref.shape[0], : ref.shape[1]]
            row += ref.shape[0]
    for into, out in steps:
        into.wait()
        out.start()
    for _, out in steps:
        out.wait()


RESULTS = (
    ((T, D), f32), ((T, D), bf16), ((HALF, 3 * D), f32), ((HALF, D), f32), ((HALF, FF), f32), ((FF_HALF, D), f32),
)


def finish_call(wide, own, vectors):
    dma = pltpu.SemaphoreType.DMA
    return pl.pallas_call(
        finish_kernel,
        out_shape=tuple(jax.ShapeDtypeStruct(*s) for s in RESULTS)
        + tuple(jax.ShapeDtypeStruct(v.shape, f32) for v in vectors),
        in_specs=[ANY] * len(RESULTS) + [VM],
        out_specs=[ANY] * len(RESULTS) + [VM] * len(vectors),
        scratch_shapes=[pltpu.VMEM(*s) for s in RESULTS] + 2 * [dma((len(RESULTS),))],
        compiler_params=pltpu.CompilerParams(vmem_limit_bytes=VMEM_LIMIT),
    )(*wide, own)

def layer_norm(hidden, gains, shifts):
    center = hidden - jnp.mean(hidden, axis=-1, keepdims=True)
    spread = jnp.mean(center * center, axis=-1, keepdims=True)
    return center * lax.rsqrt(spread + epsilon) * gains + shifts


def gelu_exact(values):
    return jax.nn.gelu(values, approximate=False)


def matmul(left, right):
    return jnp.dot(left, right, preferred_element_type=jnp.float32)


def token_info(bucket, slot_lengths, slot_keeps):
    position = jnp.arange(TOK_DEV, dtype=jnp.int32)
    span_size = jnp.where(bucket > 0, LONG, SHORT).astype(jnp.int32)
    sequence = position // span_size
    within = position - sequence * span_size
    slot_index = sequence * (span_size // SHORT)
    matches = (slot_index[:, None] == jnp.arange(SLOTS, dtype=jnp.int32)[None, :]).astype(jnp.int32)
    length = jnp.sum(matches * slot_lengths[None, :], axis=1) + bucket * (LONG - SHORT)
    keep_flags = jnp.sum(matches * slot_keeps[None, :], axis=1)
    return (sequence, within < length, keep_flags > 0)


def masked_scores(queries, key_rows, sequence, valid_key):
    scores = jnp.einsum("qhd,khd->hqk", queries, key_rows, preferred_element_type=jnp.float32)
    allowed = (sequence[:, None] == sequence[None, :]) & valid_key[None, :]
    return jnp.where(allowed[None], scores, masked_score)


def attend_block(pieces):
    queries, key_rows, values, sequence, valid_key = pieces
    scores = masked_scores(queries, key_rows, sequence, valid_key)
    highest = jnp.max(scores, axis=-1, keepdims=True)
    raised = jnp.exp(scores - highest)
    row_total = jnp.sum(raised, axis=-1, keepdims=True)
    weights = raised / row_total
    mixed_rows = jnp.einsum(
        "hqk,khd->qhd", weights.astype(jnp.bfloat16), values, preferred_element_type=jnp.float32
    )
    return (mixed_rows, highest[:, :, 0] + jnp.log(row_total[:, :, 0]))


def attend_back(pieces):
    queries, key_rows, values, sequence, valid_key, logsum, mixed_grad = pieces
    scores = masked_scores(queries, key_rows, sequence, valid_key)
    weights = jnp.exp(scores - logsum[:, :, None])
    weight_grad = jnp.einsum("qhd,khd->hqk", mixed_grad, values, preferred_element_type=jnp.float32)
    row_dot = jnp.sum(weights * weight_grad, axis=-1, keepdims=True)
    score_grad = (weights * (weight_grad - row_dot)).astype(jnp.bfloat16)
    query_part = jnp.einsum(
        "hqk,khd->qhd", score_grad, key_rows, preferred_element_type=jnp.float32
    ).astype(jnp.bfloat16)
    key_part = jnp.einsum(
        "hqk,qhd->khd", score_grad, queries, preferred_element_type=jnp.float32
    ).astype(jnp.bfloat16)
    value_part = jnp.einsum(
        "hqk,qhd->khd", weights.astype(jnp.bfloat16), mixed_grad, preferred_element_type=jnp.float32
    ).astype(jnp.bfloat16)
    return (query_part, key_part, value_part)


def heads_view(source):
    return source.reshape(source.shape[0] // LONG, LONG, HEADS, HD)


def forward_pass(inputs, weights, sequence, valid_key, keep_flags):
    (
        attend_matrix,
        attend_offset,
        merge_matrix,
        merge_offset,
        expand_matrix,
        expand_offset,
        shrink_matrix,
        shrink_offset,
        gains,
        shifts,
    ) = weights
    model_width = inputs.shape[1]
    blocks = inputs.shape[0] // LONG
    packed = matmul(inputs, attend_matrix)
    offset = attend_offset.astype(jnp.float32)
    queries = ((packed[:, :model_width] + offset[:model_width]) * 0.125).astype(jnp.bfloat16)
    key_rows = packed[:, model_width : 2 * model_width].astype(jnp.bfloat16)
    values = (packed[:, 2 * model_width :] + offset[model_width:]).astype(jnp.bfloat16)
    mixed_rows, logsum = lax.map(
        attend_block,
        (
            heads_view(queries),
            heads_view(key_rows),
            heads_view(values),
            sequence.reshape(blocks, LONG),
            valid_key.reshape(blocks, LONG),
        ),
    )
    mixed_rows = mixed_rows.reshape(-1, model_width).astype(jnp.bfloat16)
    tokens = inputs.astype(jnp.float32)
    first_sum = tokens + matmul(mixed_rows, merge_matrix) + merge_offset.astype(jnp.float32)
    normed = layer_norm(first_sum, gains[0].astype(jnp.float32), shifts[0].astype(jnp.float32))
    normed_low = normed.astype(jnp.bfloat16)
    expanded = matmul(normed_low, expand_matrix) + expand_offset.astype(jnp.float32)
    active = gelu_exact(expanded).astype(jnp.bfloat16)
    second_sum = normed + matmul(active, shrink_matrix) + shrink_offset.astype(jnp.float32)
    result = layer_norm(second_sum, gains[1].astype(jnp.float32), shifts[1].astype(jnp.float32))
    outputs = jnp.where(keep_flags[:, None], result, tokens).astype(jnp.bfloat16)
    return (
        outputs,
        (
            queries,
            key_rows,
            values,
            logsum,
            mixed_rows,
            first_sum,
            normed_low,
            expanded,
            active,
            second_sum,
        ),
    )


def backward_pass(inputs, upstream, weights, saved, sequence, valid_key, keep_flags):
    (
        attend_matrix,
        attend_offset,
        merge_matrix,
        merge_offset,
        expand_matrix,
        expand_offset,
        shrink_matrix,
        shrink_offset,
        gains,
        shifts,
    ) = weights
    (
        queries,
        key_rows,
        values,
        logsum,
        mixed_rows,
        first_sum,
        normed_low,
        expanded,
        active,
        second_sum,
    ) = saved
    model_width = inputs.shape[1]
    blocks = inputs.shape[0] // LONG
    cotangent = upstream.astype(jnp.float32)
    result_grad = jnp.where(keep_flags[:, None], cotangent, 0.0)
    second_out, pull_second = jax.vjp(
        layer_norm, second_sum, gains[1].astype(jnp.float32), shifts[1].astype(jnp.float32)
    )
    second_grad, gain_two, shift_two = pull_second(result_grad)
    shrink_in = second_grad.astype(jnp.bfloat16)
    shrink_grad = jnp.einsum("tf,td->fd", active, shrink_in, preferred_element_type=jnp.float32)
    shrink_offset_grad = jnp.sum(shrink_in.astype(jnp.float32), axis=0)
    active_grad = jnp.einsum(
        "td,fd->tf", shrink_in, shrink_matrix, preferred_element_type=jnp.float32
    )
    gelu_out, pull_gelu = jax.vjp(gelu_exact, expanded)
    expand_in = pull_gelu(active_grad)[0].astype(jnp.bfloat16)
    expand_grad = jnp.einsum("td,tf->df", normed_low, expand_in, preferred_element_type=jnp.float32)
    expand_offset_grad = jnp.sum(expand_in.astype(jnp.float32), axis=0)
    normed_grad = second_grad + jnp.einsum(
        "tf,df->td", expand_in, expand_matrix, preferred_element_type=jnp.float32
    )
    first_out, pull_first = jax.vjp(
        layer_norm, first_sum, gains[0].astype(jnp.float32), shifts[0].astype(jnp.float32)
    )
    first_grad, gain_one, shift_one = pull_first(normed_grad)
    branch_in = first_grad.astype(jnp.bfloat16)
    merge_grad = jnp.einsum("td,te->de", mixed_rows, branch_in, preferred_element_type=jnp.float32)
    merge_offset_grad = jnp.sum(branch_in.astype(jnp.float32), axis=0)
    mixed_grad = jnp.einsum(
        "te,de->td", branch_in, merge_matrix, preferred_element_type=jnp.float32
    ).astype(jnp.bfloat16)
    query_part, key_part, value_part = lax.map(
        attend_back,
        (
            heads_view(queries),
            heads_view(key_rows),
            heads_view(values),
            sequence.reshape(blocks, LONG),
            valid_key.reshape(blocks, LONG),
            logsum,
            heads_view(mixed_grad),
        ),
    )
    query_grad = query_part.reshape(-1, model_width) * 0.125
    packed_grad = jnp.concatenate(
        [query_grad, key_part.reshape(-1, model_width), value_part.reshape(-1, model_width)], axis=1
    )
    attend_grad = jnp.einsum("td,te->de", inputs, packed_grad, preferred_element_type=jnp.float32)
    attend_offset_grad = jnp.concatenate(
        [
            jnp.sum(query_grad.astype(jnp.float32), axis=0),
            jnp.sum(value_part.reshape(-1, model_width).astype(jnp.float32), axis=0),
        ]
    )
    input_grad = (
        first_grad
        + jnp.einsum("te,de->td", packed_grad, attend_matrix, preferred_element_type=jnp.float32)
        + jnp.where(keep_flags[:, None], 0.0, cotangent)
    )
    gain_grad = jnp.stack([gain_one, gain_two])
    shift_grad = jnp.stack([shift_one, shift_two])
    grads = (
        attend_grad,
        attend_offset_grad,
        merge_grad,
        merge_offset_grad,
        expand_grad,
        expand_offset_grad,
        shrink_grad,
        shrink_offset_grad,
        gain_grad,
        shift_grad,
    )
    return (grads, input_grad)


def general_device(
    inputs,
    upstream,
    buckets,
    lengths,
    layer_keep,
    attend_weight,
    attend_bias,
    merge_weight,
    merge_bias,
    expand_weight,
    expand_bias,
    shrink_weight,
    shrink_bias,
    norm_gain,
    norm_shift,
):
    sequence, valid_key, keep_flags = token_info(buckets[0], lengths[0], layer_keep[0])
    gathered = (
        lax.all_gather(attend_weight, ("group", "inner"), axis=0, tiled=True),
        lax.all_gather(attend_bias, ("group", "inner"), axis=0, tiled=True),
        lax.all_gather(merge_weight, ("group", "inner"), axis=0, tiled=True),
        lax.all_gather(merge_bias, ("group", "inner"), axis=0, tiled=True),
        lax.all_gather(expand_weight, ("group", "inner"), axis=0, tiled=True),
        lax.all_gather(expand_bias, ("group", "inner"), axis=0, tiled=True),
        lax.all_gather(shrink_weight, ("group", "inner"), axis=0, tiled=True),
        lax.all_gather(shrink_bias, ("group", "inner"), axis=0, tiled=True),
        lax.all_gather(norm_gain, ("group", "inner"), axis=1, tiled=True),
        lax.all_gather(norm_shift, ("group", "inner"), axis=1, tiled=True),
    )
    outputs, saved = forward_pass(inputs, gathered, sequence, valid_key, keep_flags)
    gathered = (
        lax.all_gather(attend_weight, ("group", "inner"), axis=0, tiled=True),
        lax.all_gather(attend_bias, ("group", "inner"), axis=0, tiled=True),
        lax.all_gather(merge_weight, ("group", "inner"), axis=0, tiled=True),
        lax.all_gather(merge_bias, ("group", "inner"), axis=0, tiled=True),
        lax.all_gather(expand_weight, ("group", "inner"), axis=0, tiled=True),
        lax.all_gather(expand_bias, ("group", "inner"), axis=0, tiled=True),
        lax.all_gather(shrink_weight, ("group", "inner"), axis=0, tiled=True),
        lax.all_gather(shrink_bias, ("group", "inner"), axis=0, tiled=True),
        lax.all_gather(norm_gain, ("group", "inner"), axis=1, tiled=True),
        lax.all_gather(norm_shift, ("group", "inner"), axis=1, tiled=True),
    )
    grads, input_grad = backward_pass(
        inputs, upstream, gathered, saved, sequence, valid_key, keep_flags
    )
    shares = (
        lax.psum_scatter(grads[0], ("group", "inner"), scatter_dimension=0, tiled=True),
        lax.psum_scatter(grads[1], ("group", "inner"), scatter_dimension=0, tiled=True),
        lax.psum_scatter(grads[2], ("group", "inner"), scatter_dimension=0, tiled=True),
        lax.psum_scatter(grads[3], ("group", "inner"), scatter_dimension=0, tiled=True),
        lax.psum_scatter(grads[4], ("group", "inner"), scatter_dimension=0, tiled=True),
        lax.psum_scatter(grads[5], ("group", "inner"), scatter_dimension=0, tiled=True),
        lax.psum_scatter(grads[6], ("group", "inner"), scatter_dimension=0, tiled=True),
        lax.psum_scatter(grads[7], ("group", "inner"), scatter_dimension=0, tiled=True),
        lax.psum_scatter(grads[8], ("group", "inner"), scatter_dimension=1, tiled=True),
        lax.psum_scatter(grads[9], ("group", "inner"), scatter_dimension=1, tiled=True),
    )
    return (
        outputs,
        input_grad,
        shares[0],
        shares[1],
        shares[2],
        shares[3],
        shares[4],
        shares[5],
        shares[6],
        shares[7],
        shares[8],
        shares[9],
    )

def slice_device(
    inputs, upstream, buckets, lengths, layer_keep, attend_weight, attend_bias, merge_weight, merge_bias,
    expand_weight, expand_bias, shrink_weight, shrink_bias, norm_gain, norm_shift,
):
    pieces = pack_pieces(attend_bias, merge_bias, expand_bias, shrink_bias, norm_gain, norm_shift)
    outputs, input_grad, attend, merge, expand, shrink, own = layer_call(
        buckets, lengths, layer_keep, inputs, upstream, attend_weight, merge_weight, expand_weight, shrink_weight, pieces
    )[:7]
    input_grad, outputs, attend, merge, expand, shrink, attend_b, merge_b, expand_b, shrink_b, gain, shift = finish_call(
        (input_grad, outputs, attend, merge, expand, shrink),
        own,
        (attend_bias, merge_bias, expand_bias, shrink_bias, norm_gain, norm_shift),
    )
    return (
        outputs, input_grad, attend, attend_b, merge, merge_b, expand, expand_b, shrink, shrink_b, gain, shift,
    )

def solution(mesh):
    on_slice = mesh.shape["group"] == Z * Y and mesh.shape["inner"] == 2 * X
    placed = (
        P(("group", "inner"), None),
        P(("group", "inner"), None),
        P(("group", "inner")),
        P(("group", "inner"), None),
        P(("group", "inner"), None),
        P(("group", "inner"), None),
        P(("group", "inner")),
        P(("group", "inner"), None),
        P(("group", "inner")),
        P(("group", "inner"), None),
        P(("group", "inner")),
        P(("group", "inner"), None),
        P(("group", "inner")),
        P(None, ("group", "inner")),
        P(None, ("group", "inner")),
    )
    return jax.shard_map(
        slice_device if on_slice else general_device,
        mesh=mesh,
        in_specs=placed,
        out_specs=(
            P(("group", "inner"), None),
            P(("group", "inner"), None),
            P(("group", "inner"), None),
            P(("group", "inner")),
            P(("group", "inner"), None),
            P(("group", "inner")),
            P(("group", "inner"), None),
            P(("group", "inner")),
            P(("group", "inner"), None),
            P(("group", "inner")),
            P(None, ("group", "inner")),
            P(None, ("group", "inner")),
        ),
        check_vma=False,
    )
```

```python
import jax
import jax.numpy as jnp
from jax import lax
from jax.experimental import pallas as pl
from jax.experimental.pallas import tpu as pltpu
from jax.sharding import PartitionSpec as P

HEADS = 12
HD = 64
LONG = 512
SHORT = 128
TOK_DEV = 1024
SLOTS = 8
D = 768
FF = 3072
LANES = 128
RSTD_LANE, KEEP_LANE = 12, 13
epsilon = 1e-05
masked_score = -1e30
f32 = jnp.float32
bf16 = jnp.bfloat16


def dot_nn(a, b):
    return lax.dot_general(a, b, (((1,), (0,)), ((), ())), preferred_element_type=f32)


def dot_nt(a, b):
    return lax.dot_general(a, b, (((1,), (1,)), ((), ())), preferred_element_type=f32)


def dot_tn(a, b):
    return lax.dot_general(a, b, (((0,), (0,)), ((), ())), preferred_element_type=f32)


def lane_index(rows):
    return lax.broadcasted_iota(jnp.int32, (rows, LANES), 1)


def token_tables(bucket, lengths, keeps, query_const, key_const, columns):
    shape = (TOK_DEV, LANES)
    position = lax.broadcasted_iota(jnp.int32, shape, 0)
    is_long = jnp.broadcast_to(bucket, shape) > 0
    slot = jnp.where(is_long, (position >> 9) << 2, position >> 7)
    offset = jnp.where(is_long, position & (LONG - 1), position & (SHORT - 1))
    length = jnp.zeros(shape, jnp.int32)
    keep = jnp.zeros(shape, jnp.int32)
    for b in range(SLOTS):
        here = slot == b
        length = jnp.where(here, lengths[b], length)
        keep = jnp.where(here, keeps[b], keep)
    length = length + bucket * (LONG - SHORT)
    valid = offset < length
    within = jnp.where(is_long, 0, (position >> 7) & 3)
    lane = lax.broadcasted_iota(jnp.int32, shape, 1) & (HD - 1)
    is_span = (lane >= 4) & (lane < 8)
    same = lane - 4 == within
    zero, one = jnp.zeros(shape, f32), jnp.ones(shape, f32)
    query_const[...] = jnp.where(lane == 3, one, jnp.where(is_span & ~same, one, zero)).astype(bf16)
    key_const[...] = jnp.where(
        lane < 3,
        one,
        jnp.where(((lane == 3) & ~valid) | (is_span & same), masked_score * one, zero),
    ).astype(bf16)
    columns[...] = jnp.where((lane_index(TOK_DEV) == KEEP_LANE) & (keep > 0), one, zero)


def column_of(columns, lane):
    return jnp.sum(jnp.where(lane_index(columns.shape[0]) == lane, columns, 0.0), axis=1, keepdims=True)


def three_parts(column, rows):
    wide = jnp.broadcast_to(column, (rows, LANES))
    high = wide.astype(bf16)
    rest = wide - high.astype(f32)
    middle = rest.astype(bf16)
    low = (rest - middle.astype(f32)).astype(bf16)
    return high, middle, low


def attend_forward(index, query_const, key_const, q_ref, k_ref, v_ref, mixed_ref, logsum_ref, tile):
    pair, block = index // 2, index % 2
    cols = pl.ds(pl.multiple_of(pair * LANES, LANES), LANES)
    rows = pl.ds(pl.multiple_of(block * LONG, LONG), LONG)
    lane_k = lane_index(LONG)
    k2, v2 = k_ref[rows, cols], v_ref[rows, cols]
    kc = key_const[rows, :]
    k_aug = [jnp.where((lane_k // HD) == half, k2, kc) for half in range(2)]
    lane_q = lane_index(tile)
    for t in range(LONG // tile):
        qrows = pl.ds(pl.multiple_of(block * LONG + t * tile, tile), tile)
        q2, qc = q_ref[qrows, cols], query_const[qrows, :]
        outs = []
        sums = logsum_ref[qrows, :]
        for half in range(2):
            q_aug = jnp.where((lane_q // HD) == half, q2, qc)
            scores = dot_nt(q_aug, k_aug[half])
            highest = jnp.max(scores, axis=1, keepdims=True)
            raised = jnp.exp(scores - highest)
            total = jnp.sum(raised, axis=1, keepdims=True)
            out = dot_nn(raised.astype(bf16), v2)
            outs.append(out * (1.0 / total))
            sums = jnp.where(lane_q == 2 * pair + half, highest + jnp.log(total), sums)
        logsum_ref[qrows, :] = sums
        mixed_ref[qrows, cols] = jnp.where(lane_q < HD, outs[0], outs[1]).astype(bf16)


def attend_backward(index, query_const, key_const, q_ref, k_ref, v_ref, mixed_ref, logsum_ref, mixed_grad_ref,
                    dq_ref, dk_ref, dv_ref, tile):
    pair, block = index // 2, index % 2
    cols = pl.ds(pl.multiple_of(pair * LANES, LANES), LANES)
    rows = pl.ds(pl.multiple_of(block * LONG, LONG), LONG)
    lane = lane_index(LONG)
    q2, dm2 = q_ref[rows, cols], mixed_grad_ref[rows, cols]
    product = dm2.astype(f32) * mixed_ref[rows, cols].astype(f32)
    sums = logsum_ref[rows, :]
    qc = query_const[rows, :]
    zero = jnp.zeros((LONG, LANES), bf16)
    q_aug, d_aug = [], []
    for half in range(2):
        mine = (lane // HD) == half
        at = lane & (HD - 1)
        logsum = jnp.sum(jnp.where(lane == 2 * pair + half, sums, 0.0), axis=1, keepdims=True)
        delta = jnp.sum(jnp.where(mine, product, 0.0), axis=1, keepdims=True)
        lh, lm, ll = three_parts(-logsum, LONG)
        dh, dm, dl = three_parts(-delta, LONG)
        extra = jnp.where(at == 0, lh, jnp.where(at == 1, lm, jnp.where(at == 2, ll, qc)))
        q_aug.append(jnp.where(mine, q2, extra))
        extra = jnp.where(at == 0, dh, jnp.where(at == 1, dm, jnp.where(at == 2, dl, zero)))
        d_aug.append(jnp.where(mine, dm2, extra))
    dq = [jnp.zeros((LONG, LANES), f32) for _ in range(2)]
    lane_t = lane_index(tile)
    one = jnp.ones((tile, LANES), bf16)
    zero_t = jnp.zeros((tile, LANES), bf16)
    for t in range(LONG // tile):
        krows = pl.ds(pl.multiple_of(block * LONG + t * tile, tile), tile)
        k2, v2, kc = k_ref[krows, cols], v_ref[krows, cols], key_const[krows, :]
        vc = jnp.where((lane_t & (HD - 1)) < 3, one, zero_t)
        dk, dv = [], []
        for half in range(2):
            mine = (lane_t // HD) == half
            weights = jnp.exp(dot_nt(jnp.where(mine, k2, kc), q_aug[half]))
            grads = weights * dot_nt(jnp.where(mine, v2, vc), d_aug[half])
            low, low_grads = weights.astype(bf16), grads.astype(bf16)
            dv.append(dot_nn(low, dm2))
            dk.append(dot_nn(low_grads, q2))
            dq[half] = dq[half] + dot_tn(low_grads, k2)
        dk_ref[krows, cols] = jnp.where(lane_t < HD, dk[0], dk[1]).astype(bf16)
        dv_ref[krows, cols] = jnp.where(lane_t < HD, dv[0], dv[1]).astype(bf16)
    dq_ref[rows, cols] = (jnp.where(lane < HD, dq[0], dq[1]).astype(bf16).astype(f32) * 0.125).astype(bf16)


def gelu_parts(x):
    magnitude = jnp.abs(x)
    base = 1.0 + (0.3275911 * 0.7071067811865476) * magnitude
    t = pl.reciprocal(base, approx=True)
    t = t * (2.0 - base * t)
    bell = jnp.exp2(x * x * -0.7213475204444817)
    tail = t * (0.127414796 + t * (-0.142248368 + t * (0.7107068705 + t * (-0.7265760135 + t * 0.5307027145)))) * bell
    phi = jnp.where(x >= 0.0, 1.0 - tail, tail)
    return x * phi, phi + x * (bell * 0.3989422804014327)


def norm_parts(x):
    center = x - jnp.mean(x, axis=-1, keepdims=True)
    spread = jnp.mean(center * center, axis=-1, keepdims=True)
    rstd = lax.rsqrt(spread + epsilon)
    return center * rstd, rstd


def norm_back(dy_hat, x_hat, rstd):
    a = jnp.mean(dy_hat, axis=-1, keepdims=True)
    b = jnp.mean(dy_hat * x_hat, axis=-1, keepdims=True)
    return rstd * (dy_hat - a - x_hat * b)

MESH = pl.DeviceIdType.MESH
Z, X, Y = 4, 2, 2
CHIPS = Z * Y * X
JOBS = 6
PART = FF // JOBS
BLOCK = D // CHIPS
FF_BLOCK = FF // CHIPS
SLICE = FF_BLOCK // JOBS
ALL = slice(None)


def aligned(value, unit):
    return pl.multiple_of(value, unit)


class Place:
    def __init__(self):
        group, inner = lax.axis_index("group"), lax.axis_index("inner")
        self.z, self.y, self.x, self.c = group // Y, group % Y, inner // 2, inner % 2
        self.index = group * (X * 2) + inner
        self.chip = group * X + self.x
        self.twin = (group, self.x * 2 + 1 - self.c)
        self.over = {
            "x": ((1 - self.x, (group, (1 - self.x) * 2 + self.c)),),
            "y": ((1 - self.y, (self.z * Y + 1 - self.y, inner)),),
            "z": tuple(
                (z, (z * Y + self.y, inner))
                for z in (self.z + 1 - 2 * (self.z % 2), (self.z + 2) % Z, Z - 1 - self.z)
            ),
        }
        self.peers = (self.twin,) + tuple(peer for axis in "xyz" for _, peer in self.over[axis])

    def greet(self):
        barrier = pltpu.get_barrier_semaphore()
        for peer in self.peers:
            pl.semaphore_signal(barrier, 1, device_id=peer, device_id_type=MESH)

    def met(self):
        pl.semaphore_wait(pltpu.get_barrier_semaphore(), len(self.peers))

    def at(self, whole, **given):
        return tuple(given[a] if a in given else ALL if a in whole else getattr(self, a) for a in "zyx")


def remote(source, target, send, recv, peer):
    return pltpu.make_async_remote_copy(
        src_ref=source, dst_ref=target, send_sem=send, recv_sem=recv, device_id=peer, device_id_type=MESH
    )


class Cut:
    def __init__(self, rows, cols, order=None, near=(ALL, ALL)):
        self.rows, self.cols, self.order, self.near = rows, cols, order, near


def row_parts(start, low, high, cols):
    return (
        Cut(pl.ds(aligned(start, 16), low), cols, "zxy", (pl.ds(0, low), ALL)),
        Cut(pl.ds(aligned(start + low, 16), high), cols, "zyx", (pl.ds(low, high), ALL)),
    )


def attend_cuts(core, g):
    cols = pl.ds(aligned(256 * g + 128 * core, 128), 128)
    low, high = (16, 32) if g % 2 == 0 else (32, 16)
    return Cut(pl.ds(0, BLOCK), cols), row_parts(0, low, high, cols)


def merge_cuts(core):
    cols = pl.ds(aligned(384 * core, 128), 384)
    return Cut(pl.ds(0, BLOCK), cols), row_parts(0, 32, 16, cols)


def expand_cuts(core, j):
    at = PART * j + 256 * core
    rows = pl.ds(0, BLOCK)
    orders = ("xzy", "zyx") if j % 2 == 0 else ("zxy", "yzx")
    return Cut(rows, pl.ds(aligned(at, 128), 256)), tuple(
        Cut(rows, pl.ds(aligned(at + 128 * n, 128), 128), orders[n]) for n in range(2)
    )


def shrink_cuts(core, j):
    cols = pl.ds(aligned(384 * core, 128), 384)
    half = SLICE // 2
    return Cut(pl.ds(aligned(SLICE * j, SLICE), SLICE), cols), row_parts(SLICE * j, half, half, cols)


def blocks(ref, at, cut):
    deep = (ALL,) if len(ref.shape) == 6 else ()
    return ref.at[at + deep + (cut.rows, cut.cols)]


class Gather:
    def __init__(self, place, ref, cuts, send, recv, twin_send, twin_recv):
        self.place, self.ref, (self.whole, self.parts) = place, ref, cuts
        self.send, self.recv, self.twin_send, self.twin_recv = send, recv, twin_send, twin_recv

    def stage(self, n, part, step):
        axis = part.order[step]
        here = blocks(self.ref, self.place.at(part.order[:step]), part)
        first = sum(len(self.place.over[a]) for a in part.order[:step])
        return [
            remote(here, here, self.send.at[n, first + m], self.recv.at[n, first + m], peer)
            for m, (_, peer) in enumerate(self.place.over[axis])
        ]

    def to_twin(self):
        here = blocks(self.ref, self.place.at("zyx"), self.whole)
        return remote(here, here, self.twin_send, self.twin_recv, self.place.twin)

    def run(self, step):
        for n, part in enumerate(self.parts):
            if step > 0:
                for copy in self.stage(n, part, step - 1):
                    copy.wait_recv()
            if step < 3:
                for copy in self.stage(n, part, step):
                    copy.start()
        if step == 3:
            self.to_twin().start()

    def ready(self):
        self.to_twin().wait_recv()

    def finish(self):
        for n, part in enumerate(self.parts):
            for step in range(3):
                for copy in self.stage(n, part, step):
                    copy.wait_send()
        self.to_twin().wait_send()


class Reduce:
    def __init__(self, place, ref, land0, lands, final, cuts, twin_cuts, sems):
        self.place, self.ref, (self.whole, self.parts), self.twin_whole = place, ref, cuts, twin_cuts[0]
        self.land0, self.lands, self.final = land0, lands, final
        self.send, self.recv, self.twin_send, self.twin_recv = sems
        self.deep = (ALL,) if len(ref.shape) == 6 else ()

    def twin(self):
        source = blocks(self.ref, self.place.at("zyx"), self.twin_whole)
        return remote(source, self.land0, self.twin_send, self.twin_recv, self.place.twin)

    def land(self, part, step, m):
        axis = part.order[3 - step]
        ref = self.lands[part.order[1] == "z"][step - 1]
        lead = ((ALL, ALL), (m, ALL) if axis == "z" else (ALL,), (m,))[step - 1]
        return ref.at[lead + self.deep + part.near]

    def stage(self, n, part, step):
        axis, left = part.order[3 - step], part.order[: 3 - step]
        first = sum(len(self.place.over[a]) for a in part.order[4 - step :])
        return [
            remote(
                blocks(self.ref, self.place.at(left, **{axis: there}), part), self.land(part, step, m),
                self.send.at[n, first + m], self.recv.at[n, first + m], peer,
            )
            for m, (there, peer) in enumerate(self.place.over[axis])
        ]

    def run(self, step):
        if step == 0:
            self.twin().start()
            return
        if step == 1:
            self.twin().wait_recv()
            mine = blocks(self.ref, self.place.at("zyx"), self.whole)
            mine[...] = (mine[...].astype(f32) + self.land0[...].astype(f32)).astype(bf16)
        for n, part in enumerate(self.parts):
            if step > 1:
                left = part.order[: 4 - step]
                mine = blocks(self.ref, self.place.at(left), part)
                value = mine[...].astype(f32)
                for m, copy in enumerate(self.stage(n, part, step - 1)):
                    copy.wait_recv()
                    value += self.land(part, step - 1, m)[...].astype(f32)
                if step < 4:
                    mine[...] = value.astype(bf16)
                else:
                    self.final[self.deep + (part.rows, part.cols)] = value
            if step < 4:
                for copy in self.stage(n, part, step):
                    copy.start()

    def finish(self):
        self.twin().wait_send()
        for n, part in enumerate(self.parts):
            for step in (1, 2, 3):
                for copy in self.stage(n, part, step):
                    copy.wait_send()

T = TOK_DEV
VEC_ROWS = 16
VECTORS = 99
PIECES = 8
ROW_MERGE, ROW_EXPAND, ROW_SHRINK, ROW_GAIN, ROW_SHIFT = 2, 3, 9, 10, 12
HALF, FF_HALF = BLOCK // 2, FF_BLOCK // 2
PACK = 3 * D + D + FF
GATHERS = 4 + 2 * JOBS
WEIGHTS = (
    ((Z, Y, X, 3, BLOCK, D), bf16),
    ((Z, Y, X, BLOCK, D), bf16),
    ((Z, Y, X, BLOCK, FF), bf16),
    ((Z, Y, X, FF_BLOCK, D), bf16),
)
VMEM_LIMIT = 255 * 2**18

G_START = [(0, 0), (0, 1), (0, 2), (1, 99), (1, 0), (1, 1), (2, 0), (0, 5), (0, 3), (1, 2), (2, 99), (2, 1), (0, 4), (3, 0), (3, 99), (1, 5), (2, 2), (3, 1)]
G_HEADS = {
    1: [(2, 5)],
    3: [(2, 3)],
    4: [],
    6: [(1, 7)],
    7: [(3, 3), (2, 4)],
    8: [],
    10: [(2, 6)],
    11: [(1, 8)],
}
G_READY = {
    0: [(0, 6), (1, 3), (0, 7), (1, 4)],
    4: [(1, 6), (0, 8), (0, 9), (3, 2)],
}
G_MERGE = [(3, 5), (3, 4), (1, 9)]
G_FFN = {
    2: [(2, 9)],
}
G_FFN_MIDDLE = {
    0: [(2, 7)],
    1: [(3, 6), (2, 8)],
    2: [(3, 7)],
    3: [(3, 8)],
    4: [(3, 9)],
}
R_FFN = {
}
R_FFN_MIDDLE = {
    1: [(1, 0)],
    2: [(1, 1)],
    3: [(1, 2)],
    4: [(2, 0), (2, 1), (1, 3)],
    5: [(2, 2), (1, 4)],
}
R_NORM = {
    1: [(3, 0)],
}
R_MERGE = []
R_HEADS = {
    0: [(3, 1), (1, 5)],
    2: [(3, 2)],
    3: [(2, 3)],
    5: [(2, 5)],
    6: [(3, 3), (1, 7)],
    8: [(2, 6)],
    9: [(1, 8), (3, 5)],
    11: [(2, 7), (3, 6)],
}
R_HEADS_END = {
    3: [(2, 4), (1, 6)],
    7: [(3, 4)],
    11: [(2, 8)],
}
R_TAIL = [[(4, 3), (4, 2), (3, 7), (1, 99), (4, 5), (1, 9), (4, 6), (2, 99), (3, 8), (4, 0), (3, 99), (4, 7), (2, 9), (4, 1), (4, 4)], [], [(3, 9), (4, 8)], [(4, 9)]]

def chosen(width, offset, start=0):
    source = lax.broadcasted_iota(jnp.int32, (LANES, D), 0)
    target = lax.broadcasted_iota(jnp.int32, (LANES, D), 1)
    mine = (source >= start) & (source < start + width)
    return jnp.where((target == source + (offset - start)) & mine, 1.0, 0.0).astype(bf16)


def vector_maps(place):
    per_row = D // (2 * HALF)
    return (
        chosen(2 * HALF, 2 * HALF * (place.index % per_row)),
        chosen(HALF, HALF * place.index),
        [chosen(SLICE, SLICE * place.chip, SLICE * n) for n in range(3)],
        place.index // per_row,
    )


def place_vectors(place, pieces_ref, out_ref):
    pieces = pieces_ref[...].astype(bf16)
    attend_map, single_map, expand_maps, half = vector_maps(place)
    attend = dot_nn(pieces, attend_map)
    single = dot_nn(pieces, single_map)
    expand = jnp.concatenate([dot_nn(pieces, m)[2:3] for m in expand_maps], axis=0)
    out_ref[...] = jnp.concatenate(
        [
            jnp.where(half == 0, attend[0:1], 0.0),
            jnp.where(half == 1, attend[0:1], 0.0),
            single[1:2],
            jnp.where(place.c == 0, expand, 0.0),
            jnp.where(place.c == 1, expand, 0.0),
            single[3:8],
            jnp.zeros((2, D), f32),
        ],
        axis=0,
    ).astype(bf16)


def own_vectors(place, sums):
    attend_map, single_map, expand_maps, half = vector_maps(place)
    high = sums.astype(bf16)
    rest = sums - high.astype(f32)
    middle = rest.astype(bf16)
    low = (rest - middle.astype(f32)).astype(bf16)
    parts = jnp.concatenate([high, middle, low], axis=0)

    def pick(chosen_map):
        found = dot_nt(parts, chosen_map)
        return found[:VEC_ROWS] + found[VEC_ROWS : 2 * VEC_ROWS] + found[2 * VEC_ROWS :]

    attend, single = pick(attend_map), pick(single_map)
    expand = 0.0
    for n, chosen_map in enumerate(expand_maps):
        found = pick(chosen_map)
        expand += jnp.where(place.c == 0, found[ROW_EXPAND + n], found[ROW_EXPAND + 3 + n])[None]
    return jnp.concatenate(
        [
            jnp.where(half == 0, attend[0:1], attend[1:2]),
            single[ROW_MERGE : ROW_MERGE + 1],
            expand,
            single[ROW_SHRINK : ROW_SHIFT + 2],
        ],
        axis=0,
    )


def lane_groups(read, write, moves):
    for target, sources in enumerate(moves):
        parts = []
        for group, (tile, at) in enumerate(sources):
            value = read(tile)
            shift = (group - at) * SLICE % LANES
            parts.append(pltpu.roll(value, shift, 1) if shift else value)
        lane = lax.broadcasted_iota(jnp.int32, parts[0].shape, 1) // SLICE
        write(target, jnp.where(lane < 2, jnp.where(lane == 0, parts[0], parts[1]), jnp.where(lane == 2, parts[2], parts[3])))


def ff_moves(inverse):
    outer, inner = (JOBS, CHIPS) if not inverse else (CHIPS, JOBS)
    units = [b * outer + a for a in range(outer) for b in range(inner)]
    return [[(u // 4, u % 4) for u in units[4 * t : 4 * t + 4]] for t in range(FF // LANES)]


def compose(place, pack_ref, twin_ref, source_cols):
    mine = pack_ref[:, source_cols].astype(f32)[:HALF]
    other = twin_ref[:, source_cols].astype(f32)[:HALF]
    first = jnp.where(place.c == 0, mine, other)
    second = jnp.where(place.c == 0, other, mine)
    return jnp.concatenate([first, second], axis=0).astype(bf16)


def layer_kernel(
    bucket, lengths, keeps, x_any, g_any, attend_any, merge_any, expand_any, shrink_any, pieces_any,
    out_any, ig_any, ga_any, gm_any, ge_any, gs_any, vec_out, active_any, slope_any,
    attend_ref, merge_ref, expand_ref, shrink_ref, pieces_ref, ge_own, wa, wm, we, ws, ga, pack, pack_twin, vec_parts, vec_land, vec,
    x, g, q, k, v, query_const, key_const, mixed, logsum, xhat, low, xt, lowt, active, slope, first,
    a0, a1, a2, a3, m0, m1, m2, m3, e0, e1, e2, e3, f1, f2, f3, s0, s1, s2, s3, fa, fm, fe, fs, gain, gain_land,
    g_send, g_recv, gt_send, gt_recv, r_send, r_recv, rt_send, rt_recv, own_send, own_recv, vec_send, vec_recv,
    sum_send, sum_recv, last_send, last_recv, local, flow,
):
    place = Place()
    c = place.c
    place.greet()
    shards = [
        pltpu.make_async_copy(source, target, local.at[4 + n])
        for n, (source, target) in enumerate(
            (
                (expand_any, expand_ref), (pieces_any, pieces_ref), (attend_any, attend_ref), (merge_any, merge_ref),
                (shrink_any, shrink_ref),
            )
        )
    ]
    x_copy = pltpu.make_async_copy(x_any, x, local.at[0])
    g_copy = pltpu.make_async_copy(g_any, g, local.at[1])
    for copy in shards + [x_copy, g_copy]:
        copy.start()
    token_tables(
        bucket[0], [lengths[0, b] for b in range(SLOTS)], [keeps[0, b] for b in range(SLOTS)],
        query_const, key_const, logsum,
    )
    for copy in shards:
        copy.wait()

    pack[0:HALF, 0 : 3 * D] = attend_ref[...]
    pack[0:HALF, 3 * D : 4 * D] = merge_ref[...]

    def put_expand(tile, value):
        pack[0:HALF, 4 * D + LANES * tile : 4 * D + LANES * (tile + 1)] = value.astype(bf16)

    lane_groups(
        lambda tile: expand_ref[:, LANES * tile : LANES * (tile + 1)].astype(f32), put_expand, ff_moves(False)
    )
    place_vectors(place, pieces_ref, vec_parts.at[0])
    x_copy.wait()
    xt[...] = x[...].T
    place.met()

    own_pack = remote(pack, pack_twin, own_send.at[0], own_recv.at[0], place.twin)
    own_pack.start()
    their_cols = pl.ds(aligned(384 * (1 - c), 128), 384)
    my_cols = pl.ds(aligned(384 * c, 128), 384)
    my_rows = pl.ds(aligned(FF_HALF * c, FF_HALF), FF_HALF)
    own_shrink = remote(
        shrink_ref.at[:, their_cols], ws.at[place.z, place.y, place.x, my_rows, their_cols],
        own_send.at[1], own_recv.at[1], place.twin,
    )

    class Sums:
        def __init__(self, source, land, sends, recvs, order):
            self.source, self.land, self.steps = source, land, []
            at = 0
            for step, peers in enumerate([(place.twin,)] + [tuple(p for _, p in place.over[a]) for a in order]):
                self.steps.append([])
                for peer in peers:
                    copy = remote(source.at[step], land.at[at], sends.at[at], recvs.at[at], peer)
                    self.steps[-1].append((copy, at))
                    at += 1

        def run(self, step):
            if step > 0:
                total = self.source[step - 1].astype(f32)
                for copy, at in self.steps[step - 1]:
                    copy.wait_recv()
                    total += self.land[at].astype(f32)
                if step == 4:
                    return total
                self.source[step] = total.astype(self.source.dtype)
            for copy, _ in self.steps[step]:
                copy.start()

        def finish(self):
            for copies in self.steps:
                for copy, _ in copies:
                    copy.wait_send()

    vec_sums = Sums(vec_parts, vec_land, vec_send, vec_recv, "zxy")
    grad_sums = Sums(gain, gain_land, sum_send, sum_recv, "xyz")

    vec_sums.run(0)
    own_shrink.start()

    def gathers(t):
        def one(ref, cuts, at):
            return Gather(place, ref, cuts, g_send.at[at], g_recv.at[at], gt_send.at[at], gt_recv.at[at])

        if t < 3:
            return [one(wa, attend_cuts(c, t), t)]
        if t == 3:
            return [one(wm, merge_cuts(c), 3)]
        j = t - 4
        return [one(we, expand_cuts(c, j), 4 + 2 * j), one(ws, shrink_cuts(c, j), 5 + 2 * j)]

    def gather_events(names):
        for step, t in names:
            if t == VECTORS:
                vec_sums.run(step)
                continue
            for one in gathers(t):
                one.run(step)

    def when(index, table, events):
        for value, names in table.items():

            @pl.when(index == value)
            def _():
                events(names)

    own_pack.wait_recv()
    for group in range(3):
        for n in range(3):
            cols = aligned(256 * group + 128 * c, 128)
            wa[place.z, place.y, place.x, n, :, pl.ds(cols, 128)] = compose(
                place, pack, pack_twin, pl.ds(aligned(D * n + cols, 128), 128)
            )
    wm[place.z, place.y, place.x, :, my_cols] = compose(
        place, pack, pack_twin, pl.ds(aligned(3 * D + 384 * c, 128), 384)
    )
    for j in range(JOBS):
        cols = aligned(PART * j + 256 * c, 128)
        we[place.z, place.y, place.x, :, pl.ds(cols, 256)] = compose(
            place, pack, pack_twin, pl.ds(aligned(4 * D + cols, 128), 256)
        )
    ws[place.z, place.y, place.x, my_rows, my_cols] = shrink_ref[:, my_cols]
    own_shrink.wait_recv()
    gather_events(G_START)
    vec[...] = vec_sums.run(4)

    def heads(i, carry):
        when(i, G_HEADS, gather_events)
        for group in range(3):

            @pl.when(i == 4 * group)
            def _():
                for one in gathers(group):
                    one.ready()

        @pl.when(i % 4 == 0)
        def _():
            cols = pl.ds(aligned(256 * (i // 4), 256), 256)
            tokens = x[...]
            part = dot_nn(tokens, wa[:, :, :, 0, :, cols].reshape(D, 256))
            q[:, cols] = ((part + vec[0:1, cols]) * 0.125).astype(bf16)
            k[:, cols] = dot_nn(tokens, wa[:, :, :, 1, :, cols].reshape(D, 256)).astype(bf16)
            part = dot_nn(tokens, wa[:, :, :, 2, :, cols].reshape(D, 256))
            v[:, cols] = (part + vec[1:2, cols]).astype(bf16)

        when(i, G_READY, gather_events)
        attend_forward(i, query_const, key_const, q, k, v, mixed, logsum, LONG)
        return carry

    lax.fori_loop(0, 12, heads, 0)
    gather_events(G_MERGE)
    for one in gathers(3):
        one.ready()
    tile = 512

    def merge_norm(i, carry):
        rows = pl.ds(aligned(i * tile, tile), tile)
        branch = dot_nn(mixed[rows, :], wm[...].reshape(D, D)) + vec[ROW_MERGE : ROW_MERGE + 1, :]
        x_hat, deviation = norm_parts(x[rows, :].astype(f32) + branch)
        xhat[rows, :] = x_hat.astype(bf16)
        logsum[rows, :] = jnp.where(lane_index(tile) == RSTD_LANE, deviation, logsum[rows, :])
        normed = x_hat * vec[ROW_GAIN : ROW_GAIN + 1, :] + vec[ROW_SHIFT : ROW_SHIFT + 1, :]
        low[rows, :] = normed.astype(bf16)
        first[rows, :] = normed + vec[ROW_SHRINK : ROW_SHRINK + 1, :]
        return carry

    lax.fori_loop(0, T // tile, merge_norm, 0)
    lowt[...] = low[...].T

    def out_copies(j):
        return (
            pltpu.make_async_copy(active.at[j % 2], active_any.at[j], flow.at[0, j % 2]),
            pltpu.make_async_copy(slope.at[j % 2], slope_any.at[j], flow.at[1, j % 2]),
        )

    def back_copies(j):
        return (
            pltpu.make_async_copy(active_any.at[j], active.at[j % 2], flow.at[0, j % 2]),
            pltpu.make_async_copy(slope_any.at[j], slope.at[j % 2], flow.at[1, j % 2]),
        )

    def expand_part(j, carry):
        when(j, G_FFN, gather_events)

        @pl.when(j >= 2)
        def _():
            for copy in out_copies(j - 2):
                copy.wait()

        for t in range(JOBS):

            @pl.when(j == t)
            def _():
                for one in gathers(4 + t):
                    one.ready()

        a_ref, s_ref = active.at[j % 2], slope.at[j % 2]
        for h in range(2):
            here = slice(256 * h, 256 * h + 256)
            cols = pl.ds(aligned(PART * j + 256 * h, 256), 256)
            bias = vec[pl.ds(ROW_EXPAND + j, 1), here]
            expanded = dot_nn(low[...], we[:, :, :, :, cols].reshape(D, 256)) + bias
            a, s = gelu_parts(expanded)
            a_ref[:, here] = a.astype(bf16)
            s_ref[:, here] = s.astype(bf16)
        when(j, G_FFN_MIDDLE, gather_events)
        rows = pl.ds(aligned(SLICE * j, SLICE), SLICE)
        first[...] += dot_nn(a_ref[...], ws[:, :, :, rows, :].reshape(PART, D))

        @pl.when(j < JOBS - 2)
        def _():
            for copy in out_copies(j):
                copy.start()

        return carry

    lax.fori_loop(0, JOBS, expand_part, 0)
    g_copy.wait()
    gain[0] = jnp.zeros((VEC_ROWS, D), f32)

    def end_of_forward(i, carry):
        rows = pl.ds(aligned(i * tile, tile), tile)
        x_hat, deviation = norm_parts(first[rows, :])
        weight = vec[ROW_GAIN + 1 : ROW_GAIN + 2, :]
        result = x_hat * weight + vec[ROW_SHIFT + 1 : ROW_SHIFT + 2, :]
        keep = column_of(logsum[rows, :], KEEP_LANE) > 0.0
        dy = jnp.where(keep, g[rows, :].astype(f32), 0.0)
        g[rows, :] = jnp.where(keep, result, x[rows, :].astype(f32)).astype(bf16)
        grad = norm_back(dy * weight, x_hat, deviation)
        first[rows, :] = grad
        branch = grad.astype(bf16)
        low[rows, :] = branch
        gain[0, ROW_GAIN + 1 : ROW_GAIN + 2, :] += jnp.sum(dy * x_hat, axis=0, keepdims=True)
        gain[0, ROW_SHIFT + 1 : ROW_SHIFT + 2, :] += jnp.sum(dy, axis=0, keepdims=True)
        gain[0, ROW_SHRINK : ROW_SHRINK + 1, :] += jnp.sum(branch.astype(f32), axis=0, keepdims=True)
        return carry

    lax.fori_loop(0, T // tile, end_of_forward, 0)
    out_copy = pltpu.make_async_copy(g, out_any, local.at[2])
    out_copy.start()

    def reductions(t):
        def one(ref, land0, lands, final, cuts, at, *args):
            sems = (r_send.at[at], r_recv.at[at], rt_send.at[at], rt_recv.at[at])
            return Reduce(place, ref, land0, lands, final, cuts(c, *args), cuts(1 - c, *args), sems)

        if t < JOBS:
            j = JOBS - 1 - t
            return [
                one(we, e0.at[t % 2], [[ref.at[t] for ref in (e1, e2, e3)], [ref.at[t] for ref in (f1, f2, f3)]], fe, expand_cuts, 2 * t, j),
                one(ws, s0.at[t % 2], [[ref.at[t] for ref in (s1, s2, s3)]], fs, shrink_cuts, 2 * t + 1, j),
            ]
        if t == JOBS:
            return [one(wm, m0, [[m1, m2, m3]], fm, merge_cuts, 2 * JOBS)]
        n = t - JOBS - 1
        return [one(ga, a0.at[n % 2], [[ref.at[n] for ref in (a1, a2, a3)]], fa, attend_cuts, 2 * JOBS + 1 + n, n)]

    def reduce_events(names):
        for step, t in names:
            if t == VECTORS:
                grad_sums.run(step)
                continue
            for one in reductions(t):
                one.run(step)

    def expand_back(b, carry):
        j = JOBS - 1 - b

        @pl.when(b >= 2)
        def _():
            for copy in back_copies(j):
                copy.wait()

        when(b, R_FFN, reduce_events)
        a_ref, s_ref = active.at[j % 2], slope.at[j % 2]
        rows = pl.ds(aligned(SLICE * j, SLICE), SLICE)
        cols = pl.ds(aligned(PART * j, PART), PART)
        s_in = low[...]
        for h in range(2):
            here = slice(256 * h, 256 * h + 256)
            e_in = dot_nt(s_in, ws[2 * h : 2 * h + 2, :, :, rows, :].reshape(256, D)) * s_ref[:, here].astype(f32)
            e_in = e_in.astype(bf16)
            s_ref[:, here] = e_in
            gain[0, pl.ds(ROW_EXPAND + j, 1), here] = jnp.sum(e_in.astype(f32), axis=0, keepdims=True)
        when(b, R_FFN_MIDDLE, reduce_events)
        for h in range(2):
            grad = dot_tn(a_ref[:, 256 * h : 256 * h + 256], s_in).astype(bf16)
            ws[2 * h : 2 * h + 2, :, :, rows, :] = grad.reshape(2, Y, X, SLICE, D)
        first[...] += dot_nt(s_ref[...], we[:, :, :, :, cols].reshape(D, PART))
        for h in range(2):
            here = pl.ds(aligned(PART * j + 256 * h, 256), 256)
            grad = dot_nn(lowt[...], s_ref[:, 256 * h : 256 * h + 256]).astype(bf16)
            we[:, :, :, :, here] = grad.reshape(Z, Y, X, BLOCK, 256)
        when(b, {t: [(0, t)] for t in range(JOBS)}, reduce_events)

        @pl.when(b < JOBS - 2)
        def _():
            for copy in back_copies(j - 2):
                copy.start()

        return carry

    for t in range(4 + JOBS):
        for one in gathers(t):
            one.finish()
    lax.fori_loop(0, JOBS, expand_back, 0)

    def middle(i, carry):
        when(i, R_NORM, reduce_events)
        rows = pl.ds(aligned(i * tile, tile), tile)
        dy, x_hat = first[rows, :], xhat[rows, :].astype(f32)
        deviation = column_of(logsum[rows, :], RSTD_LANE)
        grad = norm_back(dy * vec[ROW_GAIN : ROW_GAIN + 1, :], x_hat, deviation)
        first[rows, :] = grad
        branch = grad.astype(bf16)
        low[rows, :] = branch
        gain[0, ROW_GAIN : ROW_GAIN + 1, :] += jnp.sum(dy * x_hat, axis=0, keepdims=True)
        gain[0, ROW_SHIFT : ROW_SHIFT + 1, :] += jnp.sum(dy, axis=0, keepdims=True)
        gain[0, ROW_MERGE : ROW_MERGE + 1, :] += jnp.sum(branch.astype(f32), axis=0, keepdims=True)
        x[rows, :] = dot_nt(branch, wm[...].reshape(D, D)).astype(bf16)
        return carry

    lax.fori_loop(0, T // tile, middle, 0)
    out_copy.wait()
    g_again = pltpu.make_async_copy(g_any, g, local.at[1])
    g_again.start()
    reduce_events(R_MERGE)
    wm[...] = dot_tn(mixed[...], low[...]).astype(bf16).reshape(Z, Y, X, BLOCK, D)
    reduce_events([(0, JOBS)])

    def heads_back(i, carry):
        when(i, R_HEADS, reduce_events)
        attend_backward(i, query_const, key_const, q, k, v, mixed, logsum, x, q, k, v, LONG)

        when(i, R_HEADS_END, reduce_events)

        @pl.when(i % 4 == 3)
        def _():
            cols = pl.ds(aligned(256 * (i // 4), 256), 256)
            for n, grads in enumerate((q, k, v)):
                grad = dot_nn(xt[...], grads[:, cols]).astype(bf16)
                ga[:, :, :, n, :, cols] = grad.reshape(Z, Y, X, BLOCK, 256)
                if n != 1:
                    gain[0, n // 2 : n // 2 + 1, cols] = jnp.sum(grads[:, cols].astype(f32), axis=0, keepdims=True)

        when(i, {4 * n + 3: [(0, JOBS + 1 + n)] for n in range(3)}, reduce_events)
        return carry

    lax.fori_loop(0, 12, heads_back, 0)
    grad_sums.run(0)

    def last_copy(ref, n, cols, height):
        rows = pl.ds(aligned(height * (1 - c), 8), height)
        here = ref.at[:, rows, cols] if len(ref.shape) == 3 else ref.at[rows, cols]
        return remote(here, here, last_send.at[n], last_recv.at[n], place.twin)

    early_last = [last_copy(fm, 0, my_cols, HALF), last_copy(fs, 1, my_cols, FF_HALF)]
    early_last += [last_copy(fe, 2 + j, expand_cuts(c, j)[0].cols, HALF) for j in range(JOBS)]
    attend_last = [last_copy(fa, 2 + JOBS + n, attend_cuts(c, n)[0].cols, HALF) for n in range(3)]

    reduce_events(R_TAIL[0])
    g_again.wait()

    def inputs_part(i, carry):
        @pl.when(i == 1)
        def _():
            reduce_events(R_TAIL[1])

        rows = pl.ds(aligned(i * tile, tile), tile)
        keep = column_of(logsum[rows, :], KEEP_LANE) > 0.0
        total = first[rows, :] + jnp.where(keep, 0.0, g[rows, :].astype(f32))
        for n, grads in enumerate((q, k, v)):
            total += dot_nt(grads[rows, :], wa[:, :, :, n, :, :].reshape(D, D))
        first[rows, :] = total
        return carry

    lax.fori_loop(0, T // tile, inputs_part, 0)
    out_ig = pltpu.make_async_copy(first, ig_any, local.at[3])
    out_ig.start()
    reduce_events(R_TAIL[2])
    for copy in early_last + attend_last[:2]:
        copy.start()
    mine, ff_mine = pl.ds(aligned(HALF * c, 8), HALF), pl.ds(aligned(FF_HALF * c, 8), FF_HALF)
    for copy in early_last:
        copy.wait_recv()
    done = [
        pltpu.make_async_copy(fm.at[mine], gm_any, local.at[4]),
        pltpu.make_async_copy(fs.at[ff_mine], gs_any, local.at[5]),
        pltpu.make_async_copy(ge_own, ge_any, local.at[6]),
    ]
    done[0].start()
    done[1].start()

    def put_grad(tile, value):
        ge_own[:, LANES * tile : LANES * (tile + 1)] = value

    lane_groups(lambda tile: fe[mine, LANES * tile : LANES * (tile + 1)], put_grad, ff_moves(True))
    done[2].start()
    own_pack.wait_send()
    own_shrink.wait_send()
    for copy in early_last:
        copy.wait_send()
    vec_sums.finish()
    for t in range(JOBS + 3):
        for one in reductions(t):
            one.finish()
    for copy in attend_last[:2]:
        copy.wait_recv()
        copy.wait_send()
    vec_out[...] = own_vectors(place, grad_sums.run(4))
    grad_sums.finish()
    reduce_events(R_TAIL[3])
    attend_last[2].start()
    for one in reductions(JOBS + 3):
        one.finish()
    attend_last[2].wait_recv()
    done += [
        pltpu.make_async_copy(fa.at[n, mine], ga_any.at[:, pl.ds(D * n, D)], local.at[7 + n]) for n in range(3)
    ]
    for copy in done[3:]:
        copy.start()
    attend_last[2].wait_send()
    for copy in done + [out_ig]:
        copy.wait()


ANY = pl.BlockSpec(memory_space=pl.ANY)
VM = pl.BlockSpec(memory_space=pltpu.VMEM)
SM = pl.BlockSpec(memory_space=pltpu.SMEM)


def layer_call(buckets, lengths, keeps, inputs, upstream, attend, merge, expand, shrink, pieces):
    dma = pltpu.SemaphoreType.DMA

    def landing(rows, cols, jobs=None, deep=(), slots=None, parts=1):
        lead = (jobs,) if jobs else ()
        stages = [(Z, 2), (Z,), (3,), (Z, 2), (3, 2), (1,)][: 3 * parts]
        return [pltpu.VMEM(((slots,) if slots else lead) + (Z, Y, X) + deep + (rows, cols), bf16)] + [
            pltpu.VMEM(lead + d + deep + (rows, cols // parts), bf16) for d in stages
        ]

    tokens = [pltpu.VMEM((T, D), bf16) for _ in range(5)]
    scratch = (
        [pltpu.VMEM(a.shape, a.dtype) for a in (attend, merge, expand, shrink, pieces)]
        + [pltpu.VMEM((HALF, FF), f32)]
        + [pltpu.VMEM(*s) for s in WEIGHTS]
        + [
            pltpu.VMEM(*WEIGHTS[0]),
            pltpu.VMEM((32, PACK), bf16),
            pltpu.VMEM((32, PACK), bf16),
            pltpu.VMEM((4, VEC_ROWS, D), bf16),
            pltpu.VMEM((6, VEC_ROWS, D), bf16),
            pltpu.VMEM((VEC_ROWS, D), f32),
        ]
        + tokens
        + [
            pltpu.VMEM((T, LANES), bf16),
            pltpu.VMEM((T, LANES), bf16),
            pltpu.VMEM((T, D), bf16),
            pltpu.VMEM((T, LANES), f32),
            pltpu.VMEM((T, D), bf16),
            pltpu.VMEM((T, D), bf16),
            pltpu.VMEM((D, T), bf16),
            pltpu.VMEM((D, T), bf16),
            pltpu.VMEM((2, T, PART), bf16),
            pltpu.VMEM((2, T, PART), bf16),
            pltpu.VMEM((T, D), f32),
        ]
        + landing(BLOCK, 128, 3, (3,), slots=2)
        + landing(BLOCK, 384)
        + landing(BLOCK, 256, JOBS, slots=2, parts=2)
        + landing(SLICE, 384, JOBS, slots=2)
        + [
            pltpu.VMEM((3, BLOCK, D), f32),
            pltpu.VMEM((BLOCK, D), f32),
            pltpu.VMEM((BLOCK, FF), f32),
            pltpu.VMEM((FF_BLOCK, D), f32),
            pltpu.VMEM((4, VEC_ROWS, D), f32),
            pltpu.VMEM((6, VEC_ROWS, D), f32),
        ]
        + 2 * [dma((GATHERS, 2, 5)), dma((GATHERS, 2, 5)), dma((GATHERS,)), dma((GATHERS,))]
        + 2 * [dma((2,))]
        + 4 * [dma((6,))]
        + 2 * [dma((5 + JOBS,))]
        + [dma((10,)), dma((2, 2))]
    )
    return pl.pallas_call(
        layer_kernel,
        out_shape=tuple(
            jax.ShapeDtypeStruct(*s)
            for s in (
                ((T, D), bf16), ((T, D), f32), ((HALF, 3 * D), f32), ((HALF, D), f32), ((HALF, FF), f32),
                ((FF_HALF, D), f32), ((PIECES, LANES), f32), ((JOBS, T, PART), bf16), ((JOBS, T, PART), bf16),
            )
        ),
        in_specs=[SM] * 3 + [ANY] * 7,
        out_specs=[ANY] * 6 + [VM] + [ANY] * 2,
        scratch_shapes=scratch,
        compiler_params=pltpu.CompilerParams(collective_id=0, has_side_effects=True, vmem_limit_bytes=VMEM_LIMIT),
        cost_estimate=pl.CostEstimate(flops=60_000_000_000, bytes_accessed=60_000_000, transcendentals=20_000_000),
    )(buckets, lengths, keeps, inputs, upstream, attend, merge, expand, shrink, pieces)


def pack_pieces(attend_bias, merge_bias, expand_bias, shrink_bias, gain, shift):
    total = 0.0
    vectors = (attend_bias[None], merge_bias[None], expand_bias[None], shrink_bias[None], gain, shift)
    row = 0
    for piece in vectors:
        count, width = piece.shape
        total += jnp.pad(piece.astype(f32), ((row, PIECES - row - count), (0, LANES - width)))
        row += count
    return total


def finish_kernel(*refs):
    count = len(RESULTS)
    sources, own, wide, vectors = refs[:count], refs[count], refs[count + 1 : 2 * count + 1], refs[2 * count + 1 : -count - 2]
    held, arrive, leave = refs[-count - 2 : -2], refs[-2], refs[-1]
    steps = [
        (pltpu.make_async_copy(s, h, arrive.at[n]), pltpu.make_async_copy(h, w, leave.at[n]))
        for n, (s, h, w) in enumerate(zip(sources, held, wide))
    ]
    for into, _ in steps:
        into.start()
    row = 0
    for ref in vectors:
        if len(ref.shape) == 1:
            ref[...] = own[row, : ref.shape[0]]
            row += 1
        else:
            ref[...] = own[row : row + ref.shape[0], : ref.shape[1]]
            row += ref.shape[0]
    for into, out in steps:
        into.wait()
        out.start()
    for _, out in steps:
        out.wait()


RESULTS = (
    ((T, D), f32), ((T, D), bf16), ((HALF, 3 * D), f32), ((HALF, D), f32), ((HALF, FF), f32), ((FF_HALF, D), f32),
)


def finish_call(wide, own, vectors):
    dma = pltpu.SemaphoreType.DMA
    return pl.pallas_call(
        finish_kernel,
        out_shape=tuple(jax.ShapeDtypeStruct(*s) for s in RESULTS)
        + tuple(jax.ShapeDtypeStruct(v.shape, f32) for v in vectors),
        in_specs=[ANY] * len(RESULTS) + [VM],
        out_specs=[ANY] * len(RESULTS) + [VM] * len(vectors),
        scratch_shapes=[pltpu.VMEM(*s) for s in RESULTS] + 2 * [dma((len(RESULTS),))],
        compiler_params=pltpu.CompilerParams(vmem_limit_bytes=VMEM_LIMIT),
    )(*wide, own)

def layer_norm(hidden, gains, shifts):
    center = hidden - jnp.mean(hidden, axis=-1, keepdims=True)
    spread = jnp.mean(center * center, axis=-1, keepdims=True)
    return center * lax.rsqrt(spread + epsilon) * gains + shifts


def gelu_exact(values):
    return jax.nn.gelu(values, approximate=False)


def matmul(left, right):
    return jnp.dot(left, right, preferred_element_type=jnp.float32)


def token_info(bucket, slot_lengths, slot_keeps):
    position = jnp.arange(TOK_DEV, dtype=jnp.int32)
    span_size = jnp.where(bucket > 0, LONG, SHORT).astype(jnp.int32)
    sequence = position // span_size
    within = position - sequence * span_size
    slot_index = sequence * (span_size // SHORT)
    matches = (slot_index[:, None] == jnp.arange(SLOTS, dtype=jnp.int32)[None, :]).astype(jnp.int32)
    length = jnp.sum(matches * slot_lengths[None, :], axis=1) + bucket * (LONG - SHORT)
    keep_flags = jnp.sum(matches * slot_keeps[None, :], axis=1)
    return (sequence, within < length, keep_flags > 0)


def masked_scores(queries, key_rows, sequence, valid_key):
    scores = jnp.einsum("qhd,khd->hqk", queries, key_rows, preferred_element_type=jnp.float32)
    allowed = (sequence[:, None] == sequence[None, :]) & valid_key[None, :]
    return jnp.where(allowed[None], scores, masked_score)


def attend_block(pieces):
    queries, key_rows, values, sequence, valid_key = pieces
    scores = masked_scores(queries, key_rows, sequence, valid_key)
    highest = jnp.max(scores, axis=-1, keepdims=True)
    raised = jnp.exp(scores - highest)
    row_total = jnp.sum(raised, axis=-1, keepdims=True)
    weights = raised / row_total
    mixed_rows = jnp.einsum(
        "hqk,khd->qhd", weights.astype(jnp.bfloat16), values, preferred_element_type=jnp.float32
    )
    return (mixed_rows, highest[:, :, 0] + jnp.log(row_total[:, :, 0]))


def attend_back(pieces):
    queries, key_rows, values, sequence, valid_key, logsum, mixed_grad = pieces
    scores = masked_scores(queries, key_rows, sequence, valid_key)
    weights = jnp.exp(scores - logsum[:, :, None])
    weight_grad = jnp.einsum("qhd,khd->hqk", mixed_grad, values, preferred_element_type=jnp.float32)
    row_dot = jnp.sum(weights * weight_grad, axis=-1, keepdims=True)
    score_grad = (weights * (weight_grad - row_dot)).astype(jnp.bfloat16)
    query_part = jnp.einsum(
        "hqk,khd->qhd", score_grad, key_rows, preferred_element_type=jnp.float32
    ).astype(jnp.bfloat16)
    key_part = jnp.einsum(
        "hqk,qhd->khd", score_grad, queries, preferred_element_type=jnp.float32
    ).astype(jnp.bfloat16)
    value_part = jnp.einsum(
        "hqk,qhd->khd", weights.astype(jnp.bfloat16), mixed_grad, preferred_element_type=jnp.float32
    ).astype(jnp.bfloat16)
    return (query_part, key_part, value_part)


def heads_view(source):
    return source.reshape(source.shape[0] // LONG, LONG, HEADS, HD)


def forward_pass(inputs, weights, sequence, valid_key, keep_flags):
    (
        attend_matrix,
        attend_offset,
        merge_matrix,
        merge_offset,
        expand_matrix,
        expand_offset,
        shrink_matrix,
        shrink_offset,
        gains,
        shifts,
    ) = weights
    model_width = inputs.shape[1]
    blocks = inputs.shape[0] // LONG
    packed = matmul(inputs, attend_matrix)
    offset = attend_offset.astype(jnp.float32)
    queries = ((packed[:, :model_width] + offset[:model_width]) * 0.125).astype(jnp.bfloat16)
    key_rows = packed[:, model_width : 2 * model_width].astype(jnp.bfloat16)
    values = (packed[:, 2 * model_width :] + offset[model_width:]).astype(jnp.bfloat16)
    mixed_rows, logsum = lax.map(
        attend_block,
        (
            heads_view(queries),
            heads_view(key_rows),
            heads_view(values),
            sequence.reshape(blocks, LONG),
            valid_key.reshape(blocks, LONG),
        ),
    )
    mixed_rows = mixed_rows.reshape(-1, model_width).astype(jnp.bfloat16)
    tokens = inputs.astype(jnp.float32)
    first_sum = tokens + matmul(mixed_rows, merge_matrix) + merge_offset.astype(jnp.float32)
    normed = layer_norm(first_sum, gains[0].astype(jnp.float32), shifts[0].astype(jnp.float32))
    normed_low = normed.astype(jnp.bfloat16)
    expanded = matmul(normed_low, expand_matrix) + expand_offset.astype(jnp.float32)
    active = gelu_exact(expanded).astype(jnp.bfloat16)
    second_sum = normed + matmul(active, shrink_matrix) + shrink_offset.astype(jnp.float32)
    result = layer_norm(second_sum, gains[1].astype(jnp.float32), shifts[1].astype(jnp.float32))
    outputs = jnp.where(keep_flags[:, None], result, tokens).astype(jnp.bfloat16)
    return (
        outputs,
        (
            queries,
            key_rows,
            values,
            logsum,
            mixed_rows,
            first_sum,
            normed_low,
            expanded,
            active,
            second_sum,
        ),
    )


def backward_pass(inputs, upstream, weights, saved, sequence, valid_key, keep_flags):
    (
        attend_matrix,
        attend_offset,
        merge_matrix,
        merge_offset,
        expand_matrix,
        expand_offset,
        shrink_matrix,
        shrink_offset,
        gains,
        shifts,
    ) = weights
    (
        queries,
        key_rows,
        values,
        logsum,
        mixed_rows,
        first_sum,
        normed_low,
        expanded,
        active,
        second_sum,
    ) = saved
    model_width = inputs.shape[1]
    blocks = inputs.shape[0] // LONG
    cotangent = upstream.astype(jnp.float32)
    result_grad = jnp.where(keep_flags[:, None], cotangent, 0.0)
    second_out, pull_second = jax.vjp(
        layer_norm, second_sum, gains[1].astype(jnp.float32), shifts[1].astype(jnp.float32)
    )
    second_grad, gain_two, shift_two = pull_second(result_grad)
    shrink_in = second_grad.astype(jnp.bfloat16)
    shrink_grad = jnp.einsum("tf,td->fd", active, shrink_in, preferred_element_type=jnp.float32)
    shrink_offset_grad = jnp.sum(shrink_in.astype(jnp.float32), axis=0)
    active_grad = jnp.einsum(
        "td,fd->tf", shrink_in, shrink_matrix, preferred_element_type=jnp.float32
    )
    gelu_out, pull_gelu = jax.vjp(gelu_exact, expanded)
    expand_in = pull_gelu(active_grad)[0].astype(jnp.bfloat16)
    expand_grad = jnp.einsum("td,tf->df", normed_low, expand_in, preferred_element_type=jnp.float32)
    expand_offset_grad = jnp.sum(expand_in.astype(jnp.float32), axis=0)
    normed_grad = second_grad + jnp.einsum(
        "tf,df->td", expand_in, expand_matrix, preferred_element_type=jnp.float32
    )
    first_out, pull_first = jax.vjp(
        layer_norm, first_sum, gains[0].astype(jnp.float32), shifts[0].astype(jnp.float32)
    )
    first_grad, gain_one, shift_one = pull_first(normed_grad)
    branch_in = first_grad.astype(jnp.bfloat16)
    merge_grad = jnp.einsum("td,te->de", mixed_rows, branch_in, preferred_element_type=jnp.float32)
    merge_offset_grad = jnp.sum(branch_in.astype(jnp.float32), axis=0)
    mixed_grad = jnp.einsum(
        "te,de->td", branch_in, merge_matrix, preferred_element_type=jnp.float32
    ).astype(jnp.bfloat16)
    query_part, key_part, value_part = lax.map(
        attend_back,
        (
            heads_view(queries),
            heads_view(key_rows),
            heads_view(values),
            sequence.reshape(blocks, LONG),
            valid_key.reshape(blocks, LONG),
            logsum,
            heads_view(mixed_grad),
        ),
    )
    query_grad = query_part.reshape(-1, model_width) * 0.125
    packed_grad = jnp.concatenate(
        [query_grad, key_part.reshape(-1, model_width), value_part.reshape(-1, model_width)], axis=1
    )
    attend_grad = jnp.einsum("td,te->de", inputs, packed_grad, preferred_element_type=jnp.float32)
    attend_offset_grad = jnp.concatenate(
        [
            jnp.sum(query_grad.astype(jnp.float32), axis=0),
            jnp.sum(value_part.reshape(-1, model_width).astype(jnp.float32), axis=0),
        ]
    )
    input_grad = (
        first_grad
        + jnp.einsum("te,de->td", packed_grad, attend_matrix, preferred_element_type=jnp.float32)
        + jnp.where(keep_flags[:, None], 0.0, cotangent)
    )
    gain_grad = jnp.stack([gain_one, gain_two])
    shift_grad = jnp.stack([shift_one, shift_two])
    grads = (
        attend_grad,
        attend_offset_grad,
        merge_grad,
        merge_offset_grad,
        expand_grad,
        expand_offset_grad,
        shrink_grad,
        shrink_offset_grad,
        gain_grad,
        shift_grad,
    )
    return (grads, input_grad)


def general_device(
    inputs,
    upstream,
    buckets,
    lengths,
    layer_keep,
    attend_weight,
    attend_bias,
    merge_weight,
    merge_bias,
    expand_weight,
    expand_bias,
    shrink_weight,
    shrink_bias,
    norm_gain,
    norm_shift,
):
    sequence, valid_key, keep_flags = token_info(buckets[0], lengths[0], layer_keep[0])
    gathered = (
        lax.all_gather(attend_weight, ("group", "inner"), axis=0, tiled=True),
        lax.all_gather(attend_bias, ("group", "inner"), axis=0, tiled=True),
        lax.all_gather(merge_weight, ("group", "inner"), axis=0, tiled=True),
        lax.all_gather(merge_bias, ("group", "inner"), axis=0, tiled=True),
        lax.all_gather(expand_weight, ("group", "inner"), axis=0, tiled=True),
        lax.all_gather(expand_bias, ("group", "inner"), axis=0, tiled=True),
        lax.all_gather(shrink_weight, ("group", "inner"), axis=0, tiled=True),
        lax.all_gather(shrink_bias, ("group", "inner"), axis=0, tiled=True),
        lax.all_gather(norm_gain, ("group", "inner"), axis=1, tiled=True),
        lax.all_gather(norm_shift, ("group", "inner"), axis=1, tiled=True),
    )
    outputs, saved = forward_pass(inputs, gathered, sequence, valid_key, keep_flags)
    gathered = (
        lax.all_gather(attend_weight, ("group", "inner"), axis=0, tiled=True),
        lax.all_gather(attend_bias, ("group", "inner"), axis=0, tiled=True),
        lax.all_gather(merge_weight, ("group", "inner"), axis=0, tiled=True),
        lax.all_gather(merge_bias, ("group", "inner"), axis=0, tiled=True),
        lax.all_gather(expand_weight, ("group", "inner"), axis=0, tiled=True),
        lax.all_gather(expand_bias, ("group", "inner"), axis=0, tiled=True),
        lax.all_gather(shrink_weight, ("group", "inner"), axis=0, tiled=True),
        lax.all_gather(shrink_bias, ("group", "inner"), axis=0, tiled=True),
        lax.all_gather(norm_gain, ("group", "inner"), axis=1, tiled=True),
        lax.all_gather(norm_shift, ("group", "inner"), axis=1, tiled=True),
    )
    grads, input_grad = backward_pass(
        inputs, upstream, gathered, saved, sequence, valid_key, keep_flags
    )
    shares = (
        lax.psum_scatter(grads[0], ("group", "inner"), scatter_dimension=0, tiled=True),
        lax.psum_scatter(grads[1], ("group", "inner"), scatter_dimension=0, tiled=True),
        lax.psum_scatter(grads[2], ("group", "inner"), scatter_dimension=0, tiled=True),
        lax.psum_scatter(grads[3], ("group", "inner"), scatter_dimension=0, tiled=True),
        lax.psum_scatter(grads[4], ("group", "inner"), scatter_dimension=0, tiled=True),
        lax.psum_scatter(grads[5], ("group", "inner"), scatter_dimension=0, tiled=True),
        lax.psum_scatter(grads[6], ("group", "inner"), scatter_dimension=0, tiled=True),
        lax.psum_scatter(grads[7], ("group", "inner"), scatter_dimension=0, tiled=True),
        lax.psum_scatter(grads[8], ("group", "inner"), scatter_dimension=1, tiled=True),
        lax.psum_scatter(grads[9], ("group", "inner"), scatter_dimension=1, tiled=True),
    )
    return (
        outputs,
        input_grad,
        shares[0],
        shares[1],
        shares[2],
        shares[3],
        shares[4],
        shares[5],
        shares[6],
        shares[7],
        shares[8],
        shares[9],
    )

def slice_device(
    inputs, upstream, buckets, lengths, layer_keep, attend_weight, attend_bias, merge_weight, merge_bias,
    expand_weight, expand_bias, shrink_weight, shrink_bias, norm_gain, norm_shift,
):
    pieces = pack_pieces(attend_bias, merge_bias, expand_bias, shrink_bias, norm_gain, norm_shift)
    outputs, input_grad, attend, merge, expand, shrink, own = layer_call(
        buckets, lengths, layer_keep, inputs, upstream, attend_weight, merge_weight, expand_weight, shrink_weight, pieces
    )[:7]
    input_grad, outputs, attend, merge, expand, shrink, attend_b, merge_b, expand_b, shrink_b, gain, shift = finish_call(
        (input_grad, outputs, attend, merge, expand, shrink),
        own,
        (attend_bias, merge_bias, expand_bias, shrink_bias, norm_gain, norm_shift),
    )
    return (
        outputs, input_grad, attend, attend_b, merge, merge_b, expand, expand_b, shrink, shrink_b, gain, shift,
    )

def solution(mesh):
    on_slice = mesh.shape["group"] == Z * Y and mesh.shape["inner"] == 2 * X
    placed = (
        P(("group", "inner"), None),
        P(("group", "inner"), None),
        P(("group", "inner")),
        P(("group", "inner"), None),
        P(("group", "inner"), None),
        P(("group", "inner"), None),
        P(("group", "inner")),
        P(("group", "inner"), None),
        P(("group", "inner")),
        P(("group", "inner"), None),
        P(("group", "inner")),
        P(("group", "inner"), None),
        P(("group", "inner")),
        P(None, ("group", "inner")),
        P(None, ("group", "inner")),
    )
    return jax.shard_map(
        slice_device if on_slice else general_device,
        mesh=mesh,
        in_specs=placed,
        out_specs=(
            P(("group", "inner"), None),
            P(("group", "inner"), None),
            P(("group", "inner"), None),
            P(("group", "inner")),
            P(("group", "inner"), None),
            P(("group", "inner")),
            P(("group", "inner"), None),
            P(("group", "inner")),
            P(("group", "inner"), None),
            P(("group", "inner")),
            P(None, ("group", "inner")),
            P(None, ("group", "inner")),
        ),
        check_vma=False,
    )
```

```python
import jax
import jax.numpy as jnp
from jax import lax
from jax.experimental import pallas as pl
from jax.experimental.pallas import tpu as pltpu
from jax.sharding import PartitionSpec as P

HEADS = 12
HD = 64
LONG = 512
SHORT = 128
TOK_DEV = 1024
SLOTS = 8
D = 768
FF = 3072
LANES = 128
RSTD_LANE, KEEP_LANE = 12, 13
epsilon = 1e-05
masked_score = -1e30
f32 = jnp.float32
bf16 = jnp.bfloat16


def dot_nn(a, b):
    return lax.dot_general(a, b, (((1,), (0,)), ((), ())), preferred_element_type=f32)


def dot_nt(a, b):
    return lax.dot_general(a, b, (((1,), (1,)), ((), ())), preferred_element_type=f32)


def dot_tn(a, b):
    return lax.dot_general(a, b, (((0,), (0,)), ((), ())), preferred_element_type=f32)


def lane_index(rows):
    return lax.broadcasted_iota(jnp.int32, (rows, LANES), 1)


def token_tables(bucket, lengths, keeps, query_const, key_const, columns):
    shape = (TOK_DEV, LANES)
    position = lax.broadcasted_iota(jnp.int32, shape, 0)
    is_long = jnp.broadcast_to(bucket, shape) > 0
    slot = jnp.where(is_long, (position >> 9) << 2, position >> 7)
    offset = jnp.where(is_long, position & (LONG - 1), position & (SHORT - 1))
    length = jnp.zeros(shape, jnp.int32)
    keep = jnp.zeros(shape, jnp.int32)
    for b in range(SLOTS):
        here = slot == b
        length = jnp.where(here, lengths[b], length)
        keep = jnp.where(here, keeps[b], keep)
    length = length + bucket * (LONG - SHORT)
    valid = offset < length
    within = jnp.where(is_long, 0, (position >> 7) & 3)
    lane = lax.broadcasted_iota(jnp.int32, shape, 1) & (HD - 1)
    is_span = (lane >= 4) & (lane < 8)
    same = lane - 4 == within
    zero, one = jnp.zeros(shape, f32), jnp.ones(shape, f32)
    query_const[...] = jnp.where(lane == 3, one, jnp.where(is_span & ~same, one, zero)).astype(bf16)
    key_const[...] = jnp.where(
        lane < 3,
        one,
        jnp.where(((lane == 3) & ~valid) | (is_span & same), masked_score * one, zero),
    ).astype(bf16)
    columns[...] = jnp.where((lane_index(TOK_DEV) == KEEP_LANE) & (keep > 0), one, zero)


def column_of(columns, lane):
    return jnp.sum(jnp.where(lane_index(columns.shape[0]) == lane, columns, 0.0), axis=1, keepdims=True)


def three_parts(column, rows):
    wide = jnp.broadcast_to(column, (rows, LANES))
    high = wide.astype(bf16)
    rest = wide - high.astype(f32)
    middle = rest.astype(bf16)
    low = (rest - middle.astype(f32)).astype(bf16)
    return high, middle, low


def attend_forward(index, query_const, key_const, q_ref, k_ref, v_ref, mixed_ref, logsum_ref, tile):
    pair, block = index // 2, index % 2
    cols = pl.ds(pl.multiple_of(pair * LANES, LANES), LANES)
    rows = pl.ds(pl.multiple_of(block * LONG, LONG), LONG)
    lane_k = lane_index(LONG)
    k2, v2 = k_ref[rows, cols], v_ref[rows, cols]
    kc = key_const[rows, :]
    k_aug = [jnp.where((lane_k // HD) == half, k2, kc) for half in range(2)]
    lane_q = lane_index(tile)
    for t in range(LONG // tile):
        qrows = pl.ds(pl.multiple_of(block * LONG + t * tile, tile), tile)
        q2, qc = q_ref[qrows, cols], query_const[qrows, :]
        outs = []
        sums = logsum_ref[qrows, :]
        for half in range(2):
            q_aug = jnp.where((lane_q // HD) == half, q2, qc)
            scores = dot_nt(q_aug, k_aug[half])
            highest = jnp.max(scores, axis=1, keepdims=True)
            raised = jnp.exp(scores - highest)
            total = jnp.sum(raised, axis=1, keepdims=True)
            out = dot_nn(raised.astype(bf16), v2)
            outs.append(out * (1.0 / total))
            sums = jnp.where(lane_q == 2 * pair + half, highest + jnp.log(total), sums)
        logsum_ref[qrows, :] = sums
        mixed_ref[qrows, cols] = jnp.where(lane_q < HD, outs[0], outs[1]).astype(bf16)


def attend_backward(index, query_const, key_const, q_ref, k_ref, v_ref, mixed_ref, logsum_ref, mixed_grad_ref,
                    dq_ref, dk_ref, dv_ref, tile):
    pair, block = index // 2, index % 2
    cols = pl.ds(pl.multiple_of(pair * LANES, LANES), LANES)
    rows = pl.ds(pl.multiple_of(block * LONG, LONG), LONG)
    lane = lane_index(LONG)
    q2, dm2 = q_ref[rows, cols], mixed_grad_ref[rows, cols]
    product = dm2.astype(f32) * mixed_ref[rows, cols].astype(f32)
    sums = logsum_ref[rows, :]
    qc = query_const[rows, :]
    zero = jnp.zeros((LONG, LANES), bf16)
    q_aug, d_aug = [], []
    for half in range(2):
        mine = (lane // HD) == half
        at = lane & (HD - 1)
        logsum = jnp.sum(jnp.where(lane == 2 * pair + half, sums, 0.0), axis=1, keepdims=True)
        delta = jnp.sum(jnp.where(mine, product, 0.0), axis=1, keepdims=True)
        lh, lm, ll = three_parts(-logsum, LONG)
        dh, dm, dl = three_parts(-delta, LONG)
        extra = jnp.where(at == 0, lh, jnp.where(at == 1, lm, jnp.where(at == 2, ll, qc)))
        q_aug.append(jnp.where(mine, q2, extra))
        extra = jnp.where(at == 0, dh, jnp.where(at == 1, dm, jnp.where(at == 2, dl, zero)))
        d_aug.append(jnp.where(mine, dm2, extra))
    dq = [jnp.zeros((LONG, LANES), f32) for _ in range(2)]
    lane_t = lane_index(tile)
    one = jnp.ones((tile, LANES), bf16)
    zero_t = jnp.zeros((tile, LANES), bf16)
    for t in range(LONG // tile):
        krows = pl.ds(pl.multiple_of(block * LONG + t * tile, tile), tile)
        k2, v2, kc = k_ref[krows, cols], v_ref[krows, cols], key_const[krows, :]
        vc = jnp.where((lane_t & (HD - 1)) < 3, one, zero_t)
        dk, dv = [], []
        for half in range(2):
            mine = (lane_t // HD) == half
            weights = jnp.exp(dot_nt(jnp.where(mine, k2, kc), q_aug[half]))
            grads = weights * dot_nt(jnp.where(mine, v2, vc), d_aug[half])
            low, low_grads = weights.astype(bf16), grads.astype(bf16)
            dv.append(dot_nn(low, dm2))
            dk.append(dot_nn(low_grads, q2))
            dq[half] = dq[half] + dot_tn(low_grads, k2)
        dk_ref[krows, cols] = jnp.where(lane_t < HD, dk[0], dk[1]).astype(bf16)
        dv_ref[krows, cols] = jnp.where(lane_t < HD, dv[0], dv[1]).astype(bf16)
    dq_ref[rows, cols] = (jnp.where(lane < HD, dq[0], dq[1]).astype(bf16).astype(f32) * 0.125).astype(bf16)


def gelu_parts(x):
    magnitude = jnp.abs(x)
    base = 1.0 + (0.3275911 * 0.7071067811865476) * magnitude
    t = pl.reciprocal(base, approx=True)
    t = t * (2.0 - base * t)
    bell = jnp.exp2(x * x * -0.7213475204444817)
    tail = t * (0.127414796 + t * (-0.142248368 + t * (0.7107068705 + t * (-0.7265760135 + t * 0.5307027145)))) * bell
    phi = jnp.where(x >= 0.0, 1.0 - tail, tail)
    return x * phi, phi + x * (bell * 0.3989422804014327)


def norm_parts(x):
    center = x - jnp.mean(x, axis=-1, keepdims=True)
    spread = jnp.mean(center * center, axis=-1, keepdims=True)
    rstd = lax.rsqrt(spread + epsilon)
    return center * rstd, rstd


def norm_back(dy_hat, x_hat, rstd):
    a = jnp.mean(dy_hat, axis=-1, keepdims=True)
    b = jnp.mean(dy_hat * x_hat, axis=-1, keepdims=True)
    return rstd * (dy_hat - a - x_hat * b)

MESH = pl.DeviceIdType.MESH
Z, X, Y = 4, 2, 2
CHIPS = Z * Y * X
JOBS = 6
PART = FF // JOBS
BLOCK = D // CHIPS
FF_BLOCK = FF // CHIPS
SLICE = FF_BLOCK // JOBS
ALL = slice(None)


def aligned(value, unit):
    return pl.multiple_of(value, unit)


class Place:
    def __init__(self):
        group, inner = lax.axis_index("group"), lax.axis_index("inner")
        self.z, self.y, self.x, self.c = group // Y, group % Y, inner // 2, inner % 2
        self.index = group * (X * 2) + inner
        self.chip = group * X + self.x
        self.twin = (group, self.x * 2 + 1 - self.c)
        self.over = {
            "x": ((1 - self.x, (group, (1 - self.x) * 2 + self.c)),),
            "y": ((1 - self.y, (self.z * Y + 1 - self.y, inner)),),
            "z": tuple(
                (z, (z * Y + self.y, inner))
                for z in (self.z + 1 - 2 * (self.z % 2), (self.z + 2) % Z, Z - 1 - self.z)
            ),
        }
        self.peers = (self.twin,) + tuple(peer for axis in "xyz" for _, peer in self.over[axis])

    def greet(self):
        barrier = pltpu.get_barrier_semaphore()
        for peer in self.peers:
            pl.semaphore_signal(barrier, 1, device_id=peer, device_id_type=MESH)

    def met(self):
        pl.semaphore_wait(pltpu.get_barrier_semaphore(), len(self.peers))

    def at(self, whole, **given):
        return tuple(given[a] if a in given else ALL if a in whole else getattr(self, a) for a in "zyx")


def remote(source, target, send, recv, peer):
    return pltpu.make_async_remote_copy(
        src_ref=source, dst_ref=target, send_sem=send, recv_sem=recv, device_id=peer, device_id_type=MESH
    )


class Cut:
    def __init__(self, rows, cols, order=None, near=(ALL, ALL)):
        self.rows, self.cols, self.order, self.near = rows, cols, order, near


def row_parts(start, low, high, cols):
    return (
        Cut(pl.ds(aligned(start, 16), low), cols, "zxy", (pl.ds(0, low), ALL)),
        Cut(pl.ds(aligned(start + low, 16), high), cols, "zyx", (pl.ds(low, high), ALL)),
    )


def attend_cuts(core, g):
    cols = pl.ds(aligned(256 * g + 128 * core, 128), 128)
    low, high = (16, 32) if g % 2 == 0 else (32, 16)
    return Cut(pl.ds(0, BLOCK), cols), row_parts(0, low, high, cols)


def merge_cuts(core):
    cols = pl.ds(aligned(384 * core, 128), 384)
    return Cut(pl.ds(0, BLOCK), cols), row_parts(0, 32, 16, cols)


def expand_cuts(core, j):
    at = PART * j + 256 * core
    rows = pl.ds(0, BLOCK)
    orders = ("xzy", "zyx") if j % 2 == 0 else ("zxy", "yzx")
    return Cut(rows, pl.ds(aligned(at, 128), 256)), tuple(
        Cut(rows, pl.ds(aligned(at + 128 * n, 128), 128), orders[n]) for n in range(2)
    )


def shrink_cuts(core, j):
    cols = pl.ds(aligned(384 * core, 128), 384)
    half = SLICE // 2
    return Cut(pl.ds(aligned(SLICE * j, SLICE), SLICE), cols), row_parts(SLICE * j, half, half, cols)


def blocks(ref, at, cut):
    deep = (ALL,) if len(ref.shape) == 6 else ()
    return ref.at[at + deep + (cut.rows, cut.cols)]


class Gather:
    def __init__(self, place, ref, cuts, send, recv, twin_send, twin_recv):
        self.place, self.ref, (self.whole, self.parts) = place, ref, cuts
        self.send, self.recv, self.twin_send, self.twin_recv = send, recv, twin_send, twin_recv

    def stage(self, n, part, step):
        axis = part.order[step]
        here = blocks(self.ref, self.place.at(part.order[:step]), part)
        first = sum(len(self.place.over[a]) for a in part.order[:step])
        return [
            remote(here, here, self.send.at[n, first + m], self.recv.at[n, first + m], peer)
            for m, (_, peer) in enumerate(self.place.over[axis])
        ]

    def to_twin(self):
        here = blocks(self.ref, self.place.at("zyx"), self.whole)
        return remote(here, here, self.twin_send, self.twin_recv, self.place.twin)

    def run(self, step):
        for n, part in enumerate(self.parts):
            if step > 0:
                for copy in self.stage(n, part, step - 1):
                    copy.wait_recv()
            if step < 3:
                for copy in self.stage(n, part, step):
                    copy.start()
        if step == 3:
            self.to_twin().start()

    def ready(self):
        self.to_twin().wait_recv()

    def finish(self):
        for n, part in enumerate(self.parts):
            for step in range(3):
                for copy in self.stage(n, part, step):
                    copy.wait_send()
        self.to_twin().wait_send()


class Reduce:
    def __init__(self, place, ref, land0, lands, final, cuts, twin_cuts, sems):
        self.place, self.ref, (self.whole, self.parts), self.twin_whole = place, ref, cuts, twin_cuts[0]
        self.land0, self.lands, self.final = land0, lands, final
        self.send, self.recv, self.twin_send, self.twin_recv = sems
        self.deep = (ALL,) if len(ref.shape) == 6 else ()

    def twin(self):
        source = blocks(self.ref, self.place.at("zyx"), self.twin_whole)
        return remote(source, self.land0, self.twin_send, self.twin_recv, self.place.twin)

    def land(self, part, step, m):
        axis = part.order[3 - step]
        ref = self.lands[part.order[1] == "z"][step - 1]
        lead = ((ALL, ALL), (m, ALL) if axis == "z" else (ALL,), (m,))[step - 1]
        return ref.at[lead + self.deep + part.near]

    def stage(self, n, part, step):
        axis, left = part.order[3 - step], part.order[: 3 - step]
        first = sum(len(self.place.over[a]) for a in part.order[4 - step :])
        return [
            remote(
                blocks(self.ref, self.place.at(left, **{axis: there}), part), self.land(part, step, m),
                self.send.at[n, first + m], self.recv.at[n, first + m], peer,
            )
            for m, (there, peer) in enumerate(self.place.over[axis])
        ]

    def run(self, step):
        if step == 0:
            self.twin().start()
            return
        if step == 1:
            self.twin().wait_recv()
            mine = blocks(self.ref, self.place.at("zyx"), self.whole)
            mine[...] = (mine[...].astype(f32) + self.land0[...].astype(f32)).astype(bf16)
        for n, part in enumerate(self.parts):
            if step > 1:
                left = part.order[: 4 - step]
                mine = blocks(self.ref, self.place.at(left), part)
                value = mine[...].astype(f32)
                for m, copy in enumerate(self.stage(n, part, step - 1)):
                    copy.wait_recv()
                    value += self.land(part, step - 1, m)[...].astype(f32)
                if step < 4:
                    mine[...] = value.astype(bf16)
                else:
                    self.final[self.deep + (part.rows, part.cols)] = value
            if step < 4:
                for copy in self.stage(n, part, step):
                    copy.start()

    def finish(self):
        self.twin().wait_send()
        for n, part in enumerate(self.parts):
            for step in (1, 2, 3):
                for copy in self.stage(n, part, step):
                    copy.wait_send()

T = TOK_DEV
VEC_ROWS = 16
VECTORS = 99
PIECES = 8
ROW_MERGE, ROW_EXPAND, ROW_SHRINK, ROW_GAIN, ROW_SHIFT = 2, 3, 9, 10, 12
HALF, FF_HALF = BLOCK // 2, FF_BLOCK // 2
PACK = 3 * D + D + FF
GATHERS = 4 + 2 * JOBS
WEIGHTS = (
    ((Z, Y, X, 3, BLOCK, D), bf16),
    ((Z, Y, X, BLOCK, D), bf16),
    ((Z, Y, X, BLOCK, FF), bf16),
    ((Z, Y, X, FF_BLOCK, D), bf16),
)
VMEM_LIMIT = 255 * 2**18

G_START = [(0, 0), (0, 3), (1, 99), (1, 0), (0, 1), (1, 3), (0, 2), (2, 0), (2, 99), (2, 3), (0, 5), (1, 1), (0, 4), (0, 6), (3, 0), (3, 99), (1, 2)]
G_HEADS = {
    1: [(1, 4)],
    2: [(0, 7), (3, 1)],
    3: [(1, 6)],
    4: [(0, 8), (2, 5)],
    5: [(3, 2)],
    6: [(2, 4)],
    8: [],
    10: [(0, 9), (2, 6)],
    11: [(3, 5)],
}
G_READY = {
    0: [(2, 1), (1, 5), (2, 2), (3, 3)],
    8: [(1, 7)],
}
G_MERGE = [(3, 4), (1, 8)]
G_FFN = {
    2: [(2, 8)],
}
G_FFN_MIDDLE = {
    0: [(2, 7)],
    1: [(3, 6), (1, 9)],
    2: [(3, 7), (2, 9)],
    3: [(3, 8)],
    4: [(3, 9)],
}
R_FFN = {
}
R_FFN_MIDDLE = {
    1: [(1, 0)],
    2: [(1, 1)],
    3: [(1, 2)],
    4: [(2, 0), (2, 1), (1, 3)],
    5: [(1, 4)],
}
R_NORM = {
    1: [(3, 0), (2, 2), (1, 5)],
}
R_MERGE = []
R_HEADS = {
    1: [(2, 3)],
    2: [(3, 1)],
    3: [(2, 4)],
    5: [(1, 6)],
    6: [(2, 5), (3, 3)],
    7: [(3, 4), (1, 7)],
    8: [(2, 6)],
    9: [(1, 8), (3, 5)],
    11: [(2, 7), (3, 6)],
}
R_HEADS_END = {
    3: [(3, 2)],
}
R_TAIL = [[(2, 8), (4, 1), (3, 7), (1, 99), (1, 9), (4, 3)], [(3, 8), (2, 99)], [(3, 99), (2, 9), (4, 0), (4, 4), (4, 7), (3, 9), (4, 6), (4, 5), (4, 2), (4, 8)], [(4, 9)]]

def chosen(width, offset, start=0):
    source = lax.broadcasted_iota(jnp.int32, (LANES, D), 0)
    target = lax.broadcasted_iota(jnp.int32, (LANES, D), 1)
    mine = (source >= start) & (source < start + width)
    return jnp.where((target == source + (offset - start)) & mine, 1.0, 0.0).astype(bf16)


def vector_maps(place):
    per_row = D // (2 * HALF)
    return (
        chosen(2 * HALF, 2 * HALF * (place.index % per_row)),
        chosen(HALF, HALF * place.index),
        [chosen(SLICE, SLICE * place.chip, SLICE * n) for n in range(3)],
        place.index // per_row,
    )


def place_vectors(place, pieces_ref, out_ref):
    pieces = pieces_ref[...].astype(bf16)
    attend_map, single_map, expand_maps, half = vector_maps(place)
    attend = dot_nn(pieces, attend_map)
    single = dot_nn(pieces, single_map)
    expand = jnp.concatenate([dot_nn(pieces, m)[2:3] for m in expand_maps], axis=0)
    out_ref[...] = jnp.concatenate(
        [
            jnp.where(half == 0, attend[0:1], 0.0),
            jnp.where(half == 1, attend[0:1], 0.0),
            single[1:2],
            jnp.where(place.c == 0, expand, 0.0),
            jnp.where(place.c == 1, expand, 0.0),
            single[3:8],
            jnp.zeros((2, D), f32),
        ],
        axis=0,
    ).astype(bf16)


def own_vectors(place, sums):
    attend_map, single_map, expand_maps, half = vector_maps(place)
    high = sums.astype(bf16)
    rest = sums - high.astype(f32)
    middle = rest.astype(bf16)
    low = (rest - middle.astype(f32)).astype(bf16)
    parts = jnp.concatenate([high, middle, low], axis=0)

    def pick(chosen_map):
        found = dot_nt(parts, chosen_map)
        return found[:VEC_ROWS] + found[VEC_ROWS : 2 * VEC_ROWS] + found[2 * VEC_ROWS :]

    attend, single = pick(attend_map), pick(single_map)
    expand = 0.0
    for n, chosen_map in enumerate(expand_maps):
        found = pick(chosen_map)
        expand += jnp.where(place.c == 0, found[ROW_EXPAND + n], found[ROW_EXPAND + 3 + n])[None]
    return jnp.concatenate(
        [
            jnp.where(half == 0, attend[0:1], attend[1:2]),
            single[ROW_MERGE : ROW_MERGE + 1],
            expand,
            single[ROW_SHRINK : ROW_SHIFT + 2],
        ],
        axis=0,
    )


def lane_groups(read, write, moves):
    for target, sources in enumerate(moves):
        parts = []
        for group, (tile, at) in enumerate(sources):
            value = read(tile)
            shift = (group - at) * SLICE % LANES
            parts.append(pltpu.roll(value, shift, 1) if shift else value)
        lane = lax.broadcasted_iota(jnp.int32, parts[0].shape, 1) // SLICE
        write(target, jnp.where(lane < 2, jnp.where(lane == 0, parts[0], parts[1]), jnp.where(lane == 2, parts[2], parts[3])))


def ff_moves(inverse):
    outer, inner = (JOBS, CHIPS) if not inverse else (CHIPS, JOBS)
    units = [b * outer + a for a in range(outer) for b in range(inner)]
    return [[(u // 4, u % 4) for u in units[4 * t : 4 * t + 4]] for t in range(FF // LANES)]


def compose(place, pack_ref, twin_ref, source_cols):
    mine = pack_ref[:, source_cols].astype(f32)[:HALF]
    other = twin_ref[:, source_cols].astype(f32)[:HALF]
    first = jnp.where(place.c == 0, mine, other)
    second = jnp.where(place.c == 0, other, mine)
    return jnp.concatenate([first, second], axis=0).astype(bf16)


def layer_kernel(
    bucket, lengths, keeps, x_any, g_any, attend_any, merge_any, expand_any, shrink_any, pieces_any,
    out_any, ig_any, ga_any, gm_any, ge_any, gs_any, vec_out, active_any, slope_any,
    attend_ref, merge_ref, expand_ref, shrink_ref, pieces_ref, ge_own, wa, wm, we, ws, ga, pack, pack_twin, vec_parts, vec_land, vec,
    x, g, q, k, v, query_const, key_const, mixed, logsum, xhat, low, xt, lowt, active, slope, first,
    a0, a1, a2, a3, m0, m1, m2, m3, e0, e1, e2, e3, f1, f2, f3, s0, s1, s2, s3, fa, fm, fe, fs, gain, gain_land,
    g_send, g_recv, gt_send, gt_recv, r_send, r_recv, rt_send, rt_recv, own_send, own_recv, vec_send, vec_recv,
    sum_send, sum_recv, last_send, last_recv, local, flow,
):
    place = Place()
    c = place.c
    place.greet()
    shards = [
        pltpu.make_async_copy(source, target, local.at[4 + n])
        for n, (source, target) in enumerate(
            (
                (expand_any, expand_ref), (pieces_any, pieces_ref), (attend_any, attend_ref), (merge_any, merge_ref),
                (shrink_any, shrink_ref),
            )
        )
    ]
    x_copy = pltpu.make_async_copy(x_any, x, local.at[0])
    g_copy = pltpu.make_async_copy(g_any, g, local.at[1])
    for copy in shards + [x_copy, g_copy]:
        copy.start()
    token_tables(
        bucket[0], [lengths[0, b] for b in range(SLOTS)], [keeps[0, b] for b in range(SLOTS)],
        query_const, key_const, logsum,
    )
    for copy in shards:
        copy.wait()

    pack[0:HALF, 0 : 3 * D] = attend_ref[...]
    pack[0:HALF, 3 * D : 4 * D] = merge_ref[...]

    def put_expand(tile, value):
        pack[0:HALF, 4 * D + LANES * tile : 4 * D + LANES * (tile + 1)] = value.astype(bf16)

    lane_groups(
        lambda tile: expand_ref[:, LANES * tile : LANES * (tile + 1)].astype(f32), put_expand, ff_moves(False)
    )
    place_vectors(place, pieces_ref, vec_parts.at[0])
    x_copy.wait()
    xt[...] = x[...].T
    place.met()

    own_pack = remote(pack, pack_twin, own_send.at[0], own_recv.at[0], place.twin)
    own_pack.start()
    their_cols = pl.ds(aligned(384 * (1 - c), 128), 384)
    my_cols = pl.ds(aligned(384 * c, 128), 384)
    my_rows = pl.ds(aligned(FF_HALF * c, FF_HALF), FF_HALF)
    own_shrink = remote(
        shrink_ref.at[:, their_cols], ws.at[place.z, place.y, place.x, my_rows, their_cols],
        own_send.at[1], own_recv.at[1], place.twin,
    )

    class Sums:
        def __init__(self, source, land, sends, recvs, order):
            self.source, self.land, self.steps = source, land, []
            at = 0
            for step, peers in enumerate([(place.twin,)] + [tuple(p for _, p in place.over[a]) for a in order]):
                self.steps.append([])
                for peer in peers:
                    copy = remote(source.at[step], land.at[at], sends.at[at], recvs.at[at], peer)
                    self.steps[-1].append((copy, at))
                    at += 1

        def run(self, step):
            if step > 0:
                total = self.source[step - 1].astype(f32)
                for copy, at in self.steps[step - 1]:
                    copy.wait_recv()
                    total += self.land[at].astype(f32)
                if step == 4:
                    return total
                self.source[step] = total.astype(self.source.dtype)
            for copy, _ in self.steps[step]:
                copy.start()

        def finish(self):
            for copies in self.steps:
                for copy, _ in copies:
                    copy.wait_send()

    vec_sums = Sums(vec_parts, vec_land, vec_send, vec_recv, "zxy")
    grad_sums = Sums(gain, gain_land, sum_send, sum_recv, "xyz")

    vec_sums.run(0)
    own_shrink.start()

    def gathers(t):
        def one(ref, cuts, at):
            return Gather(place, ref, cuts, g_send.at[at], g_recv.at[at], gt_send.at[at], gt_recv.at[at])

        if t < 3:
            return [one(wa, attend_cuts(c, t), t)]
        if t == 3:
            return [one(wm, merge_cuts(c), 3)]
        j = t - 4
        return [one(we, expand_cuts(c, j), 4 + 2 * j), one(ws, shrink_cuts(c, j), 5 + 2 * j)]

    def gather_events(names):
        for step, t in names:
            if t == VECTORS:
                vec_sums.run(step)
                continue
            for one in gathers(t):
                one.run(step)

    def when(index, table, events):
        for value, names in table.items():

            @pl.when(index == value)
            def _():
                events(names)

    own_pack.wait_recv()
    for group in range(3):
        for n in range(3):
            cols = aligned(256 * group + 128 * c, 128)
            wa[place.z, place.y, place.x, n, :, pl.ds(cols, 128)] = compose(
                place, pack, pack_twin, pl.ds(aligned(D * n + cols, 128), 128)
            )
    wm[place.z, place.y, place.x, :, my_cols] = compose(
        place, pack, pack_twin, pl.ds(aligned(3 * D + 384 * c, 128), 384)
    )
    for j in range(JOBS):
        cols = aligned(PART * j + 256 * c, 128)
        we[place.z, place.y, place.x, :, pl.ds(cols, 256)] = compose(
            place, pack, pack_twin, pl.ds(aligned(4 * D + cols, 128), 256)
        )
    ws[place.z, place.y, place.x, my_rows, my_cols] = shrink_ref[:, my_cols]
    own_shrink.wait_recv()
    gather_events(G_START)
    vec[...] = vec_sums.run(4)

    def heads(i, carry):
        when(i, G_HEADS, gather_events)
        for group in range(3):

            @pl.when(i == 4 * group)
            def _():
                for one in gathers(group):
                    one.ready()

        @pl.when(i % 4 == 0)
        def _():
            cols = pl.ds(aligned(256 * (i // 4), 256), 256)
            tokens = x[...]
            part = dot_nn(tokens, wa[:, :, :, 0, :, cols].reshape(D, 256))
            q[:, cols] = ((part + vec[0:1, cols]) * 0.125).astype(bf16)
            k[:, cols] = dot_nn(tokens, wa[:, :, :, 1, :, cols].reshape(D, 256)).astype(bf16)
            part = dot_nn(tokens, wa[:, :, :, 2, :, cols].reshape(D, 256))
            v[:, cols] = (part + vec[1:2, cols]).astype(bf16)

        when(i, G_READY, gather_events)
        attend_forward(i, query_const, key_const, q, k, v, mixed, logsum, LONG)
        return carry

    lax.fori_loop(0, 12, heads, 0)
    gather_events(G_MERGE)
    for one in gathers(3):
        one.ready()
    tile = 512

    def merge_norm(i, carry):
        rows = pl.ds(aligned(i * tile, tile), tile)
        branch = dot_nn(mixed[rows, :], wm[...].reshape(D, D)) + vec[ROW_MERGE : ROW_MERGE + 1, :]
        x_hat, deviation = norm_parts(x[rows, :].astype(f32) + branch)
        xhat[rows, :] = x_hat.astype(bf16)
        logsum[rows, :] = jnp.where(lane_index(tile) == RSTD_LANE, deviation, logsum[rows, :])
        normed = x_hat * vec[ROW_GAIN : ROW_GAIN + 1, :] + vec[ROW_SHIFT : ROW_SHIFT + 1, :]
        low[rows, :] = normed.astype(bf16)
        first[rows, :] = normed + vec[ROW_SHRINK : ROW_SHRINK + 1, :]
        return carry

    lax.fori_loop(0, T // tile, merge_norm, 0)
    lowt[...] = low[...].T

    def out_copies(j):
        return (
            pltpu.make_async_copy(active.at[j % 2], active_any.at[j], flow.at[0, j % 2]),
            pltpu.make_async_copy(slope.at[j % 2], slope_any.at[j], flow.at[1, j % 2]),
        )

    def back_copies(j):
        return (
            pltpu.make_async_copy(active_any.at[j], active.at[j % 2], flow.at[0, j % 2]),
            pltpu.make_async_copy(slope_any.at[j], slope.at[j % 2], flow.at[1, j % 2]),
        )

    def expand_part(j, carry):
        when(j, G_FFN, gather_events)

        @pl.when(j >= 2)
        def _():
            for copy in out_copies(j - 2):
                copy.wait()

        for t in range(JOBS):

            @pl.when(j == t)
            def _():
                for one in gathers(4 + t):
                    one.ready()

        a_ref, s_ref = active.at[j % 2], slope.at[j % 2]
        for h in range(2):
            here = slice(256 * h, 256 * h + 256)
            cols = pl.ds(aligned(PART * j + 256 * h, 256), 256)
            bias = vec[pl.ds(ROW_EXPAND + j, 1), here]
            expanded = dot_nn(low[...], we[:, :, :, :, cols].reshape(D, 256)) + bias
            a, s = gelu_parts(expanded)
            a_ref[:, here] = a.astype(bf16)
            s_ref[:, here] = s.astype(bf16)
        when(j, G_FFN_MIDDLE, gather_events)
        rows = pl.ds(aligned(SLICE * j, SLICE), SLICE)
        first[...] += dot_nn(a_ref[...], ws[:, :, :, rows, :].reshape(PART, D))

        @pl.when(j < JOBS - 2)
        def _():
            for copy in out_copies(j):
                copy.start()

        return carry

    lax.fori_loop(0, JOBS, expand_part, 0)
    g_copy.wait()
    gain[0] = jnp.zeros((VEC_ROWS, D), f32)

    def end_of_forward(i, carry):
        rows = pl.ds(aligned(i * tile, tile), tile)
        x_hat, deviation = norm_parts(first[rows, :])
        weight = vec[ROW_GAIN + 1 : ROW_GAIN + 2, :]
        result = x_hat * weight + vec[ROW_SHIFT + 1 : ROW_SHIFT + 2, :]
        keep = column_of(logsum[rows, :], KEEP_LANE) > 0.0
        dy = jnp.where(keep, g[rows, :].astype(f32), 0.0)
        g[rows, :] = jnp.where(keep, result, x[rows, :].astype(f32)).astype(bf16)
        grad = norm_back(dy * weight, x_hat, deviation)
        first[rows, :] = grad
        branch = grad.astype(bf16)
        low[rows, :] = branch
        gain[0, ROW_GAIN + 1 : ROW_GAIN + 2, :] += jnp.sum(dy * x_hat, axis=0, keepdims=True)
        gain[0, ROW_SHIFT + 1 : ROW_SHIFT + 2, :] += jnp.sum(dy, axis=0, keepdims=True)
        gain[0, ROW_SHRINK : ROW_SHRINK + 1, :] += jnp.sum(branch.astype(f32), axis=0, keepdims=True)
        return carry

    lax.fori_loop(0, T // tile, end_of_forward, 0)
    out_copy = pltpu.make_async_copy(g, out_any, local.at[2])
    out_copy.start()

    def reductions(t):
        def one(ref, land0, lands, final, cuts, at, *args):
            sems = (r_send.at[at], r_recv.at[at], rt_send.at[at], rt_recv.at[at])
            return Reduce(place, ref, land0, lands, final, cuts(c, *args), cuts(1 - c, *args), sems)

        if t < JOBS:
            j = JOBS - 1 - t
            return [
                one(we, e0.at[t % 2], [[ref.at[t] for ref in (e1, e2, e3)], [ref.at[t] for ref in (f1, f2, f3)]], fe, expand_cuts, 2 * t, j),
                one(ws, s0.at[t % 2], [[ref.at[t] for ref in (s1, s2, s3)]], fs, shrink_cuts, 2 * t + 1, j),
            ]
        if t == JOBS:
            return [one(wm, m0, [[m1, m2, m3]], fm, merge_cuts, 2 * JOBS)]
        n = t - JOBS - 1
        return [one(ga, a0.at[n % 2], [[ref.at[n] for ref in (a1, a2, a3)]], fa, attend_cuts, 2 * JOBS + 1 + n, n)]

    def reduce_events(names):
        for step, t in names:
            if t == VECTORS:
                grad_sums.run(step)
                continue
            for one in reductions(t):
                one.run(step)

    def expand_back(b, carry):
        j = JOBS - 1 - b

        @pl.when(b >= 2)
        def _():
            for copy in back_copies(j):
                copy.wait()

        when(b, R_FFN, reduce_events)
        a_ref, s_ref = active.at[j % 2], slope.at[j % 2]
        rows = pl.ds(aligned(SLICE * j, SLICE), SLICE)
        cols = pl.ds(aligned(PART * j, PART), PART)
        s_in = low[...]
        for h in range(2):
            here = slice(256 * h, 256 * h + 256)
            e_in = dot_nt(s_in, ws[2 * h : 2 * h + 2, :, :, rows, :].reshape(256, D)) * s_ref[:, here].astype(f32)
            e_in = e_in.astype(bf16)
            s_ref[:, here] = e_in
            gain[0, pl.ds(ROW_EXPAND + j, 1), here] = jnp.sum(e_in.astype(f32), axis=0, keepdims=True)
        when(b, R_FFN_MIDDLE, reduce_events)
        for h in range(2):
            grad = dot_tn(a_ref[:, 256 * h : 256 * h + 256], s_in).astype(bf16)
            ws[2 * h : 2 * h + 2, :, :, rows, :] = grad.reshape(2, Y, X, SLICE, D)
        first[...] += dot_nt(s_ref[...], we[:, :, :, :, cols].reshape(D, PART))
        for h in range(2):
            here = pl.ds(aligned(PART * j + 256 * h, 256), 256)
            grad = dot_nn(lowt[...], s_ref[:, 256 * h : 256 * h + 256]).astype(bf16)
            we[:, :, :, :, here] = grad.reshape(Z, Y, X, BLOCK, 256)
        when(b, {t: [(0, t)] for t in range(JOBS)}, reduce_events)

        @pl.when(b < JOBS - 2)
        def _():
            for copy in back_copies(j - 2):
                copy.start()

        return carry

    for t in range(4 + JOBS):
        for one in gathers(t):
            one.finish()
    lax.fori_loop(0, JOBS, expand_back, 0)

    def middle(i, carry):
        when(i, R_NORM, reduce_events)
        rows = pl.ds(aligned(i * tile, tile), tile)
        dy, x_hat = first[rows, :], xhat[rows, :].astype(f32)
        deviation = column_of(logsum[rows, :], RSTD_LANE)
        grad = norm_back(dy * vec[ROW_GAIN : ROW_GAIN + 1, :], x_hat, deviation)
        first[rows, :] = grad
        branch = grad.astype(bf16)
        low[rows, :] = branch
        gain[0, ROW_GAIN : ROW_GAIN + 1, :] += jnp.sum(dy * x_hat, axis=0, keepdims=True)
        gain[0, ROW_SHIFT : ROW_SHIFT + 1, :] += jnp.sum(dy, axis=0, keepdims=True)
        gain[0, ROW_MERGE : ROW_MERGE + 1, :] += jnp.sum(branch.astype(f32), axis=0, keepdims=True)
        x[rows, :] = dot_nt(branch, wm[...].reshape(D, D)).astype(bf16)
        return carry

    lax.fori_loop(0, T // tile, middle, 0)
    out_copy.wait()
    g_again = pltpu.make_async_copy(g_any, g, local.at[1])
    g_again.start()
    reduce_events(R_MERGE)
    wm[...] = dot_tn(mixed[...], low[...]).astype(bf16).reshape(Z, Y, X, BLOCK, D)
    reduce_events([(0, JOBS)])

    def heads_back(i, carry):
        when(i, R_HEADS, reduce_events)
        attend_backward(i, query_const, key_const, q, k, v, mixed, logsum, x, q, k, v, LONG)

        when(i, R_HEADS_END, reduce_events)

        @pl.when(i % 4 == 3)
        def _():
            cols = pl.ds(aligned(256 * (i // 4), 256), 256)
            for n, grads in enumerate((q, k, v)):
                grad = dot_nn(xt[...], grads[:, cols]).astype(bf16)
                ga[:, :, :, n, :, cols] = grad.reshape(Z, Y, X, BLOCK, 256)
                if n != 1:
                    gain[0, n // 2 : n // 2 + 1, cols] = jnp.sum(grads[:, cols].astype(f32), axis=0, keepdims=True)

        when(i, {4 * n + 3: [(0, JOBS + 1 + n)] for n in range(3)}, reduce_events)
        return carry

    lax.fori_loop(0, 12, heads_back, 0)
    grad_sums.run(0)

    def last_copy(ref, n, cols, height):
        rows = pl.ds(aligned(height * (1 - c), 8), height)
        here = ref.at[:, rows, cols] if len(ref.shape) == 3 else ref.at[rows, cols]
        return remote(here, here, last_send.at[n], last_recv.at[n], place.twin)

    early_last = [last_copy(fm, 0, my_cols, HALF), last_copy(fs, 1, my_cols, FF_HALF)]
    early_last += [last_copy(fe, 2 + j, expand_cuts(c, j)[0].cols, HALF) for j in range(JOBS)]
    attend_last = [last_copy(fa, 2 + JOBS + n, attend_cuts(c, n)[0].cols, HALF) for n in range(3)]

    reduce_events(R_TAIL[0])
    g_again.wait()

    def inputs_part(i, carry):
        @pl.when(i == 1)
        def _():
            reduce_events(R_TAIL[1])

        rows = pl.ds(aligned(i * tile, tile), tile)
        keep = column_of(logsum[rows, :], KEEP_LANE) > 0.0
        total = first[rows, :] + jnp.where(keep, 0.0, g[rows, :].astype(f32))
        for n, grads in enumerate((q, k, v)):
            total += dot_nt(grads[rows, :], wa[:, :, :, n, :, :].reshape(D, D))
        first[rows, :] = total
        return carry

    lax.fori_loop(0, T // tile, inputs_part, 0)
    out_ig = pltpu.make_async_copy(first, ig_any, local.at[3])
    out_ig.start()
    reduce_events(R_TAIL[2])
    for copy in early_last + attend_last[:2]:
        copy.start()
    mine, ff_mine = pl.ds(aligned(HALF * c, 8), HALF), pl.ds(aligned(FF_HALF * c, 8), FF_HALF)
    for copy in early_last:
        copy.wait_recv()
    done = [
        pltpu.make_async_copy(fm.at[mine], gm_any, local.at[4]),
        pltpu.make_async_copy(fs.at[ff_mine], gs_any, local.at[5]),
        pltpu.make_async_copy(ge_own, ge_any, local.at[6]),
    ]
    done[0].start()
    done[1].start()

    def put_grad(tile, value):
        ge_own[:, LANES * tile : LANES * (tile + 1)] = value

    lane_groups(lambda tile: fe[mine, LANES * tile : LANES * (tile + 1)], put_grad, ff_moves(True))
    done[2].start()
    own_pack.wait_send()
    own_shrink.wait_send()
    for copy in early_last:
        copy.wait_send()
    vec_sums.finish()
    for t in range(JOBS + 3):
        for one in reductions(t):
            one.finish()
    for copy in attend_last[:2]:
        copy.wait_recv()
        copy.wait_send()
    vec_out[...] = own_vectors(place, grad_sums.run(4))
    grad_sums.finish()
    reduce_events(R_TAIL[3])
    attend_last[2].start()
    for one in reductions(JOBS + 3):
        one.finish()
    attend_last[2].wait_recv()
    done += [
        pltpu.make_async_copy(fa.at[n, mine], ga_any.at[:, pl.ds(D * n, D)], local.at[7 + n]) for n in range(3)
    ]
    for copy in done[3:]:
        copy.start()
    attend_last[2].wait_send()
    for copy in done + [out_ig]:
        copy.wait()


ANY = pl.BlockSpec(memory_space=pl.ANY)
VM = pl.BlockSpec(memory_space=pltpu.VMEM)
SM = pl.BlockSpec(memory_space=pltpu.SMEM)


def layer_call(buckets, lengths, keeps, inputs, upstream, attend, merge, expand, shrink, pieces):
    dma = pltpu.SemaphoreType.DMA

    def landing(rows, cols, jobs=None, deep=(), slots=None, parts=1):
        lead = (jobs,) if jobs else ()
        stages = [(Z, 2), (Z,), (3,), (Z, 2), (3, 2), (1,)][: 3 * parts]
        return [pltpu.VMEM(((slots,) if slots else lead) + (Z, Y, X) + deep + (rows, cols), bf16)] + [
            pltpu.VMEM(lead + d + deep + (rows, cols // parts), bf16) for d in stages
        ]

    tokens = [pltpu.VMEM((T, D), bf16) for _ in range(5)]
    scratch = (
        [pltpu.VMEM(a.shape, a.dtype) for a in (attend, merge, expand, shrink, pieces)]
        + [pltpu.VMEM((HALF, FF), f32)]
        + [pltpu.VMEM(*s) for s in WEIGHTS]
        + [
            pltpu.VMEM(*WEIGHTS[0]),
            pltpu.VMEM((32, PACK), bf16),
            pltpu.VMEM((32, PACK), bf16),
            pltpu.VMEM((4, VEC_ROWS, D), bf16),
            pltpu.VMEM((6, VEC_ROWS, D), bf16),
            pltpu.VMEM((VEC_ROWS, D), f32),
        ]
        + tokens
        + [
            pltpu.VMEM((T, LANES), bf16),
            pltpu.VMEM((T, LANES), bf16),
            pltpu.VMEM((T, D), bf16),
            pltpu.VMEM((T, LANES), f32),
            pltpu.VMEM((T, D), bf16),
            pltpu.VMEM((T, D), bf16),
            pltpu.VMEM((D, T), bf16),
            pltpu.VMEM((D, T), bf16),
            pltpu.VMEM((2, T, PART), bf16),
            pltpu.VMEM((2, T, PART), bf16),
            pltpu.VMEM((T, D), f32),
        ]
        + landing(BLOCK, 128, 3, (3,), slots=2)
        + landing(BLOCK, 384)
        + landing(BLOCK, 256, JOBS, slots=2, parts=2)
        + landing(SLICE, 384, JOBS, slots=2)
        + [
            pltpu.VMEM((3, BLOCK, D), f32),
            pltpu.VMEM((BLOCK, D), f32),
            pltpu.VMEM((BLOCK, FF), f32),
            pltpu.VMEM((FF_BLOCK, D), f32),
            pltpu.VMEM((4, VEC_ROWS, D), f32),
            pltpu.VMEM((6, VEC_ROWS, D), f32),
        ]
        + 2 * [dma((GATHERS, 2, 5)), dma((GATHERS, 2, 5)), dma((GATHERS,)), dma((GATHERS,))]
        + 2 * [dma((2,))]
        + 4 * [dma((6,))]
        + 2 * [dma((5 + JOBS,))]
        + [dma((10,)), dma((2, 2))]
    )
    return pl.pallas_call(
        layer_kernel,
        out_shape=tuple(
            jax.ShapeDtypeStruct(*s)
            for s in (
                ((T, D), bf16), ((T, D), f32), ((HALF, 3 * D), f32), ((HALF, D), f32), ((HALF, FF), f32),
                ((FF_HALF, D), f32), ((PIECES, LANES), f32), ((JOBS, T, PART), bf16), ((JOBS, T, PART), bf16),
            )
        ),
        in_specs=[SM] * 3 + [ANY] * 7,
        out_specs=[ANY] * 6 + [VM] + [ANY] * 2,
        scratch_shapes=scratch,
        compiler_params=pltpu.CompilerParams(collective_id=0, has_side_effects=True, vmem_limit_bytes=VMEM_LIMIT),
        cost_estimate=pl.CostEstimate(flops=60_000_000_000, bytes_accessed=60_000_000, transcendentals=20_000_000),
    )(buckets, lengths, keeps, inputs, upstream, attend, merge, expand, shrink, pieces)


def pack_pieces(attend_bias, merge_bias, expand_bias, shrink_bias, gain, shift):
    total = 0.0
    vectors = (attend_bias[None], merge_bias[None], expand_bias[None], shrink_bias[None], gain, shift)
    row = 0
    for piece in vectors:
        count, width = piece.shape
        total += jnp.pad(piece.astype(f32), ((row, PIECES - row - count), (0, LANES - width)))
        row += count
    return total


def finish_kernel(*refs):
    count = len(RESULTS)
    sources, own, wide, vectors = refs[:count], refs[count], refs[count + 1 : 2 * count + 1], refs[2 * count + 1 : -count - 2]
    held, arrive, leave = refs[-count - 2 : -2], refs[-2], refs[-1]
    steps = [
        (pltpu.make_async_copy(s, h, arrive.at[n]), pltpu.make_async_copy(h, w, leave.at[n]))
        for n, (s, h, w) in enumerate(zip(sources, held, wide))
    ]
    for into, _ in steps:
        into.start()
    row = 0
    for ref in vectors:
        if len(ref.shape) == 1:
            ref[...] = own[row, : ref.shape[0]]
            row += 1
        else:
            ref[...] = own[row : row + ref.shape[0], : ref.shape[1]]
            row += ref.shape[0]
    for into, out in steps:
        into.wait()
        out.start()
    for _, out in steps:
        out.wait()


RESULTS = (
    ((T, D), f32), ((T, D), bf16), ((HALF, 3 * D), f32), ((HALF, D), f32), ((HALF, FF), f32), ((FF_HALF, D), f32),
)


def finish_call(wide, own, vectors):
    dma = pltpu.SemaphoreType.DMA
    return pl.pallas_call(
        finish_kernel,
        out_shape=tuple(jax.ShapeDtypeStruct(*s) for s in RESULTS)
        + tuple(jax.ShapeDtypeStruct(v.shape, f32) for v in vectors),
        in_specs=[ANY] * len(RESULTS) + [VM],
        out_specs=[ANY] * len(RESULTS) + [VM] * len(vectors),
        scratch_shapes=[pltpu.VMEM(*s) for s in RESULTS] + 2 * [dma((len(RESULTS),))],
        compiler_params=pltpu.CompilerParams(vmem_limit_bytes=VMEM_LIMIT),
    )(*wide, own)

def layer_norm(hidden, gains, shifts):
    center = hidden - jnp.mean(hidden, axis=-1, keepdims=True)
    spread = jnp.mean(center * center, axis=-1, keepdims=True)
    return center * lax.rsqrt(spread + epsilon) * gains + shifts


def gelu_exact(values):
    return jax.nn.gelu(values, approximate=False)


def matmul(left, right):
    return jnp.dot(left, right, preferred_element_type=jnp.float32)


def token_info(bucket, slot_lengths, slot_keeps):
    position = jnp.arange(TOK_DEV, dtype=jnp.int32)
    span_size = jnp.where(bucket > 0, LONG, SHORT).astype(jnp.int32)
    sequence = position // span_size
    within = position - sequence * span_size
    slot_index = sequence * (span_size // SHORT)
    matches = (slot_index[:, None] == jnp.arange(SLOTS, dtype=jnp.int32)[None, :]).astype(jnp.int32)
    length = jnp.sum(matches * slot_lengths[None, :], axis=1) + bucket * (LONG - SHORT)
    keep_flags = jnp.sum(matches * slot_keeps[None, :], axis=1)
    return (sequence, within < length, keep_flags > 0)


def masked_scores(queries, key_rows, sequence, valid_key):
    scores = jnp.einsum("qhd,khd->hqk", queries, key_rows, preferred_element_type=jnp.float32)
    allowed = (sequence[:, None] == sequence[None, :]) & valid_key[None, :]
    return jnp.where(allowed[None], scores, masked_score)


def attend_block(pieces):
    queries, key_rows, values, sequence, valid_key = pieces
    scores = masked_scores(queries, key_rows, sequence, valid_key)
    highest = jnp.max(scores, axis=-1, keepdims=True)
    raised = jnp.exp(scores - highest)
    row_total = jnp.sum(raised, axis=-1, keepdims=True)
    weights = raised / row_total
    mixed_rows = jnp.einsum(
        "hqk,khd->qhd", weights.astype(jnp.bfloat16), values, preferred_element_type=jnp.float32
    )
    return (mixed_rows, highest[:, :, 0] + jnp.log(row_total[:, :, 0]))


def attend_back(pieces):
    queries, key_rows, values, sequence, valid_key, logsum, mixed_grad = pieces
    scores = masked_scores(queries, key_rows, sequence, valid_key)
    weights = jnp.exp(scores - logsum[:, :, None])
    weight_grad = jnp.einsum("qhd,khd->hqk", mixed_grad, values, preferred_element_type=jnp.float32)
    row_dot = jnp.sum(weights * weight_grad, axis=-1, keepdims=True)
    score_grad = (weights * (weight_grad - row_dot)).astype(jnp.bfloat16)
    query_part = jnp.einsum(
        "hqk,khd->qhd", score_grad, key_rows, preferred_element_type=jnp.float32
    ).astype(jnp.bfloat16)
    key_part = jnp.einsum(
        "hqk,qhd->khd", score_grad, queries, preferred_element_type=jnp.float32
    ).astype(jnp.bfloat16)
    value_part = jnp.einsum(
        "hqk,qhd->khd", weights.astype(jnp.bfloat16), mixed_grad, preferred_element_type=jnp.float32
    ).astype(jnp.bfloat16)
    return (query_part, key_part, value_part)


def heads_view(source):
    return source.reshape(source.shape[0] // LONG, LONG, HEADS, HD)


def forward_pass(inputs, weights, sequence, valid_key, keep_flags):
    (
        attend_matrix,
        attend_offset,
        merge_matrix,
        merge_offset,
        expand_matrix,
        expand_offset,
        shrink_matrix,
        shrink_offset,
        gains,
        shifts,
    ) = weights
    model_width = inputs.shape[1]
    blocks = inputs.shape[0] // LONG
    packed = matmul(inputs, attend_matrix)
    offset = attend_offset.astype(jnp.float32)
    queries = ((packed[:, :model_width] + offset[:model_width]) * 0.125).astype(jnp.bfloat16)
    key_rows = packed[:, model_width : 2 * model_width].astype(jnp.bfloat16)
    values = (packed[:, 2 * model_width :] + offset[model_width:]).astype(jnp.bfloat16)
    mixed_rows, logsum = lax.map(
        attend_block,
        (
            heads_view(queries),
            heads_view(key_rows),
            heads_view(values),
            sequence.reshape(blocks, LONG),
            valid_key.reshape(blocks, LONG),
        ),
    )
    mixed_rows = mixed_rows.reshape(-1, model_width).astype(jnp.bfloat16)
    tokens = inputs.astype(jnp.float32)
    first_sum = tokens + matmul(mixed_rows, merge_matrix) + merge_offset.astype(jnp.float32)
    normed = layer_norm(first_sum, gains[0].astype(jnp.float32), shifts[0].astype(jnp.float32))
    normed_low = normed.astype(jnp.bfloat16)
    expanded = matmul(normed_low, expand_matrix) + expand_offset.astype(jnp.float32)
    active = gelu_exact(expanded).astype(jnp.bfloat16)
    second_sum = normed + matmul(active, shrink_matrix) + shrink_offset.astype(jnp.float32)
    result = layer_norm(second_sum, gains[1].astype(jnp.float32), shifts[1].astype(jnp.float32))
    outputs = jnp.where(keep_flags[:, None], result, tokens).astype(jnp.bfloat16)
    return (
        outputs,
        (
            queries,
            key_rows,
            values,
            logsum,
            mixed_rows,
            first_sum,
            normed_low,
            expanded,
            active,
            second_sum,
        ),
    )


def backward_pass(inputs, upstream, weights, saved, sequence, valid_key, keep_flags):
    (
        attend_matrix,
        attend_offset,
        merge_matrix,
        merge_offset,
        expand_matrix,
        expand_offset,
        shrink_matrix,
        shrink_offset,
        gains,
        shifts,
    ) = weights
    (
        queries,
        key_rows,
        values,
        logsum,
        mixed_rows,
        first_sum,
        normed_low,
        expanded,
        active,
        second_sum,
    ) = saved
    model_width = inputs.shape[1]
    blocks = inputs.shape[0] // LONG
    cotangent = upstream.astype(jnp.float32)
    result_grad = jnp.where(keep_flags[:, None], cotangent, 0.0)
    second_out, pull_second = jax.vjp(
        layer_norm, second_sum, gains[1].astype(jnp.float32), shifts[1].astype(jnp.float32)
    )
    second_grad, gain_two, shift_two = pull_second(result_grad)
    shrink_in = second_grad.astype(jnp.bfloat16)
    shrink_grad = jnp.einsum("tf,td->fd", active, shrink_in, preferred_element_type=jnp.float32)
    shrink_offset_grad = jnp.sum(shrink_in.astype(jnp.float32), axis=0)
    active_grad = jnp.einsum(
        "td,fd->tf", shrink_in, shrink_matrix, preferred_element_type=jnp.float32
    )
    gelu_out, pull_gelu = jax.vjp(gelu_exact, expanded)
    expand_in = pull_gelu(active_grad)[0].astype(jnp.bfloat16)
    expand_grad = jnp.einsum("td,tf->df", normed_low, expand_in, preferred_element_type=jnp.float32)
    expand_offset_grad = jnp.sum(expand_in.astype(jnp.float32), axis=0)
    normed_grad = second_grad + jnp.einsum(
        "tf,df->td", expand_in, expand_matrix, preferred_element_type=jnp.float32
    )
    first_out, pull_first = jax.vjp(
        layer_norm, first_sum, gains[0].astype(jnp.float32), shifts[0].astype(jnp.float32)
    )
    first_grad, gain_one, shift_one = pull_first(normed_grad)
    branch_in = first_grad.astype(jnp.bfloat16)
    merge_grad = jnp.einsum("td,te->de", mixed_rows, branch_in, preferred_element_type=jnp.float32)
    merge_offset_grad = jnp.sum(branch_in.astype(jnp.float32), axis=0)
    mixed_grad = jnp.einsum(
        "te,de->td", branch_in, merge_matrix, preferred_element_type=jnp.float32
    ).astype(jnp.bfloat16)
    query_part, key_part, value_part = lax.map(
        attend_back,
        (
            heads_view(queries),
            heads_view(key_rows),
            heads_view(values),
            sequence.reshape(blocks, LONG),
            valid_key.reshape(blocks, LONG),
            logsum,
            heads_view(mixed_grad),
        ),
    )
    query_grad = query_part.reshape(-1, model_width) * 0.125
    packed_grad = jnp.concatenate(
        [query_grad, key_part.reshape(-1, model_width), value_part.reshape(-1, model_width)], axis=1
    )
    attend_grad = jnp.einsum("td,te->de", inputs, packed_grad, preferred_element_type=jnp.float32)
    attend_offset_grad = jnp.concatenate(
        [
            jnp.sum(query_grad.astype(jnp.float32), axis=0),
            jnp.sum(value_part.reshape(-1, model_width).astype(jnp.float32), axis=0),
        ]
    )
    input_grad = (
        first_grad
        + jnp.einsum("te,de->td", packed_grad, attend_matrix, preferred_element_type=jnp.float32)
        + jnp.where(keep_flags[:, None], 0.0, cotangent)
    )
    gain_grad = jnp.stack([gain_one, gain_two])
    shift_grad = jnp.stack([shift_one, shift_two])
    grads = (
        attend_grad,
        attend_offset_grad,
        merge_grad,
        merge_offset_grad,
        expand_grad,
        expand_offset_grad,
        shrink_grad,
        shrink_offset_grad,
        gain_grad,
        shift_grad,
    )
    return (grads, input_grad)


def general_device(
    inputs,
    upstream,
    buckets,
    lengths,
    layer_keep,
    attend_weight,
    attend_bias,
    merge_weight,
    merge_bias,
    expand_weight,
    expand_bias,
    shrink_weight,
    shrink_bias,
    norm_gain,
    norm_shift,
):
    sequence, valid_key, keep_flags = token_info(buckets[0], lengths[0], layer_keep[0])
    gathered = (
        lax.all_gather(attend_weight, ("group", "inner"), axis=0, tiled=True),
        lax.all_gather(attend_bias, ("group", "inner"), axis=0, tiled=True),
        lax.all_gather(merge_weight, ("group", "inner"), axis=0, tiled=True),
        lax.all_gather(merge_bias, ("group", "inner"), axis=0, tiled=True),
        lax.all_gather(expand_weight, ("group", "inner"), axis=0, tiled=True),
        lax.all_gather(expand_bias, ("group", "inner"), axis=0, tiled=True),
        lax.all_gather(shrink_weight, ("group", "inner"), axis=0, tiled=True),
        lax.all_gather(shrink_bias, ("group", "inner"), axis=0, tiled=True),
        lax.all_gather(norm_gain, ("group", "inner"), axis=1, tiled=True),
        lax.all_gather(norm_shift, ("group", "inner"), axis=1, tiled=True),
    )
    outputs, saved = forward_pass(inputs, gathered, sequence, valid_key, keep_flags)
    gathered = (
        lax.all_gather(attend_weight, ("group", "inner"), axis=0, tiled=True),
        lax.all_gather(attend_bias, ("group", "inner"), axis=0, tiled=True),
        lax.all_gather(merge_weight, ("group", "inner"), axis=0, tiled=True),
        lax.all_gather(merge_bias, ("group", "inner"), axis=0, tiled=True),
        lax.all_gather(expand_weight, ("group", "inner"), axis=0, tiled=True),
        lax.all_gather(expand_bias, ("group", "inner"), axis=0, tiled=True),
        lax.all_gather(shrink_weight, ("group", "inner"), axis=0, tiled=True),
        lax.all_gather(shrink_bias, ("group", "inner"), axis=0, tiled=True),
        lax.all_gather(norm_gain, ("group", "inner"), axis=1, tiled=True),
        lax.all_gather(norm_shift, ("group", "inner"), axis=1, tiled=True),
    )
    grads, input_grad = backward_pass(
        inputs, upstream, gathered, saved, sequence, valid_key, keep_flags
    )
    shares = (
        lax.psum_scatter(grads[0], ("group", "inner"), scatter_dimension=0, tiled=True),
        lax.psum_scatter(grads[1], ("group", "inner"), scatter_dimension=0, tiled=True),
        lax.psum_scatter(grads[2], ("group", "inner"), scatter_dimension=0, tiled=True),
        lax.psum_scatter(grads[3], ("group", "inner"), scatter_dimension=0, tiled=True),
        lax.psum_scatter(grads[4], ("group", "inner"), scatter_dimension=0, tiled=True),
        lax.psum_scatter(grads[5], ("group", "inner"), scatter_dimension=0, tiled=True),
        lax.psum_scatter(grads[6], ("group", "inner"), scatter_dimension=0, tiled=True),
        lax.psum_scatter(grads[7], ("group", "inner"), scatter_dimension=0, tiled=True),
        lax.psum_scatter(grads[8], ("group", "inner"), scatter_dimension=1, tiled=True),
        lax.psum_scatter(grads[9], ("group", "inner"), scatter_dimension=1, tiled=True),
    )
    return (
        outputs,
        input_grad,
        shares[0],
        shares[1],
        shares[2],
        shares[3],
        shares[4],
        shares[5],
        shares[6],
        shares[7],
        shares[8],
        shares[9],
    )

def slice_device(
    inputs, upstream, buckets, lengths, layer_keep, attend_weight, attend_bias, merge_weight, merge_bias,
    expand_weight, expand_bias, shrink_weight, shrink_bias, norm_gain, norm_shift,
):
    pieces = pack_pieces(attend_bias, merge_bias, expand_bias, shrink_bias, norm_gain, norm_shift)
    outputs, input_grad, attend, merge, expand, shrink, own = layer_call(
        buckets, lengths, layer_keep, inputs, upstream, attend_weight, merge_weight, expand_weight, shrink_weight, pieces
    )[:7]
    input_grad, outputs, attend, merge, expand, shrink, attend_b, merge_b, expand_b, shrink_b, gain, shift = finish_call(
        (input_grad, outputs, attend, merge, expand, shrink),
        own,
        (attend_bias, merge_bias, expand_bias, shrink_bias, norm_gain, norm_shift),
    )
    return (
        outputs, input_grad, attend, attend_b, merge, merge_b, expand, expand_b, shrink, shrink_b, gain, shift,
    )

def solution(mesh):
    on_slice = mesh.shape["group"] == Z * Y and mesh.shape["inner"] == 2 * X
    placed = (
        P(("group", "inner"), None),
        P(("group", "inner"), None),
        P(("group", "inner")),
        P(("group", "inner"), None),
        P(("group", "inner"), None),
        P(("group", "inner"), None),
        P(("group", "inner")),
        P(("group", "inner"), None),
        P(("group", "inner")),
        P(("group", "inner"), None),
        P(("group", "inner")),
        P(("group", "inner"), None),
        P(("group", "inner")),
        P(None, ("group", "inner")),
        P(None, ("group", "inner")),
    )
    return jax.shard_map(
        slice_device if on_slice else general_device,
        mesh=mesh,
        in_specs=placed,
        out_specs=(
            P(("group", "inner"), None),
            P(("group", "inner"), None),
            P(("group", "inner"), None),
            P(("group", "inner")),
            P(("group", "inner"), None),
            P(("group", "inner")),
            P(("group", "inner"), None),
            P(("group", "inner")),
            P(("group", "inner"), None),
            P(("group", "inner")),
            P(None, ("group", "inner")),
            P(None, ("group", "inner")),
        ),
        check_vma=False,
    )
```

```python
import jax
import jax.numpy as jnp
from jax import lax
from jax.experimental import pallas as pl
from jax.experimental.pallas import tpu as pltpu
from jax.sharding import PartitionSpec as P

HEADS = 12
HD = 64
LONG = 512
SHORT = 128
TOK_DEV = 1024
SLOTS = 8
D = 768
FF = 3072
LANES = 128
RSTD_LANE, KEEP_LANE = 12, 13
epsilon = 1e-05
masked_score = -1e30
f32 = jnp.float32
bf16 = jnp.bfloat16


def dot_nn(a, b):
    return lax.dot_general(a, b, (((1,), (0,)), ((), ())), preferred_element_type=f32)


def dot_nt(a, b):
    return lax.dot_general(a, b, (((1,), (1,)), ((), ())), preferred_element_type=f32)


def dot_tn(a, b):
    return lax.dot_general(a, b, (((0,), (0,)), ((), ())), preferred_element_type=f32)


def lane_index(rows):
    return lax.broadcasted_iota(jnp.int32, (rows, LANES), 1)


def token_tables(bucket, lengths, keeps, query_const, key_const, columns):
    shape = (TOK_DEV, LANES)
    position = lax.broadcasted_iota(jnp.int32, shape, 0)
    is_long = jnp.broadcast_to(bucket, shape) > 0
    slot = jnp.where(is_long, (position >> 9) << 2, position >> 7)
    offset = jnp.where(is_long, position & (LONG - 1), position & (SHORT - 1))
    length = jnp.zeros(shape, jnp.int32)
    keep = jnp.zeros(shape, jnp.int32)
    for b in range(SLOTS):
        here = slot == b
        length = jnp.where(here, lengths[b], length)
        keep = jnp.where(here, keeps[b], keep)
    length = length + bucket * (LONG - SHORT)
    valid = offset < length
    within = jnp.where(is_long, 0, (position >> 7) & 3)
    lane = lax.broadcasted_iota(jnp.int32, shape, 1) & (HD - 1)
    is_span = (lane >= 4) & (lane < 8)
    same = lane - 4 == within
    zero, one = jnp.zeros(shape, f32), jnp.ones(shape, f32)
    query_const[...] = jnp.where(lane == 3, one, jnp.where(is_span & ~same, one, zero)).astype(bf16)
    key_const[...] = jnp.where(
        lane < 3,
        one,
        jnp.where(((lane == 3) & ~valid) | (is_span & same), masked_score * one, zero),
    ).astype(bf16)
    columns[...] = jnp.where((lane_index(TOK_DEV) == KEEP_LANE) & (keep > 0), one, zero)


def column_of(columns, lane):
    return jnp.sum(jnp.where(lane_index(columns.shape[0]) == lane, columns, 0.0), axis=1, keepdims=True)


def three_parts(column, rows):
    wide = jnp.broadcast_to(column, (rows, LANES))
    high = wide.astype(bf16)
    rest = wide - high.astype(f32)
    middle = rest.astype(bf16)
    low = (rest - middle.astype(f32)).astype(bf16)
    return high, middle, low


def attend_forward(index, query_const, key_const, q_ref, k_ref, v_ref, mixed_ref, logsum_ref, tile):
    pair, block = index // 2, index % 2
    cols = pl.ds(pl.multiple_of(pair * LANES, LANES), LANES)
    rows = pl.ds(pl.multiple_of(block * LONG, LONG), LONG)
    lane_k = lane_index(LONG)
    k2, v2 = k_ref[rows, cols], v_ref[rows, cols]
    kc = key_const[rows, :]
    k_aug = [jnp.where((lane_k // HD) == half, k2, kc) for half in range(2)]
    lane_q = lane_index(tile)
    for t in range(LONG // tile):
        qrows = pl.ds(pl.multiple_of(block * LONG + t * tile, tile), tile)
        q2, qc = q_ref[qrows, cols], query_const[qrows, :]
        outs = []
        sums = logsum_ref[qrows, :]
        for half in range(2):
            q_aug = jnp.where((lane_q // HD) == half, q2, qc)
            scores = dot_nt(q_aug, k_aug[half])
            highest = jnp.max(scores, axis=1, keepdims=True)
            raised = jnp.exp(scores - highest)
            total = jnp.sum(raised, axis=1, keepdims=True)
            out = dot_nn(raised.astype(bf16), v2)
            outs.append(out * (1.0 / total))
            sums = jnp.where(lane_q == 2 * pair + half, highest + jnp.log(total), sums)
        logsum_ref[qrows, :] = sums
        mixed_ref[qrows, cols] = jnp.where(lane_q < HD, outs[0], outs[1]).astype(bf16)


def attend_backward(index, query_const, key_const, q_ref, k_ref, v_ref, mixed_ref, logsum_ref, mixed_grad_ref,
                    dq_ref, dk_ref, dv_ref, tile):
    pair, block = index // 2, index % 2
    cols = pl.ds(pl.multiple_of(pair * LANES, LANES), LANES)
    rows = pl.ds(pl.multiple_of(block * LONG, LONG), LONG)
    lane = lane_index(LONG)
    q2, dm2 = q_ref[rows, cols], mixed_grad_ref[rows, cols]
    product = dm2.astype(f32) * mixed_ref[rows, cols].astype(f32)
    sums = logsum_ref[rows, :]
    qc = query_const[rows, :]
    zero = jnp.zeros((LONG, LANES), bf16)
    q_aug, d_aug = [], []
    for half in range(2):
        mine = (lane // HD) == half
        at = lane & (HD - 1)
        logsum = jnp.sum(jnp.where(lane == 2 * pair + half, sums, 0.0), axis=1, keepdims=True)
        delta = jnp.sum(jnp.where(mine, product, 0.0), axis=1, keepdims=True)
        lh, lm, ll = three_parts(-logsum, LONG)
        dh, dm, dl = three_parts(-delta, LONG)
        extra = jnp.where(at == 0, lh, jnp.where(at == 1, lm, jnp.where(at == 2, ll, qc)))
        q_aug.append(jnp.where(mine, q2, extra))
        extra = jnp.where(at == 0, dh, jnp.where(at == 1, dm, jnp.where(at == 2, dl, zero)))
        d_aug.append(jnp.where(mine, dm2, extra))
    dq = [jnp.zeros((LONG, LANES), f32) for _ in range(2)]
    lane_t = lane_index(tile)
    one = jnp.ones((tile, LANES), bf16)
    zero_t = jnp.zeros((tile, LANES), bf16)
    for t in range(LONG // tile):
        krows = pl.ds(pl.multiple_of(block * LONG + t * tile, tile), tile)
        k2, v2, kc = k_ref[krows, cols], v_ref[krows, cols], key_const[krows, :]
        vc = jnp.where((lane_t & (HD - 1)) < 3, one, zero_t)
        dk, dv = [], []
        for half in range(2):
            mine = (lane_t // HD) == half
            weights = jnp.exp(dot_nt(jnp.where(mine, k2, kc), q_aug[half]))
            grads = weights * dot_nt(jnp.where(mine, v2, vc), d_aug[half])
            low, low_grads = weights.astype(bf16), grads.astype(bf16)
            dv.append(dot_nn(low, dm2))
            dk.append(dot_nn(low_grads, q2))
            dq[half] = dq[half] + dot_tn(low_grads, k2)
        dk_ref[krows, cols] = jnp.where(lane_t < HD, dk[0], dk[1]).astype(bf16)
        dv_ref[krows, cols] = jnp.where(lane_t < HD, dv[0], dv[1]).astype(bf16)
    dq_ref[rows, cols] = (jnp.where(lane < HD, dq[0], dq[1]).astype(bf16).astype(f32) * 0.125).astype(bf16)


def gelu_parts(x):
    magnitude = jnp.abs(x)
    base = 1.0 + (0.3275911 * 0.7071067811865476) * magnitude
    t = pl.reciprocal(base, approx=True)
    t = t * (2.0 - base * t)
    bell = jnp.exp2(x * x * -0.7213475204444817)
    tail = t * (0.127414796 + t * (-0.142248368 + t * (0.7107068705 + t * (-0.7265760135 + t * 0.5307027145)))) * bell
    phi = jnp.where(x >= 0.0, 1.0 - tail, tail)
    return x * phi, phi + x * (bell * 0.3989422804014327)


def norm_parts(x):
    center = x - jnp.mean(x, axis=-1, keepdims=True)
    spread = jnp.mean(center * center, axis=-1, keepdims=True)
    rstd = lax.rsqrt(spread + epsilon)
    return center * rstd, rstd


def norm_back(dy_hat, x_hat, rstd):
    a = jnp.mean(dy_hat, axis=-1, keepdims=True)
    b = jnp.mean(dy_hat * x_hat, axis=-1, keepdims=True)
    return rstd * (dy_hat - a - x_hat * b)

MESH = pl.DeviceIdType.MESH
Z, X, Y = 4, 2, 2
CHIPS = Z * Y * X
JOBS = 6
PART = FF // JOBS
BLOCK = D // CHIPS
FF_BLOCK = FF // CHIPS
SLICE = FF_BLOCK // JOBS
ALL = slice(None)


def aligned(value, unit):
    return pl.multiple_of(value, unit)


class Place:
    def __init__(self):
        group, inner = lax.axis_index("group"), lax.axis_index("inner")
        self.z, self.y, self.x, self.c = group // Y, group % Y, inner // 2, inner % 2
        self.index = group * (X * 2) + inner
        self.chip = group * X + self.x
        self.twin = (group, self.x * 2 + 1 - self.c)
        self.over = {
            "x": ((1 - self.x, (group, (1 - self.x) * 2 + self.c)),),
            "y": ((1 - self.y, (self.z * Y + 1 - self.y, inner)),),
            "z": tuple(
                (z, (z * Y + self.y, inner))
                for z in (self.z + 1 - 2 * (self.z % 2), (self.z + 2) % Z, Z - 1 - self.z)
            ),
        }
        self.peers = (self.twin,) + tuple(peer for axis in "xyz" for _, peer in self.over[axis])

    def greet(self):
        barrier = pltpu.get_barrier_semaphore()
        for peer in self.peers:
            pl.semaphore_signal(barrier, 1, device_id=peer, device_id_type=MESH)

    def met(self):
        pl.semaphore_wait(pltpu.get_barrier_semaphore(), len(self.peers))

    def at(self, whole, **given):
        return tuple(given[a] if a in given else ALL if a in whole else getattr(self, a) for a in "zyx")


def remote(source, target, send, recv, peer):
    return pltpu.make_async_remote_copy(
        src_ref=source, dst_ref=target, send_sem=send, recv_sem=recv, device_id=peer, device_id_type=MESH
    )


class Cut:
    def __init__(self, rows, cols, order=None, near=(ALL, ALL)):
        self.rows, self.cols, self.order, self.near = rows, cols, order, near


def row_parts(start, low, high, cols):
    return (
        Cut(pl.ds(aligned(start, 16), low), cols, "zxy", (pl.ds(0, low), ALL)),
        Cut(pl.ds(aligned(start + low, 16), high), cols, "zyx", (pl.ds(low, high), ALL)),
    )


def attend_cuts(core, g):
    cols = pl.ds(aligned(256 * g + 128 * core, 128), 128)
    low, high = (16, 32) if g % 2 == 0 else (32, 16)
    return Cut(pl.ds(0, BLOCK), cols), row_parts(0, low, high, cols)


def merge_cuts(core):
    cols = pl.ds(aligned(384 * core, 128), 384)
    return Cut(pl.ds(0, BLOCK), cols), row_parts(0, 32, 16, cols)


def expand_cuts(core, j):
    at = PART * j + 256 * core
    rows = pl.ds(0, BLOCK)
    orders = ("xzy", "zyx") if j % 2 == 0 else ("zxy", "yzx")
    return Cut(rows, pl.ds(aligned(at, 128), 256)), tuple(
        Cut(rows, pl.ds(aligned(at + 128 * n, 128), 128), orders[n]) for n in range(2)
    )


def shrink_cuts(core, j):
    cols = pl.ds(aligned(384 * core, 128), 384)
    half = SLICE // 2
    return Cut(pl.ds(aligned(SLICE * j, SLICE), SLICE), cols), row_parts(SLICE * j, half, half, cols)


def blocks(ref, at, cut):
    deep = (ALL,) if len(ref.shape) == 6 else ()
    return ref.at[at + deep + (cut.rows, cut.cols)]


class Gather:
    def __init__(self, place, ref, cuts, send, recv, twin_send, twin_recv):
        self.place, self.ref, (self.whole, self.parts) = place, ref, cuts
        self.send, self.recv, self.twin_send, self.twin_recv = send, recv, twin_send, twin_recv

    def stage(self, n, part, step):
        axis = part.order[step]
        here = blocks(self.ref, self.place.at(part.order[:step]), part)
        first = sum(len(self.place.over[a]) for a in part.order[:step])
        return [
            remote(here, here, self.send.at[n, first + m], self.recv.at[n, first + m], peer)
            for m, (_, peer) in enumerate(self.place.over[axis])
        ]

    def to_twin(self):
        here = blocks(self.ref, self.place.at("zyx"), self.whole)
        return remote(here, here, self.twin_send, self.twin_recv, self.place.twin)

    def run(self, step):
        for n, part in enumerate(self.parts):
            if step > 0:
                for copy in self.stage(n, part, step - 1):
                    copy.wait_recv()
            if step < 3:
                for copy in self.stage(n, part, step):
                    copy.start()
        if step == 3:
            self.to_twin().start()

    def ready(self):
        self.to_twin().wait_recv()

    def finish(self):
        for n, part in enumerate(self.parts):
            for step in range(3):
                for copy in self.stage(n, part, step):
                    copy.wait_send()
        self.to_twin().wait_send()


class Reduce:
    def __init__(self, place, ref, land0, lands, final, cuts, twin_cuts, sems):
        self.place, self.ref, (self.whole, self.parts), self.twin_whole = place, ref, cuts, twin_cuts[0]
        self.land0, self.lands, self.final = land0, lands, final
        self.send, self.recv, self.twin_send, self.twin_recv = sems
        self.deep = (ALL,) if len(ref.shape) == 6 else ()

    def twin(self):
        source = blocks(self.ref, self.place.at("zyx"), self.twin_whole)
        return remote(source, self.land0, self.twin_send, self.twin_recv, self.place.twin)

    def land(self, part, step, m):
        axis = part.order[3 - step]
        ref = self.lands[part.order[1] == "z"][step - 1]
        lead = ((ALL, ALL), (m, ALL) if axis == "z" else (ALL,), (m,))[step - 1]
        return ref.at[lead + self.deep + part.near]

    def stage(self, n, part, step):
        axis, left = part.order[3 - step], part.order[: 3 - step]
        first = sum(len(self.place.over[a]) for a in part.order[4 - step :])
        return [
            remote(
                blocks(self.ref, self.place.at(left, **{axis: there}), part), self.land(part, step, m),
                self.send.at[n, first + m], self.recv.at[n, first + m], peer,
            )
            for m, (there, peer) in enumerate(self.place.over[axis])
        ]

    def run(self, step):
        if step == 0:
            self.twin().start()
            return
        if step == 1:
            self.twin().wait_recv()
            mine = blocks(self.ref, self.place.at("zyx"), self.whole)
            mine[...] = (mine[...].astype(f32) + self.land0[...].astype(f32)).astype(bf16)
        for n, part in enumerate(self.parts):
            if step > 1:
                left = part.order[: 4 - step]
                mine = blocks(self.ref, self.place.at(left), part)
                value = mine[...].astype(f32)
                for m, copy in enumerate(self.stage(n, part, step - 1)):
                    copy.wait_recv()
                    value += self.land(part, step - 1, m)[...].astype(f32)
                if step < 4:
                    mine[...] = value.astype(bf16)
                else:
                    self.final[self.deep + (part.rows, part.cols)] = value
            if step < 4:
                for copy in self.stage(n, part, step):
                    copy.start()

    def finish(self):
        self.twin().wait_send()
        for n, part in enumerate(self.parts):
            for step in (1, 2, 3):
                for copy in self.stage(n, part, step):
                    copy.wait_send()

T = TOK_DEV
VEC_ROWS = 16
VECTORS = 99
PIECES = 8
ROW_MERGE, ROW_EXPAND, ROW_SHRINK, ROW_GAIN, ROW_SHIFT = 2, 3, 9, 10, 12
HALF, FF_HALF = BLOCK // 2, FF_BLOCK // 2
PACK = 3 * D + D + FF
GATHERS = 4 + 2 * JOBS
WEIGHTS = (
    ((Z, Y, X, 3, BLOCK, D), bf16),
    ((Z, Y, X, BLOCK, D), bf16),
    ((Z, Y, X, BLOCK, FF), bf16),
    ((Z, Y, X, FF_BLOCK, D), bf16),
)
VMEM_LIMIT = 255 * 2**18

G_START = [(0, 0), (0, 3), (1, 99), (1, 0), (0, 1), (1, 3), (0, 2), (2, 0), (2, 99), (2, 3), (0, 5), (1, 1), (0, 4), (0, 6), (3, 0), (3, 99), (1, 2)]
G_HEADS = {
    1: [(1, 4)],
    2: [(0, 7), (3, 1)],
    3: [(1, 6)],
    4: [(0, 8), (2, 5)],
    5: [(3, 2)],
    6: [(2, 4)],
    8: [],
    10: [(0, 9), (2, 6)],
    11: [(3, 5)],
}
G_READY = {
    0: [(2, 1), (1, 5), (2, 2), (3, 3)],
    8: [(1, 7)],
}
G_MERGE = [(3, 4), (1, 8)]
G_FFN = {
    2: [(2, 8)],
}
G_FFN_MIDDLE = {
    0: [(2, 7)],
    1: [(3, 6), (1, 9)],
    2: [(3, 7), (2, 9)],
    3: [(3, 8)],
    4: [(3, 9)],
}
R_FFN = {
}
R_FFN_MIDDLE = {
    1: [(1, 0)],
    2: [(1, 1)],
    3: [(1, 2)],
    4: [(2, 0), (2, 1), (1, 3)],
    5: [(1, 4)],
}
R_NORM = {
    1: [(3, 0), (2, 2), (1, 5)],
}
R_MERGE = []
R_HEADS = {
    1: [(2, 3)],
    2: [(3, 1)],
    3: [(2, 4)],
    5: [(1, 6)],
    6: [(2, 5), (3, 3)],
    7: [(3, 4), (1, 7)],
    8: [(2, 6)],
    9: [(1, 8), (3, 5)],
    11: [(2, 7), (3, 6)],
}
R_HEADS_END = {
    3: [(3, 2)],
}
R_TAIL = [[(2, 8), (4, 1), (3, 7), (1, 99), (1, 9), (4, 3)], [(3, 8), (2, 99)], [(3, 99), (2, 9), (4, 0), (4, 4), (4, 7), (3, 9), (4, 6), (4, 5), (4, 2), (4, 8)], [(4, 9)]]

def chosen(width, offset, start=0):
    source = lax.broadcasted_iota(jnp.int32, (LANES, D), 0)
    target = lax.broadcasted_iota(jnp.int32, (LANES, D), 1)
    mine = (source >= start) & (source < start + width)
    return jnp.where((target == source + (offset - start)) & mine, 1.0, 0.0).astype(bf16)


def vector_maps(place):
    per_row = D // (2 * HALF)
    return (
        chosen(2 * HALF, 2 * HALF * (place.index % per_row)),
        chosen(HALF, HALF * place.index),
        [chosen(SLICE, SLICE * place.chip, SLICE * n) for n in range(3)],
        place.index // per_row,
    )


def place_vectors(place, pieces_ref, out_ref):
    pieces = pieces_ref[...].astype(bf16)
    attend_map, single_map, expand_maps, half = vector_maps(place)
    attend = dot_nn(pieces, attend_map)
    single = dot_nn(pieces, single_map)
    expand = jnp.concatenate([dot_nn(pieces, m)[2:3] for m in expand_maps], axis=0)
    out_ref[...] = jnp.concatenate(
        [
            jnp.where(half == 0, attend[0:1], 0.0),
            jnp.where(half == 1, attend[0:1], 0.0),
            single[1:2],
            jnp.where(place.c == 0, expand, 0.0),
            jnp.where(place.c == 1, expand, 0.0),
            single[3:8],
            jnp.zeros((2, D), f32),
        ],
        axis=0,
    ).astype(bf16)


def own_vectors(place, sums):
    attend_map, single_map, expand_maps, half = vector_maps(place)
    high = sums.astype(bf16)
    rest = sums - high.astype(f32)
    middle = rest.astype(bf16)
    low = (rest - middle.astype(f32)).astype(bf16)
    parts = jnp.concatenate([high, middle, low], axis=0)

    def pick(chosen_map):
        found = dot_nt(parts, chosen_map)
        return found[:VEC_ROWS] + found[VEC_ROWS : 2 * VEC_ROWS] + found[2 * VEC_ROWS :]

    attend, single = pick(attend_map), pick(single_map)
    expand = 0.0
    for n, chosen_map in enumerate(expand_maps):
        found = pick(chosen_map)
        expand += jnp.where(place.c == 0, found[ROW_EXPAND + n], found[ROW_EXPAND + 3 + n])[None]
    return jnp.concatenate(
        [
            jnp.where(half == 0, attend[0:1], attend[1:2]),
            single[ROW_MERGE : ROW_MERGE + 1],
            expand,
            single[ROW_SHRINK : ROW_SHIFT + 2],
        ],
        axis=0,
    )


def lane_groups(read, write, moves):
    for target, sources in enumerate(moves):
        parts = []
        for group, (tile, at) in enumerate(sources):
            value = read(tile)
            shift = (group - at) * SLICE % LANES
            parts.append(pltpu.roll(value, shift, 1) if shift else value)
        lane = lax.broadcasted_iota(jnp.int32, parts[0].shape, 1) // SLICE
        write(target, jnp.where(lane < 2, jnp.where(lane == 0, parts[0], parts[1]), jnp.where(lane == 2, parts[2], parts[3])))


def ff_moves(inverse):
    outer, inner = (JOBS, CHIPS) if not inverse else (CHIPS, JOBS)
    units = [b * outer + a for a in range(outer) for b in range(inner)]
    return [[(u // 4, u % 4) for u in units[4 * t : 4 * t + 4]] for t in range(FF // LANES)]


def compose(place, pack_ref, twin_ref, source_cols):
    mine = pack_ref[:, source_cols].astype(f32)[:HALF]
    other = twin_ref[:, source_cols].astype(f32)[:HALF]
    first = jnp.where(place.c == 0, mine, other)
    second = jnp.where(place.c == 0, other, mine)
    return jnp.concatenate([first, second], axis=0).astype(bf16)


def layer_kernel(
    bucket, lengths, keeps, x_any, g_any, attend_any, merge_any, expand_any, shrink_any, pieces_any,
    out_any, ig_any, ga_any, gm_any, ge_any, gs_any, vec_out, active_any, slope_any,
    attend_ref, merge_ref, expand_ref, shrink_ref, pieces_ref, ge_own, wa, wm, we, ws, ga, pack, pack_twin, vec_parts, vec_land, vec,
    x, g, q, k, v, query_const, key_const, mixed, logsum, xhat, low, xt, lowt, active, slope, first,
    a0, a1, a2, a3, m0, m1, m2, m3, e0, e1, e2, e3, f1, f2, f3, s0, s1, s2, s3, fa, fm, fe, fs, gain, gain_land,
    g_send, g_recv, gt_send, gt_recv, r_send, r_recv, rt_send, rt_recv, own_send, own_recv, vec_send, vec_recv,
    sum_send, sum_recv, last_send, last_recv, local, flow,
):
    place = Place()
    c = place.c
    place.greet()
    shards = [
        pltpu.make_async_copy(source, target, local.at[4 + n])
        for n, (source, target) in enumerate(
            (
                (expand_any, expand_ref), (pieces_any, pieces_ref), (attend_any, attend_ref), (merge_any, merge_ref),
                (shrink_any, shrink_ref),
            )
        )
    ]
    x_copy = pltpu.make_async_copy(x_any, x, local.at[0])
    g_copy = pltpu.make_async_copy(g_any, g, local.at[1])
    for copy in shards + [x_copy, g_copy]:
        copy.start()
    for copy in shards:
        copy.wait()

    pack[0:HALF, 0 : 3 * D] = attend_ref[...]
    pack[0:HALF, 3 * D : 4 * D] = merge_ref[...]

    def put_expand(tile, value):
        pack[0:HALF, 4 * D + LANES * tile : 4 * D + LANES * (tile + 1)] = value.astype(bf16)

    lane_groups(
        lambda tile: expand_ref[:, LANES * tile : LANES * (tile + 1)].astype(f32), put_expand, ff_moves(False)
    )
    place_vectors(place, pieces_ref, vec_parts.at[0])
    place.met()

    own_pack = remote(pack, pack_twin, own_send.at[0], own_recv.at[0], place.twin)
    own_pack.start()
    their_cols = pl.ds(aligned(384 * (1 - c), 128), 384)
    my_cols = pl.ds(aligned(384 * c, 128), 384)
    my_rows = pl.ds(aligned(FF_HALF * c, FF_HALF), FF_HALF)
    own_shrink = remote(
        shrink_ref.at[:, their_cols], ws.at[place.z, place.y, place.x, my_rows, their_cols],
        own_send.at[1], own_recv.at[1], place.twin,
    )

    class Sums:
        def __init__(self, source, land, sends, recvs, order):
            self.source, self.land, self.steps = source, land, []
            at = 0
            for step, peers in enumerate([(place.twin,)] + [tuple(p for _, p in place.over[a]) for a in order]):
                self.steps.append([])
                for peer in peers:
                    copy = remote(source.at[step], land.at[at], sends.at[at], recvs.at[at], peer)
                    self.steps[-1].append((copy, at))
                    at += 1

        def run(self, step):
            if step > 0:
                total = self.source[step - 1].astype(f32)
                for copy, at in self.steps[step - 1]:
                    copy.wait_recv()
                    total += self.land[at].astype(f32)
                if step == 4:
                    return total
                self.source[step] = total.astype(self.source.dtype)
            for copy, _ in self.steps[step]:
                copy.start()

        def finish(self):
            for copies in self.steps:
                for copy, _ in copies:
                    copy.wait_send()

    vec_sums = Sums(vec_parts, vec_land, vec_send, vec_recv, "zxy")
    grad_sums = Sums(gain, gain_land, sum_send, sum_recv, "xyz")

    vec_sums.run(0)
    own_shrink.start()

    def gathers(t):
        def one(ref, cuts, at):
            return Gather(place, ref, cuts, g_send.at[at], g_recv.at[at], gt_send.at[at], gt_recv.at[at])

        if t < 3:
            return [one(wa, attend_cuts(c, t), t)]
        if t == 3:
            return [one(wm, merge_cuts(c), 3)]
        j = t - 4
        return [one(we, expand_cuts(c, j), 4 + 2 * j), one(ws, shrink_cuts(c, j), 5 + 2 * j)]

    def gather_events(names):
        for step, t in names:
            if t == VECTORS:
                vec_sums.run(step)
                continue
            for one in gathers(t):
                one.run(step)

    def when(index, table, events):
        for value, names in table.items():

            @pl.when(index == value)
            def _():
                events(names)

    own_pack.wait_recv()
    for group in range(3):
        for n in range(3):
            cols = aligned(256 * group + 128 * c, 128)
            wa[place.z, place.y, place.x, n, :, pl.ds(cols, 128)] = compose(
                place, pack, pack_twin, pl.ds(aligned(D * n + cols, 128), 128)
            )
    wm[place.z, place.y, place.x, :, my_cols] = compose(
        place, pack, pack_twin, pl.ds(aligned(3 * D + 384 * c, 128), 384)
    )
    for j in range(JOBS):
        cols = aligned(PART * j + 256 * c, 128)
        we[place.z, place.y, place.x, :, pl.ds(cols, 256)] = compose(
            place, pack, pack_twin, pl.ds(aligned(4 * D + cols, 128), 256)
        )
    ws[place.z, place.y, place.x, my_rows, my_cols] = shrink_ref[:, my_cols]
    own_shrink.wait_recv()
    gather_events(G_START[:3])
    token_tables(
        bucket[0], [lengths[0, b] for b in range(SLOTS)], [keeps[0, b] for b in range(SLOTS)],
        query_const, key_const, logsum,
    )
    x_copy.wait()
    xt[...] = x[...].T
    gather_events(G_START[3:])
    vec[...] = vec_sums.run(4)

    def heads(i, carry):
        when(i, G_HEADS, gather_events)
        for group in range(3):

            @pl.when(i == 4 * group)
            def _():
                for one in gathers(group):
                    one.ready()

        @pl.when(i % 4 == 0)
        def _():
            cols = pl.ds(aligned(256 * (i // 4), 256), 256)
            tokens = x[...]
            part = dot_nn(tokens, wa[:, :, :, 0, :, cols].reshape(D, 256))
            q[:, cols] = ((part + vec[0:1, cols]) * 0.125).astype(bf16)
            k[:, cols] = dot_nn(tokens, wa[:, :, :, 1, :, cols].reshape(D, 256)).astype(bf16)
            part = dot_nn(tokens, wa[:, :, :, 2, :, cols].reshape(D, 256))
            v[:, cols] = (part + vec[1:2, cols]).astype(bf16)

        when(i, G_READY, gather_events)
        attend_forward(i, query_const, key_const, q, k, v, mixed, logsum, LONG)
        return carry

    lax.fori_loop(0, 12, heads, 0)
    gather_events(G_MERGE)
    for one in gathers(3):
        one.ready()
    tile = 512

    def merge_norm(i, carry):
        rows = pl.ds(aligned(i * tile, tile), tile)
        branch = dot_nn(mixed[rows, :], wm[...].reshape(D, D)) + vec[ROW_MERGE : ROW_MERGE + 1, :]
        x_hat, deviation = norm_parts(x[rows, :].astype(f32) + branch)
        xhat[rows, :] = x_hat.astype(bf16)
        logsum[rows, :] = jnp.where(lane_index(tile) == RSTD_LANE, deviation, logsum[rows, :])
        normed = x_hat * vec[ROW_GAIN : ROW_GAIN + 1, :] + vec[ROW_SHIFT : ROW_SHIFT + 1, :]
        low[rows, :] = normed.astype(bf16)
        first[rows, :] = normed + vec[ROW_SHRINK : ROW_SHRINK + 1, :]
        return carry

    lax.fori_loop(0, T // tile, merge_norm, 0)
    lowt[...] = low[...].T

    def out_copies(j):
        return (
            pltpu.make_async_copy(active.at[j % 2], active_any.at[j], flow.at[0, j % 2]),
            pltpu.make_async_copy(slope.at[j % 2], slope_any.at[j], flow.at[1, j % 2]),
        )

    def back_copies(j):
        return (
            pltpu.make_async_copy(active_any.at[j], active.at[j % 2], flow.at[0, j % 2]),
            pltpu.make_async_copy(slope_any.at[j], slope.at[j % 2], flow.at[1, j % 2]),
        )

    def expand_part(j, carry):
        when(j, G_FFN, gather_events)

        @pl.when(j >= 2)
        def _():
            for copy in out_copies(j - 2):
                copy.wait()

        for t in range(JOBS):

            @pl.when(j == t)
            def _():
                for one in gathers(4 + t):
                    one.ready()

        a_ref, s_ref = active.at[j % 2], slope.at[j % 2]
        for h in range(2):
            here = slice(256 * h, 256 * h + 256)
            cols = pl.ds(aligned(PART * j + 256 * h, 256), 256)
            bias = vec[pl.ds(ROW_EXPAND + j, 1), here]
            expanded = dot_nn(low[...], we[:, :, :, :, cols].reshape(D, 256)) + bias
            a, s = gelu_parts(expanded)
            a_ref[:, here] = a.astype(bf16)
            s_ref[:, here] = s.astype(bf16)
        when(j, G_FFN_MIDDLE, gather_events)
        rows = pl.ds(aligned(SLICE * j, SLICE), SLICE)
        first[...] += dot_nn(a_ref[...], ws[:, :, :, rows, :].reshape(PART, D))

        @pl.when(j < JOBS - 2)
        def _():
            for copy in out_copies(j):
                copy.start()

        return carry

    lax.fori_loop(0, JOBS, expand_part, 0)
    g_copy.wait()
    gain[0] = jnp.zeros((VEC_ROWS, D), f32)

    def end_of_forward(i, carry):
        rows = pl.ds(aligned(i * tile, tile), tile)
        x_hat, deviation = norm_parts(first[rows, :])
        weight = vec[ROW_GAIN + 1 : ROW_GAIN + 2, :]
        result = x_hat * weight + vec[ROW_SHIFT + 1 : ROW_SHIFT + 2, :]
        keep = column_of(logsum[rows, :], KEEP_LANE) > 0.0
        dy = jnp.where(keep, g[rows, :].astype(f32), 0.0)
        g[rows, :] = jnp.where(keep, result, x[rows, :].astype(f32)).astype(bf16)
        grad = norm_back(dy * weight, x_hat, deviation)
        first[rows, :] = grad
        branch = grad.astype(bf16)
        low[rows, :] = branch
        gain[0, ROW_GAIN + 1 : ROW_GAIN + 2, :] += jnp.sum(dy * x_hat, axis=0, keepdims=True)
        gain[0, ROW_SHIFT + 1 : ROW_SHIFT + 2, :] += jnp.sum(dy, axis=0, keepdims=True)
        gain[0, ROW_SHRINK : ROW_SHRINK + 1, :] += jnp.sum(branch.astype(f32), axis=0, keepdims=True)
        return carry

    lax.fori_loop(0, T // tile, end_of_forward, 0)
    out_copy = pltpu.make_async_copy(g, out_any, local.at[2])
    out_copy.start()

    def reductions(t):
        def one(ref, land0, lands, final, cuts, at, *args):
            sems = (r_send.at[at], r_recv.at[at], rt_send.at[at], rt_recv.at[at])
            return Reduce(place, ref, land0, lands, final, cuts(c, *args), cuts(1 - c, *args), sems)

        if t < JOBS:
            j = JOBS - 1 - t
            return [
                one(we, e0.at[t % 2], [[ref.at[t] for ref in (e1, e2, e3)], [ref.at[t] for ref in (f1, f2, f3)]], fe, expand_cuts, 2 * t, j),
                one(ws, s0.at[t % 2], [[ref.at[t] for ref in (s1, s2, s3)]], fs, shrink_cuts, 2 * t + 1, j),
            ]
        if t == JOBS:
            return [one(wm, m0, [[m1, m2, m3]], fm, merge_cuts, 2 * JOBS)]
        n = t - JOBS - 1
        return [one(ga, a0.at[n % 2], [[ref.at[n] for ref in (a1, a2, a3)]], fa, attend_cuts, 2 * JOBS + 1 + n, n)]

    def reduce_events(names):
        for step, t in names:
            if t == VECTORS:
                grad_sums.run(step)
                continue
            for one in reductions(t):
                one.run(step)

    def expand_back(b, carry):
        j = JOBS - 1 - b

        @pl.when(b >= 2)
        def _():
            for copy in back_copies(j):
                copy.wait()

        when(b, R_FFN, reduce_events)
        a_ref, s_ref = active.at[j % 2], slope.at[j % 2]
        rows = pl.ds(aligned(SLICE * j, SLICE), SLICE)
        cols = pl.ds(aligned(PART * j, PART), PART)
        s_in = low[...]
        for h in range(2):
            here = slice(256 * h, 256 * h + 256)
            e_in = dot_nt(s_in, ws[2 * h : 2 * h + 2, :, :, rows, :].reshape(256, D)) * s_ref[:, here].astype(f32)
            e_in = e_in.astype(bf16)
            s_ref[:, here] = e_in
            gain[0, pl.ds(ROW_EXPAND + j, 1), here] = jnp.sum(e_in.astype(f32), axis=0, keepdims=True)
        when(b, R_FFN_MIDDLE, reduce_events)
        for h in range(2):
            grad = dot_tn(a_ref[:, 256 * h : 256 * h + 256], s_in).astype(bf16)
            ws[2 * h : 2 * h + 2, :, :, rows, :] = grad.reshape(2, Y, X, SLICE, D)
        first[...] += dot_nt(s_ref[...], we[:, :, :, :, cols].reshape(D, PART))
        for h in range(2):
            here = pl.ds(aligned(PART * j + 256 * h, 256), 256)
            grad = dot_nn(lowt[...], s_ref[:, 256 * h : 256 * h + 256]).astype(bf16)
            we[:, :, :, :, here] = grad.reshape(Z, Y, X, BLOCK, 256)
        when(b, {t: [(0, t)] for t in range(JOBS)}, reduce_events)

        @pl.when(b < JOBS - 2)
        def _():
            for copy in back_copies(j - 2):
                copy.start()

        return carry

    for t in range(4 + JOBS):
        for one in gathers(t):
            one.finish()
    lax.fori_loop(0, JOBS, expand_back, 0)

    def middle(i, carry):
        when(i, R_NORM, reduce_events)
        rows = pl.ds(aligned(i * tile, tile), tile)
        dy, x_hat = first[rows, :], xhat[rows, :].astype(f32)
        deviation = column_of(logsum[rows, :], RSTD_LANE)
        grad = norm_back(dy * vec[ROW_GAIN : ROW_GAIN + 1, :], x_hat, deviation)
        first[rows, :] = grad
        branch = grad.astype(bf16)
        low[rows, :] = branch
        gain[0, ROW_GAIN : ROW_GAIN + 1, :] += jnp.sum(dy * x_hat, axis=0, keepdims=True)
        gain[0, ROW_SHIFT : ROW_SHIFT + 1, :] += jnp.sum(dy, axis=0, keepdims=True)
        gain[0, ROW_MERGE : ROW_MERGE + 1, :] += jnp.sum(branch.astype(f32), axis=0, keepdims=True)
        x[rows, :] = dot_nt(branch, wm[...].reshape(D, D)).astype(bf16)
        return carry

    lax.fori_loop(0, T // tile, middle, 0)
    out_copy.wait()
    g_again = pltpu.make_async_copy(g_any, g, local.at[1])
    g_again.start()
    reduce_events(R_MERGE)
    wm[...] = dot_tn(mixed[...], low[...]).astype(bf16).reshape(Z, Y, X, BLOCK, D)
    reduce_events([(0, JOBS)])

    def heads_back(i, carry):
        when(i, R_HEADS, reduce_events)
        attend_backward(i, query_const, key_const, q, k, v, mixed, logsum, x, q, k, v, LONG)

        when(i, R_HEADS_END, reduce_events)

        @pl.when(i % 4 == 3)
        def _():
            cols = pl.ds(aligned(256 * (i // 4), 256), 256)
            for n, grads in enumerate((q, k, v)):
                grad = dot_nn(xt[...], grads[:, cols]).astype(bf16)
                ga[:, :, :, n, :, cols] = grad.reshape(Z, Y, X, BLOCK, 256)
                if n != 1:
                    gain[0, n // 2 : n // 2 + 1, cols] = jnp.sum(grads[:, cols].astype(f32), axis=0, keepdims=True)

        when(i, {4 * n + 3: [(0, JOBS + 1 + n)] for n in range(3)}, reduce_events)
        return carry

    lax.fori_loop(0, 12, heads_back, 0)
    grad_sums.run(0)

    def last_copy(ref, n, cols, height):
        rows = pl.ds(aligned(height * (1 - c), 8), height)
        here = ref.at[:, rows, cols] if len(ref.shape) == 3 else ref.at[rows, cols]
        return remote(here, here, last_send.at[n], last_recv.at[n], place.twin)

    early_last = [last_copy(fm, 0, my_cols, HALF), last_copy(fs, 1, my_cols, FF_HALF)]
    early_last += [last_copy(fe, 2 + j, expand_cuts(c, j)[0].cols, HALF) for j in range(JOBS)]
    attend_last = [last_copy(fa, 2 + JOBS + n, attend_cuts(c, n)[0].cols, HALF) for n in range(3)]

    reduce_events(R_TAIL[0])
    g_again.wait()

    def inputs_part(i, carry):
        @pl.when(i == 1)
        def _():
            reduce_events(R_TAIL[1])

        rows = pl.ds(aligned(i * tile, tile), tile)
        keep = column_of(logsum[rows, :], KEEP_LANE) > 0.0
        total = first[rows, :] + jnp.where(keep, 0.0, g[rows, :].astype(f32))
        for n, grads in enumerate((q, k, v)):
            total += dot_nt(grads[rows, :], wa[:, :, :, n, :, :].reshape(D, D))
        first[rows, :] = total
        return carry

    lax.fori_loop(0, T // tile, inputs_part, 0)
    out_ig = pltpu.make_async_copy(first, ig_any, local.at[3])
    out_ig.start()
    reduce_events(R_TAIL[2])
    for copy in early_last + attend_last[:2]:
        copy.start()
    mine, ff_mine = pl.ds(aligned(HALF * c, 8), HALF), pl.ds(aligned(FF_HALF * c, 8), FF_HALF)
    for copy in early_last:
        copy.wait_recv()
    done = [
        pltpu.make_async_copy(fm.at[mine], gm_any, local.at[4]),
        pltpu.make_async_copy(fs.at[ff_mine], gs_any, local.at[5]),
        pltpu.make_async_copy(ge_own, ge_any, local.at[6]),
    ]
    done[0].start()
    done[1].start()

    def put_grad(tile, value):
        ge_own[:, LANES * tile : LANES * (tile + 1)] = value

    lane_groups(lambda tile: fe[mine, LANES * tile : LANES * (tile + 1)], put_grad, ff_moves(True))
    done[2].start()
    own_pack.wait_send()
    own_shrink.wait_send()
    for copy in early_last:
        copy.wait_send()
    vec_sums.finish()
    for t in range(JOBS + 3):
        for one in reductions(t):
            one.finish()
    for copy in attend_last[:2]:
        copy.wait_recv()
        copy.wait_send()
    vec_out[...] = own_vectors(place, grad_sums.run(4))
    grad_sums.finish()
    reduce_events(R_TAIL[3])
    attend_last[2].start()
    for one in reductions(JOBS + 3):
        one.finish()
    attend_last[2].wait_recv()
    done += [
        pltpu.make_async_copy(fa.at[n, mine], ga_any.at[:, pl.ds(D * n, D)], local.at[7 + n]) for n in range(3)
    ]
    for copy in done[3:]:
        copy.start()
    attend_last[2].wait_send()
    for copy in done + [out_ig]:
        copy.wait()


ANY = pl.BlockSpec(memory_space=pl.ANY)
VM = pl.BlockSpec(memory_space=pltpu.VMEM)
SM = pl.BlockSpec(memory_space=pltpu.SMEM)


def layer_call(buckets, lengths, keeps, inputs, upstream, attend, merge, expand, shrink, pieces):
    dma = pltpu.SemaphoreType.DMA

    def landing(rows, cols, jobs=None, deep=(), slots=None, parts=1):
        lead = (jobs,) if jobs else ()
        stages = [(Z, 2), (Z,), (3,), (Z, 2), (3, 2), (1,)][: 3 * parts]
        return [pltpu.VMEM(((slots,) if slots else lead) + (Z, Y, X) + deep + (rows, cols), bf16)] + [
            pltpu.VMEM(lead + d + deep + (rows, cols // parts), bf16) for d in stages
        ]

    tokens = [pltpu.VMEM((T, D), bf16) for _ in range(5)]
    scratch = (
        [pltpu.VMEM(a.shape, a.dtype) for a in (attend, merge, expand, shrink, pieces)]
        + [pltpu.VMEM((HALF, FF), f32)]
        + [pltpu.VMEM(*s) for s in WEIGHTS]
        + [
            pltpu.VMEM(*WEIGHTS[0]),
            pltpu.VMEM((32, PACK), bf16),
            pltpu.VMEM((32, PACK), bf16),
            pltpu.VMEM((4, VEC_ROWS, D), bf16),
            pltpu.VMEM((6, VEC_ROWS, D), bf16),
            pltpu.VMEM((VEC_ROWS, D), f32),
        ]
        + tokens
        + [
            pltpu.VMEM((T, LANES), bf16),
            pltpu.VMEM((T, LANES), bf16),
            pltpu.VMEM((T, D), bf16),
            pltpu.VMEM((T, LANES), f32),
            pltpu.VMEM((T, D), bf16),
            pltpu.VMEM((T, D), bf16),
            pltpu.VMEM((D, T), bf16),
            pltpu.VMEM((D, T), bf16),
            pltpu.VMEM((2, T, PART), bf16),
            pltpu.VMEM((2, T, PART), bf16),
            pltpu.VMEM((T, D), f32),
        ]
        + landing(BLOCK, 128, 3, (3,), slots=2)
        + landing(BLOCK, 384)
        + landing(BLOCK, 256, JOBS, slots=2, parts=2)
        + landing(SLICE, 384, JOBS, slots=2)
        + [
            pltpu.VMEM((3, BLOCK, D), f32),
            pltpu.VMEM((BLOCK, D), f32),
            pltpu.VMEM((BLOCK, FF), f32),
            pltpu.VMEM((FF_BLOCK, D), f32),
            pltpu.VMEM((4, VEC_ROWS, D), f32),
            pltpu.VMEM((6, VEC_ROWS, D), f32),
        ]
        + 2 * [dma((GATHERS, 2, 5)), dma((GATHERS, 2, 5)), dma((GATHERS,)), dma((GATHERS,))]
        + 2 * [dma((2,))]
        + 4 * [dma((6,))]
        + 2 * [dma((5 + JOBS,))]
        + [dma((10,)), dma((2, 2))]
    )
    return pl.pallas_call(
        layer_kernel,
        out_shape=tuple(
            jax.ShapeDtypeStruct(*s)
            for s in (
                ((T, D), bf16), ((T, D), f32), ((HALF, 3 * D), f32), ((HALF, D), f32), ((HALF, FF), f32),
                ((FF_HALF, D), f32), ((PIECES, LANES), f32), ((JOBS, T, PART), bf16), ((JOBS, T, PART), bf16),
            )
        ),
        in_specs=[SM] * 3 + [ANY] * 7,
        out_specs=[ANY] * 6 + [VM] + [ANY] * 2,
        scratch_shapes=scratch,
        compiler_params=pltpu.CompilerParams(collective_id=0, has_side_effects=True, vmem_limit_bytes=VMEM_LIMIT),
        cost_estimate=pl.CostEstimate(flops=60_000_000_000, bytes_accessed=60_000_000, transcendentals=20_000_000),
    )(buckets, lengths, keeps, inputs, upstream, attend, merge, expand, shrink, pieces)


def pack_pieces(attend_bias, merge_bias, expand_bias, shrink_bias, gain, shift):
    total = 0.0
    vectors = (attend_bias[None], merge_bias[None], expand_bias[None], shrink_bias[None], gain, shift)
    row = 0
    for piece in vectors:
        count, width = piece.shape
        total += jnp.pad(piece.astype(f32), ((row, PIECES - row - count), (0, LANES - width)))
        row += count
    return total


def finish_kernel(*refs):
    count = len(RESULTS)
    sources, own, wide, vectors = refs[:count], refs[count], refs[count + 1 : 2 * count + 1], refs[2 * count + 1 : -count - 2]
    held, arrive, leave = refs[-count - 2 : -2], refs[-2], refs[-1]
    steps = [
        (pltpu.make_async_copy(s, h, arrive.at[n]), pltpu.make_async_copy(h, w, leave.at[n]))
        for n, (s, h, w) in enumerate(zip(sources, held, wide))
    ]
    for into, _ in steps:
        into.start()
    row = 0
    for ref in vectors:
        if len(ref.shape) == 1:
            ref[...] = own[row, : ref.shape[0]]
            row += 1
        else:
            ref[...] = own[row : row + ref.shape[0], : ref.shape[1]]
            row += ref.shape[0]
    for into, out in steps:
        into.wait()
        out.start()
    for _, out in steps:
        out.wait()


RESULTS = (
    ((T, D), f32), ((T, D), bf16), ((HALF, 3 * D), f32), ((HALF, D), f32), ((HALF, FF), f32), ((FF_HALF, D), f32),
)


def finish_call(wide, own, vectors):
    dma = pltpu.SemaphoreType.DMA
    return pl.pallas_call(
        finish_kernel,
        out_shape=tuple(jax.ShapeDtypeStruct(*s) for s in RESULTS)
        + tuple(jax.ShapeDtypeStruct(v.shape, f32) for v in vectors),
        in_specs=[ANY] * len(RESULTS) + [VM],
        out_specs=[ANY] * len(RESULTS) + [VM] * len(vectors),
        scratch_shapes=[pltpu.VMEM(*s) for s in RESULTS] + 2 * [dma((len(RESULTS),))],
        compiler_params=pltpu.CompilerParams(vmem_limit_bytes=VMEM_LIMIT),
    )(*wide, own)

def layer_norm(hidden, gains, shifts):
    center = hidden - jnp.mean(hidden, axis=-1, keepdims=True)
    spread = jnp.mean(center * center, axis=-1, keepdims=True)
    return center * lax.rsqrt(spread + epsilon) * gains + shifts


def gelu_exact(values):
    return jax.nn.gelu(values, approximate=False)


def matmul(left, right):
    return jnp.dot(left, right, preferred_element_type=jnp.float32)


def token_info(bucket, slot_lengths, slot_keeps):
    position = jnp.arange(TOK_DEV, dtype=jnp.int32)
    span_size = jnp.where(bucket > 0, LONG, SHORT).astype(jnp.int32)
    sequence = position // span_size
    within = position - sequence * span_size
    slot_index = sequence * (span_size // SHORT)
    matches = (slot_index[:, None] == jnp.arange(SLOTS, dtype=jnp.int32)[None, :]).astype(jnp.int32)
    length = jnp.sum(matches * slot_lengths[None, :], axis=1) + bucket * (LONG - SHORT)
    keep_flags = jnp.sum(matches * slot_keeps[None, :], axis=1)
    return (sequence, within < length, keep_flags > 0)


def masked_scores(queries, key_rows, sequence, valid_key):
    scores = jnp.einsum("qhd,khd->hqk", queries, key_rows, preferred_element_type=jnp.float32)
    allowed = (sequence[:, None] == sequence[None, :]) & valid_key[None, :]
    return jnp.where(allowed[None], scores, masked_score)


def attend_block(pieces):
    queries, key_rows, values, sequence, valid_key = pieces
    scores = masked_scores(queries, key_rows, sequence, valid_key)
    highest = jnp.max(scores, axis=-1, keepdims=True)
    raised = jnp.exp(scores - highest)
    row_total = jnp.sum(raised, axis=-1, keepdims=True)
    weights = raised / row_total
    mixed_rows = jnp.einsum(
        "hqk,khd->qhd", weights.astype(jnp.bfloat16), values, preferred_element_type=jnp.float32
    )
    return (mixed_rows, highest[:, :, 0] + jnp.log(row_total[:, :, 0]))


def attend_back(pieces):
    queries, key_rows, values, sequence, valid_key, logsum, mixed_grad = pieces
    scores = masked_scores(queries, key_rows, sequence, valid_key)
    weights = jnp.exp(scores - logsum[:, :, None])
    weight_grad = jnp.einsum("qhd,khd->hqk", mixed_grad, values, preferred_element_type=jnp.float32)
    row_dot = jnp.sum(weights * weight_grad, axis=-1, keepdims=True)
    score_grad = (weights * (weight_grad - row_dot)).astype(jnp.bfloat16)
    query_part = jnp.einsum(
        "hqk,khd->qhd", score_grad, key_rows, preferred_element_type=jnp.float32
    ).astype(jnp.bfloat16)
    key_part = jnp.einsum(
        "hqk,qhd->khd", score_grad, queries, preferred_element_type=jnp.float32
    ).astype(jnp.bfloat16)
    value_part = jnp.einsum(
        "hqk,qhd->khd", weights.astype(jnp.bfloat16), mixed_grad, preferred_element_type=jnp.float32
    ).astype(jnp.bfloat16)
    return (query_part, key_part, value_part)


def heads_view(source):
    return source.reshape(source.shape[0] // LONG, LONG, HEADS, HD)


def forward_pass(inputs, weights, sequence, valid_key, keep_flags):
    (
        attend_matrix,
        attend_offset,
        merge_matrix,
        merge_offset,
        expand_matrix,
        expand_offset,
        shrink_matrix,
        shrink_offset,
        gains,
        shifts,
    ) = weights
    model_width = inputs.shape[1]
    blocks = inputs.shape[0] // LONG
    packed = matmul(inputs, attend_matrix)
    offset = attend_offset.astype(jnp.float32)
    queries = ((packed[:, :model_width] + offset[:model_width]) * 0.125).astype(jnp.bfloat16)
    key_rows = packed[:, model_width : 2 * model_width].astype(jnp.bfloat16)
    values = (packed[:, 2 * model_width :] + offset[model_width:]).astype(jnp.bfloat16)
    mixed_rows, logsum = lax.map(
        attend_block,
        (
            heads_view(queries),
            heads_view(key_rows),
            heads_view(values),
            sequence.reshape(blocks, LONG),
            valid_key.reshape(blocks, LONG),
        ),
    )
    mixed_rows = mixed_rows.reshape(-1, model_width).astype(jnp.bfloat16)
    tokens = inputs.astype(jnp.float32)
    first_sum = tokens + matmul(mixed_rows, merge_matrix) + merge_offset.astype(jnp.float32)
    normed = layer_norm(first_sum, gains[0].astype(jnp.float32), shifts[0].astype(jnp.float32))
    normed_low = normed.astype(jnp.bfloat16)
    expanded = matmul(normed_low, expand_matrix) + expand_offset.astype(jnp.float32)
    active = gelu_exact(expanded).astype(jnp.bfloat16)
    second_sum = normed + matmul(active, shrink_matrix) + shrink_offset.astype(jnp.float32)
    result = layer_norm(second_sum, gains[1].astype(jnp.float32), shifts[1].astype(jnp.float32))
    outputs = jnp.where(keep_flags[:, None], result, tokens).astype(jnp.bfloat16)
    return (
        outputs,
        (
            queries,
            key_rows,
            values,
            logsum,
            mixed_rows,
            first_sum,
            normed_low,
            expanded,
            active,
            second_sum,
        ),
    )


def backward_pass(inputs, upstream, weights, saved, sequence, valid_key, keep_flags):
    (
        attend_matrix,
        attend_offset,
        merge_matrix,
        merge_offset,
        expand_matrix,
        expand_offset,
        shrink_matrix,
        shrink_offset,
        gains,
        shifts,
    ) = weights
    (
        queries,
        key_rows,
        values,
        logsum,
        mixed_rows,
        first_sum,
        normed_low,
        expanded,
        active,
        second_sum,
    ) = saved
    model_width = inputs.shape[1]
    blocks = inputs.shape[0] // LONG
    cotangent = upstream.astype(jnp.float32)
    result_grad = jnp.where(keep_flags[:, None], cotangent, 0.0)
    second_out, pull_second = jax.vjp(
        layer_norm, second_sum, gains[1].astype(jnp.float32), shifts[1].astype(jnp.float32)
    )
    second_grad, gain_two, shift_two = pull_second(result_grad)
    shrink_in = second_grad.astype(jnp.bfloat16)
    shrink_grad = jnp.einsum("tf,td->fd", active, shrink_in, preferred_element_type=jnp.float32)
    shrink_offset_grad = jnp.sum(shrink_in.astype(jnp.float32), axis=0)
    active_grad = jnp.einsum(
        "td,fd->tf", shrink_in, shrink_matrix, preferred_element_type=jnp.float32
    )
    gelu_out, pull_gelu = jax.vjp(gelu_exact, expanded)
    expand_in = pull_gelu(active_grad)[0].astype(jnp.bfloat16)
    expand_grad = jnp.einsum("td,tf->df", normed_low, expand_in, preferred_element_type=jnp.float32)
    expand_offset_grad = jnp.sum(expand_in.astype(jnp.float32), axis=0)
    normed_grad = second_grad + jnp.einsum(
        "tf,df->td", expand_in, expand_matrix, preferred_element_type=jnp.float32
    )
    first_out, pull_first = jax.vjp(
        layer_norm, first_sum, gains[0].astype(jnp.float32), shifts[0].astype(jnp.float32)
    )
    first_grad, gain_one, shift_one = pull_first(normed_grad)
    branch_in = first_grad.astype(jnp.bfloat16)
    merge_grad = jnp.einsum("td,te->de", mixed_rows, branch_in, preferred_element_type=jnp.float32)
    merge_offset_grad = jnp.sum(branch_in.astype(jnp.float32), axis=0)
    mixed_grad = jnp.einsum(
        "te,de->td", branch_in, merge_matrix, preferred_element_type=jnp.float32
    ).astype(jnp.bfloat16)
    query_part, key_part, value_part = lax.map(
        attend_back,
        (
            heads_view(queries),
            heads_view(key_rows),
            heads_view(values),
            sequence.reshape(blocks, LONG),
            valid_key.reshape(blocks, LONG),
            logsum,
            heads_view(mixed_grad),
        ),
    )
    query_grad = query_part.reshape(-1, model_width) * 0.125
    packed_grad = jnp.concatenate(
        [query_grad, key_part.reshape(-1, model_width), value_part.reshape(-1, model_width)], axis=1
    )
    attend_grad = jnp.einsum("td,te->de", inputs, packed_grad, preferred_element_type=jnp.float32)
    attend_offset_grad = jnp.concatenate(
        [
            jnp.sum(query_grad.astype(jnp.float32), axis=0),
            jnp.sum(value_part.reshape(-1, model_width).astype(jnp.float32), axis=0),
        ]
    )
    input_grad = (
        first_grad
        + jnp.einsum("te,de->td", packed_grad, attend_matrix, preferred_element_type=jnp.float32)
        + jnp.where(keep_flags[:, None], 0.0, cotangent)
    )
    gain_grad = jnp.stack([gain_one, gain_two])
    shift_grad = jnp.stack([shift_one, shift_two])
    grads = (
        attend_grad,
        attend_offset_grad,
        merge_grad,
        merge_offset_grad,
        expand_grad,
        expand_offset_grad,
        shrink_grad,
        shrink_offset_grad,
        gain_grad,
        shift_grad,
    )
    return (grads, input_grad)


def general_device(
    inputs,
    upstream,
    buckets,
    lengths,
    layer_keep,
    attend_weight,
    attend_bias,
    merge_weight,
    merge_bias,
    expand_weight,
    expand_bias,
    shrink_weight,
    shrink_bias,
    norm_gain,
    norm_shift,
):
    sequence, valid_key, keep_flags = token_info(buckets[0], lengths[0], layer_keep[0])
    gathered = (
        lax.all_gather(attend_weight, ("group", "inner"), axis=0, tiled=True),
        lax.all_gather(attend_bias, ("group", "inner"), axis=0, tiled=True),
        lax.all_gather(merge_weight, ("group", "inner"), axis=0, tiled=True),
        lax.all_gather(merge_bias, ("group", "inner"), axis=0, tiled=True),
        lax.all_gather(expand_weight, ("group", "inner"), axis=0, tiled=True),
        lax.all_gather(expand_bias, ("group", "inner"), axis=0, tiled=True),
        lax.all_gather(shrink_weight, ("group", "inner"), axis=0, tiled=True),
        lax.all_gather(shrink_bias, ("group", "inner"), axis=0, tiled=True),
        lax.all_gather(norm_gain, ("group", "inner"), axis=1, tiled=True),
        lax.all_gather(norm_shift, ("group", "inner"), axis=1, tiled=True),
    )
    outputs, saved = forward_pass(inputs, gathered, sequence, valid_key, keep_flags)
    gathered = (
        lax.all_gather(attend_weight, ("group", "inner"), axis=0, tiled=True),
        lax.all_gather(attend_bias, ("group", "inner"), axis=0, tiled=True),
        lax.all_gather(merge_weight, ("group", "inner"), axis=0, tiled=True),
        lax.all_gather(merge_bias, ("group", "inner"), axis=0, tiled=True),
        lax.all_gather(expand_weight, ("group", "inner"), axis=0, tiled=True),
        lax.all_gather(expand_bias, ("group", "inner"), axis=0, tiled=True),
        lax.all_gather(shrink_weight, ("group", "inner"), axis=0, tiled=True),
        lax.all_gather(shrink_bias, ("group", "inner"), axis=0, tiled=True),
        lax.all_gather(norm_gain, ("group", "inner"), axis=1, tiled=True),
        lax.all_gather(norm_shift, ("group", "inner"), axis=1, tiled=True),
    )
    grads, input_grad = backward_pass(
        inputs, upstream, gathered, saved, sequence, valid_key, keep_flags
    )
    shares = (
        lax.psum_scatter(grads[0], ("group", "inner"), scatter_dimension=0, tiled=True),
        lax.psum_scatter(grads[1], ("group", "inner"), scatter_dimension=0, tiled=True),
        lax.psum_scatter(grads[2], ("group", "inner"), scatter_dimension=0, tiled=True),
        lax.psum_scatter(grads[3], ("group", "inner"), scatter_dimension=0, tiled=True),
        lax.psum_scatter(grads[4], ("group", "inner"), scatter_dimension=0, tiled=True),
        lax.psum_scatter(grads[5], ("group", "inner"), scatter_dimension=0, tiled=True),
        lax.psum_scatter(grads[6], ("group", "inner"), scatter_dimension=0, tiled=True),
        lax.psum_scatter(grads[7], ("group", "inner"), scatter_dimension=0, tiled=True),
        lax.psum_scatter(grads[8], ("group", "inner"), scatter_dimension=1, tiled=True),
        lax.psum_scatter(grads[9], ("group", "inner"), scatter_dimension=1, tiled=True),
    )
    return (
        outputs,
        input_grad,
        shares[0],
        shares[1],
        shares[2],
        shares[3],
        shares[4],
        shares[5],
        shares[6],
        shares[7],
        shares[8],
        shares[9],
    )

def slice_device(
    inputs, upstream, buckets, lengths, layer_keep, attend_weight, attend_bias, merge_weight, merge_bias,
    expand_weight, expand_bias, shrink_weight, shrink_bias, norm_gain, norm_shift,
):
    pieces = pack_pieces(attend_bias, merge_bias, expand_bias, shrink_bias, norm_gain, norm_shift)
    outputs, input_grad, attend, merge, expand, shrink, own = layer_call(
        buckets, lengths, layer_keep, inputs, upstream, attend_weight, merge_weight, expand_weight, shrink_weight, pieces
    )[:7]
    input_grad, outputs, attend, merge, expand, shrink, attend_b, merge_b, expand_b, shrink_b, gain, shift = finish_call(
        (input_grad, outputs, attend, merge, expand, shrink),
        own,
        (attend_bias, merge_bias, expand_bias, shrink_bias, norm_gain, norm_shift),
    )
    return (
        outputs, input_grad, attend, attend_b, merge, merge_b, expand, expand_b, shrink, shrink_b, gain, shift,
    )

def solution(mesh):
    on_slice = mesh.shape["group"] == Z * Y and mesh.shape["inner"] == 2 * X
    placed = (
        P(("group", "inner"), None),
        P(("group", "inner"), None),
        P(("group", "inner")),
        P(("group", "inner"), None),
        P(("group", "inner"), None),
        P(("group", "inner"), None),
        P(("group", "inner")),
        P(("group", "inner"), None),
        P(("group", "inner")),
        P(("group", "inner"), None),
        P(("group", "inner")),
        P(("group", "inner"), None),
        P(("group", "inner")),
        P(None, ("group", "inner")),
        P(None, ("group", "inner")),
    )
    return jax.shard_map(
        slice_device if on_slice else general_device,
        mesh=mesh,
        in_specs=placed,
        out_specs=(
            P(("group", "inner"), None),
            P(("group", "inner"), None),
            P(("group", "inner"), None),
            P(("group", "inner")),
            P(("group", "inner"), None),
            P(("group", "inner")),
            P(("group", "inner"), None),
            P(("group", "inner")),
            P(("group", "inner"), None),
            P(("group", "inner")),
            P(None, ("group", "inner")),
            P(None, ("group", "inner")),
        ),
        check_vma=False,
    )
```
